256 devices in a mesh: member: 4 (over z_hi), region: 32 (over z_lo, x, y), fine: 2 (over core).
Axes of the slice: x: 4, y: 4, z: 8 (z_hi: 4, z_lo: 2; z = z_hi * 2 + z_lo), core: 2. Of those that a mesh axis runs over, the one named last changes fastest.
Arguments:
- sample_surface_elevation: float32 [256, 32, 4096], P('member', 'region', 'fine'), may hold values from -6 to 6
- sample_zonal_current: float32 [256, 32, 4096], P('member', 'region', 'fine'), may hold values from -6 to 6
- sample_meridional_current: float32 [256, 32, 4096], P('member', 'region', 'fine'), may hold values from -6 to 6
- zonal_edge_layer_courant: float32 [32, 4096], P('region', 'fine'), may hold values from 0.1 to 0.45
- meridional_edge_layer_courant: float32 [32, 4096], P('region', 'fine'), may hold values from 0.1 to 0.45
- obs_index: int32 [512, 512, 4], P(('member', 'region', 'fine')), may hold values from 0 to 767
- obs_weight: float32 [512, 512, 4], P(('member', 'region', 'fine')), may hold values from 0.1 to 1
- obs_value: float32 [512, 512], P(('member', 'region', 'fine')), may hold values from -12 to 12
- obs_var: float32 [512, 512], P(('member', 'region', 'fine')), may hold values from 0.25 to 4
- obs_count: int32 [512], P(('member', 'region', 'fine')), may hold values from 64 to 512, as said below
- fine_ctrl: float32 [3, 64, 2, 4096], P(None, 'region', 'fine', 'member'), may hold values from -6 to 6
Outputs:
- ana_h: float32 [256, 32, 4096], P('member', 'region', 'fine')
- ana_u: float32 [256, 32, 4096], P('member', 'region', 'fine')
- ana_v: float32 [256, 32, 4096], P('member', 'region', 'fine')
- fine_out: float32 [3, 64, 2, 4096], P(None, 'region', 'fine', 'member')
The draws below stay inside these ranges and needn't reach their ends.
Inputs may be any that keep to these rules, and one draw needn't show every extreme that they name: `obs_count`: each region's count is 512 // 8 times 1, 2, 4 or 8; some region has 512 and some 512 // 8 in every draw; the live observations of a region are its first count slots.
All inputs are finite; a program needn't handle non-finite values.
Results may differ from the reference program's by a relative error of at most 0.0003.
Values sent between devices are 32-bit elements; how exact they have to be, the bound alone decides.
A program may use at most 64 MiB of HBM per device.

```python
import math
import jax
import jax.numpy as jnp
from jax import lax

K = 256
ROWS_DEV = 1
RCOLS = 16
REG_DEV = 2
NOBS = 512
STEPS = 4
NEWTON = 8
NY = 32
NX = 4096
CELLS_REG = 256
NREG = 512
FNY = 64
FNX = 8192
N_MEMBER = 4
N_REGION = 32
N_FINE = 2


def draw_obs_count(key, part):
    key_pick = jax.random.fold_in(key, 11)
    key_order = jax.random.fold_in(key, 23)
    pick = jax.random.randint(key_pick, (NREG,), 0, 4)
    table = jnp.array([1, 2, 4, 8], dtype=jnp.int32)
    counts = NOBS // 8 * jnp.take(table, pick)
    order = jax.random.permutation(key_order, NREG)
    counts = counts.at[order[0]].set(NOBS)
    counts = counts.at[order[1]].set(NOBS // 8)
    return counts.astype(jnp.int32)


def touch_ends(drawn, stream_key, least, largest):
    place = [jax.random.randint(jax.random.fold_in(stream_key, axis), (), 0, length) for axis, length in enumerate(drawn.shape)]
    main_axis = drawn.shape.index(max(drawn.shape))
    next_to = place[:main_axis] + [(place[main_axis] + 1) % drawn.shape[main_axis]] + place[main_axis + 1:]
    return drawn.at[tuple(place)].set(least).at[tuple(next_to)].set(largest)


def block_scale(own_key, shape, cuts, least, largest):
    level, own = 1.0, jax.random.fold_in(own_key, 6)
    for dim, blocks in cuts:
        draws = jnp.exp(jax.random.uniform(jax.random.fold_in(own, dim), (blocks,), jnp.float32, least / len(cuts), largest / len(cuts)))
        level = level * jnp.repeat(draws, shape[dim] // blocks).reshape([-1 if axis == dim else 1 for axis in range(len(shape))])
    return level


def scatter_about(key, extent, deviation, limit, shards=(), kind=jnp.bfloat16):
    level = block_scale(key, extent, shards, -0.22, 0.18) if shards else 1.0
    values = jax.random.normal(key, extent, jnp.float32) * deviation * level
    return jnp.minimum(jnp.maximum(values, -limit), limit).astype(kind)


def setup_inputs(seed: int = 0) -> dict:
    arg_keys = jax.random.split(jax.random.key(seed), 12)
    sample_surface_elevation = scatter_about(arg_keys[0], (K, NY, NX), 1.0, 6.0, ((0, 4), (1, 32), (2, 2)), jnp.float32)
    sample_zonal_current = scatter_about(arg_keys[1], (K, NY, NX), 1.0, 6.0, ((0, 4), (1, 32), (2, 2)), jnp.float32)
    sample_meridional_current = scatter_about(arg_keys[2], (K, NY, NX), 1.0, 6.0, ((0, 4), (1, 32), (2, 2)), jnp.float32)
    zonal_edge_layer_courant = jnp.clip(jnp.exp(math.log(0.45) - 1.50407736 * jax.random.uniform(arg_keys[3], (NY, NX), jnp.float32) ** block_scale(arg_keys[3], (NY, NX), ((0, 32), (1, 2)), -0.2, 0.2)), 0.1, 0.45)
    meridional_edge_layer_courant = jnp.clip(jnp.exp(math.log(0.45) - 1.50407736 * jax.random.uniform(arg_keys[4], (NY, NX), jnp.float32) ** block_scale(arg_keys[4], (NY, NX), ((0, 32), (1, 2)), -0.2, 0.2)), 0.1, 0.45)
    obs_index = touch_ends(jax.random.randint(arg_keys[5], (NREG, NOBS, 4), 0, 3 * CELLS_REG), jax.random.fold_in(arg_keys[5], 1), 0, (3 * CELLS_REG) - 1).astype(jnp.int32)
    obs_weight = jnp.clip(jnp.exp(math.log(1.0) - 2.3025851 * jax.random.uniform(arg_keys[6], (NREG, NOBS, 4), jnp.float32) ** block_scale(arg_keys[6], (NREG, NOBS, 4), ((0, 256),), -0.2, 0.2)), 0.1, 1.0)
    obs_value = scatter_about(arg_keys[7], (NREG, NOBS), 2.0, 12.0, ((0, 256),), jnp.float32)
    obs_var = jnp.clip(jnp.exp(math.log(4.0) - 2.7725887 * jax.random.uniform(arg_keys[8], (NREG, NOBS), jnp.float32) ** block_scale(arg_keys[8], (NREG, NOBS), ((0, 256),), -0.2, 0.2)), 0.25, 4.0)
    obs_count = draw_obs_count(jax.random.fold_in(arg_keys[11], 71), 0)
    fine_ctrl = scatter_about(arg_keys[10], (3, FNY, N_FINE, FNX // N_FINE), 1.0, 6.0, ((1, 32), (2, 2), (3, 4)), jnp.float32)
    return dict(sample_surface_elevation=sample_surface_elevation, sample_zonal_current=sample_zonal_current, sample_meridional_current=sample_meridional_current, zonal_edge_layer_courant=zonal_edge_layer_courant, meridional_edge_layer_courant=meridional_edge_layer_courant, obs_index=obs_index, obs_weight=obs_weight, obs_value=obs_value, obs_var=obs_var, obs_count=obs_count, fine_ctrl=fine_ctrl)


HIGHEST = lax.Precision.HIGHEST

def propagate_trajectories(sample_surface_elevation, sample_zonal_current, sample_meridional_current, zonal_edge_layer_courant, meridional_edge_layer_courant):
    for pass_no in range(STEPS):
        flux_u = zonal_edge_layer_courant * sample_zonal_current
        flux_v = meridional_edge_layer_courant * sample_meridional_current
        south_flux = jnp.concatenate([jnp.zeros_like(flux_v[:, :1]), flux_v[:, :-1]], axis=1)
        sample_surface_elevation = sample_surface_elevation - (flux_u - jnp.roll(flux_u, 1, axis=2) + flux_v - south_flux)
        north_rows = jnp.concatenate([sample_surface_elevation[:, 1:], jnp.zeros_like(sample_surface_elevation[:, :1])], axis=1)
        sample_zonal_current = sample_zonal_current - (jnp.roll(sample_surface_elevation, -1, axis=2) - sample_surface_elevation)
        sample_meridional_current = sample_meridional_current - (north_rows - sample_surface_elevation)
    return (sample_surface_elevation, sample_zonal_current, sample_meridional_current)

def to_regions(field):
    shaped = field.reshape(K, REG_DEV, N_REGION // REG_DEV, ROWS_DEV, N_FINE, N_MEMBER, N_REGION, RCOLS)
    shaped = shaped.transpose(5, 6, 4, 1, 0, 2, 3, 7)
    return shaped.reshape(NREG, K, CELLS_REG)

def from_regions(blocks):
    shaped = blocks.reshape(N_MEMBER, N_REGION, N_FINE, REG_DEV, K, N_REGION // REG_DEV, ROWS_DEV, RCOLS)
    shaped = shaped.transpose(4, 3, 5, 6, 2, 0, 1, 7)
    return shaped.reshape(K, NY, NX)

def increment_grid(blocks):
    shaped = blocks.reshape(N_MEMBER, N_REGION, N_FINE, REG_DEV, N_REGION // REG_DEV, ROWS_DEV, RCOLS)
    shaped = shaped.transpose(3, 4, 5, 2, 0, 1, 6)
    return shaped.reshape(NY, NX)

def analyse(packed):
    ensemble, region_index, region_weight, region_value, region_var, region_count = packed
    mean_state = lax.optimization_barrier(jnp.mean(ensemble, axis=0))
    spread = ensemble - mean_state
    picked = ensemble[:, region_index]
    predicted = lax.optimization_barrier(jnp.sum(picked * region_weight, axis=2))
    mean_obs = lax.optimization_barrier(jnp.mean(predicted, axis=0))
    obs_spread = predicted - mean_obs
    active_obs = (jnp.arange(NOBS) < region_count).astype(jnp.float32)
    weighted = obs_spread * (active_obs / region_var)
    gram_sum = jnp.dot(weighted, obs_spread.T, precision=HIGHEST)
    identity = jnp.eye(K, dtype=jnp.float32)
    scaled = identity + gram_sum / (K - 1)
    frobenius = jnp.sqrt(jnp.sum(scaled * scaled))
    iterate = scaled / frobenius
    inverse_root = identity
    for sweep in range(NEWTON):
        factor = 1.5 * identity - 0.5 * jnp.dot(inverse_root, iterate, precision=HIGHEST)
        iterate = jnp.dot(iterate, factor, precision=HIGHEST)
        inverse_root = jnp.dot(factor, inverse_root, precision=HIGHEST)
    transform = inverse_root / jnp.sqrt(frobenius)
    innovation = jnp.dot(region_value - mean_obs, weighted.T, precision=HIGHEST)
    halfway = jnp.dot(transform, innovation, precision=HIGHEST)
    mean_weights = jnp.dot(transform, halfway, precision=HIGHEST) / (K - 1)
    increment = jnp.dot(mean_weights, spread, precision=HIGHEST)
    members = (mean_state + increment)[None, :] + jnp.dot(transform.T, spread, precision=HIGHEST)
    return (members, increment)

def reference(sample_surface_elevation, sample_zonal_current, sample_meridional_current, zonal_edge_layer_courant, meridional_edge_layer_courant, obs_index, obs_weight, obs_value, obs_var, obs_count, fine_ctrl):
    prognostic_quantities = propagate_trajectories(sample_surface_elevation, sample_zonal_current, sample_meridional_current, zonal_edge_layer_courant, meridional_edge_layer_courant)
    ensemble = jnp.concatenate([to_regions(field) for field in prognostic_quantities], axis=2)
    members, increment = lax.map(analyse, (ensemble, obs_index, obs_weight, obs_value, obs_var, obs_count))
    outputs = [from_regions(members[:, :, vari * CELLS_REG:(vari + 1) * CELLS_REG]) for vari in range(3)]
    grids = jnp.stack([increment_grid(increment[:, vari * CELLS_REG:(vari + 1) * CELLS_REG]) for vari in range(3)])
    widened = jnp.repeat(jnp.repeat(grids, 2, axis=1), 2, axis=2)
    fine_out = fine_ctrl + widened.reshape(fine_ctrl.shape)
    return (outputs[0], outputs[1], outputs[2], fine_out)
```

```python
import functools

import jax
import jax.numpy as jnp
from jax import lax
from jax.experimental import pallas as pl
from jax.experimental.pallas import tpu as pltpu
from jax.sharding import PartitionSpec as P

MESH = pl.DeviceIdType.MESH
STEPS = 4
NEWTON = 8
HIGHEST = lax.Precision.HIGHEST
LANES = 128
MEMS = 64
COLS = 16


def dot(x, y, contract=((1,), (0,))):
    return lax.dot_general(
        x, y, (contract, ((), ())), precision=HIGHEST, preferred_element_type=jnp.float32
    )


def all_sum(x):
    return jnp.sum(jnp.sum(x, axis=1, keepdims=True), axis=0, keepdims=True)


def kernel(
    dims,
    h_ref, u_ref, v_ref, cu_ref, cv_ref, idx_ref, wt_ref, val_ref, var_ref, cnt_ref, fc_ref,
    ah_ref, au_ref, av_ref, fo_ref,
    out_box, in_box, c_out, c_in, to_west, to_east, from_east, from_west,
    state, cour_u, cour_v, stencil, ana, back_out, back_in, inc_out, inc_in,
    out_sem, in_sem, c_out_sem, c_in_sem, halo_sem, back_out_sem, back_in_sem, inc_out_sem,
    inc_in_sem,
):
    n_mem, n_reg = dims
    peers = n_mem * n_reg
    tiles = peers * COLS // LANES
    lane_tiles = n_mem * MEMS // LANES
    members = n_mem * MEMS
    half_rows = n_reg // 2
    cells = half_rows * COLS
    own_tiles = n_reg * COLS // LANES
    a = lax.axis_index("member")
    b = lax.axis_index("region")
    f = lax.axis_index("fine")
    me = a * n_reg + b

    def place(p):
        return (lax.div(p, n_reg), lax.rem(p, n_reg), f)

    ring = f * peers + me
    east = lax.rem(ring + 1, 2 * peers)
    west = lax.rem(ring + 2 * peers - 1, 2 * peers)

    def ring_place(n):
        p = lax.rem(n, peers)
        return (lax.div(p, n_reg), lax.rem(p, n_reg), lax.div(n, peers))

    barrier = pltpu.get_barrier_semaphore()

    def greet(i, carry):
        pl.semaphore_signal(
            barrier, inc=1, device_id=place(lax.rem(me + i, peers)), device_id_type=MESH
        )
        return carry

    lax.fori_loop(1, peers, greet, 0)
    pl.semaphore_signal(barrier, inc=1, device_id=ring_place(east), device_id_type=MESH)
    pl.semaphore_signal(barrier, inc=1, device_id=ring_place(west), device_id_type=MESH)

    lane = lax.broadcasted_iota(jnp.int32, (8, LANES), 1)
    left = lane < MEMS
    wide_lane = lax.broadcasted_iota(jnp.int32, (8, members), 1)
    low = lax.broadcasted_iota(jnp.int32, (8, members), 0) < 4

    def turned(block):
        pair = jnp.concatenate([block, pltpu.roll(block, LANES - 8, axis=1)], axis=0)
        return pair.T

    def pack(j, carry):
        for var, ref in enumerate((h_ref, u_ref, v_ref)):
            t = turned(ref[pl.ds(j, MEMS, stride=tiles), :])
            for k in range(8):
                out_box[j * 8 + k, var] = t[COLS * k : COLS * k + 8]
        return carry

    lax.fori_loop(0, tiles, pack, 0)
    for j in range(own_tiles):
        cu = jnp.broadcast_to(cu_ref[pl.ds(a * own_tiles + j, 1), :], (32, LANES))
        cv = jnp.broadcast_to(cv_ref[pl.ds(a * own_tiles + j, 1), :], (32, LANES))
        t = turned(jnp.concatenate([cu, cv], axis=0))
        for k in range(8):
            c_out[j * 8 + k] = t[COLS * k : COLS * k + 8]

    pl.semaphore_wait(barrier, peers + 1)

    def send_courant(i, carry):
        p = lax.rem(b + i, n_reg)
        pltpu.make_async_remote_copy(
            src_ref=c_out.at[p], dst_ref=c_in.at[b], send_sem=c_out_sem, recv_sem=c_in_sem,
            device_id=(a, p, f), device_id_type=MESH,
        ).start()
        return carry

    def send_state(i, carry):
        p = lax.rem(me + i * 37, peers)
        pltpu.make_async_remote_copy(
            src_ref=out_box.at[p], dst_ref=in_box.at[me], send_sem=out_sem, recv_sem=in_sem,
            device_id=place(p), device_id_type=MESH,
        ).start()
        return carry

    lax.fori_loop(1, n_reg, send_courant, 0)
    lax.fori_loop(1, peers, send_state, 0)
    c_in[b] = c_out[b]
    in_box[me] = out_box[me]

    obs = idx_ref.shape[2]
    for q in range(2):

        def spread_weights(g, carry):
            start = pl.multiple_of(g * 8, 8)
            cell = lax.broadcasted_iota(jnp.int32, (8, obs), 0) + g * 8
            total = jnp.zeros((8, obs), jnp.float32)
            for j in range(4):
                total += jnp.where(idx_ref[q, j : j + 1, :] == cell, wt_ref[q, j : j + 1, :], 0.0)
            stencil[q, pl.ds(start, 8), :] = total
            return carry

        lax.fori_loop(0, 3 * cells // 8, spread_weights, 0)

    def wait_bytes(ref, sem):
        pltpu.make_async_copy(ref, ref, sem).wait()

    wait_bytes(c_in.at[pl.ds(0, n_reg - 1)], c_in_sem)
    wait_bytes(in_box.at[pl.ds(0, peers - 1)], in_sem)

    def assemble(r, carry):
        c = c_in[r]
        for k in range(2):
            cour_u[r, 8 * k : 8 * k + 8] = jnp.broadcast_to(c[:, 64 * k : 64 * k + 1], (8, LANES))
            cour_v[r, 8 * k : 8 * k + 8] = jnp.broadcast_to(
                c[:, 64 * k + 32 : 64 * k + 33], (8, LANES)
            )
        for t in range(lane_tiles):
            at = slice(t * LANES, (t + 1) * LANES)
            for var in range(3):
                x = in_box[2 * t * n_reg + r, var]
                y = in_box[(2 * t + 1) * n_reg + r, var]
                state[var, r, 0:8, at] = jnp.where(left, x, pltpu.roll(y, MEMS, axis=1))
                state[var, r, 8:16, at] = jnp.where(left, pltpu.roll(x, MEMS, axis=1), y)
            c0 = jnp.where(left, cour_u[r, 0:8], cour_v[r, 0:8])
            c1 = jnp.where(left, cour_u[r, 8:16], cour_v[r, 8:16])
            low_t = low[:, at]

            def up(x):
                return pltpu.roll(x, 4, axis=0)

            to_west[r, 0, :, at] = jnp.where(
                low_t, state[0, r, 0:8, at], up(state[1, r, 0:8, at])
            )
            to_west[r, 1, :, at] = jnp.where(low_t, state[2, r, 0:8, at], up(c0))
            to_east[r, 0, :, at] = jnp.where(
                low_t, up(state[1, r, 8:16, at]), state[0, r, 8:16, at]
            )
            to_east[r, 1, :, at] = jnp.where(low_t, up(c1), state[2, r, 8:16, at])
        return carry

    lax.fori_loop(0, n_reg, assemble, 0)
    go_west = pltpu.make_async_remote_copy(
        src_ref=to_west, dst_ref=from_east, send_sem=halo_sem.at[0], recv_sem=halo_sem.at[1],
        device_id=ring_place(west), device_id_type=MESH,
    )
    go_east = pltpu.make_async_remote_copy(
        src_ref=to_east, dst_ref=from_west, send_sem=halo_sem.at[2], recv_sem=halo_sem.at[3],
        device_id=ring_place(east), device_id_type=MESH,
    )
    go_west.start()
    go_east.start()
    go_west.wait_recv()
    go_east.wait_recv()

    def rim(r, carry):
        for t in range(lane_tiles):
            at = slice(t * LANES, (t + 1) * LANES)
            low_t = low[:, at]
            e0, e1 = from_east[r, 0, :, at], from_east[r, 1, :, at]
            w0, w1 = from_west[r, 0, :, at], from_west[r, 1, :, at]
            state[0, r, 16:24, at] = jnp.where(low_t, e0, w0)
            state[1, r, 16:24, at] = pltpu.roll(jnp.where(low_t, w0, e0), 4, axis=0)
            state[2, r, 16:24, at] = jnp.where(low_t, e1, w1)
            if t == 0:
                c = pltpu.roll(jnp.where(low_t, w1, e1), 4, axis=0)
                cour_u[r, 16:24] = jnp.broadcast_to(c[:, 0:1], (8, LANES))
                cour_v[r, 16:24] = jnp.broadcast_to(c[:, 64:65], (8, LANES))
        return carry

    lax.fori_loop(0, n_reg, rim, 0)

    for t in range(lane_tiles):
        at = slice(t * LANES, (t + 1) * LANES)

        def advance(r, carry):
            flux_below, h_below, v_below = carry
            h, u, v = state[0, r, :, at], state[1, r, :, at], state[2, r, :, at]
            flux_u, flux_v = cour_u[r] * u, cour_v[r] * v
            h = h - (flux_u - pltpu.roll(flux_u, 1, axis=0) + flux_v - flux_below)
            state[0, r, :, at] = h
            state[1, r, :, at] = u - (pltpu.roll(h, 23, axis=0) - h)
            state[2, jnp.maximum(r - 1, 0), :, at] = v_below - (h - h_below)
            return flux_v, h, v

        def one_step(s, carry):
            zero = jnp.zeros((24, LANES), jnp.float32)
            _, h, v = lax.fori_loop(0, n_reg, advance, (zero, zero, zero))
            state[2, n_reg - 1, :, at] = v + h
            return carry

        lax.fori_loop(0, STEPS, one_step, 0)

    row_i = lax.broadcasted_iota(jnp.int32, (members, members), 0)
    col_i = lax.broadcasted_iota(jnp.int32, (members, members), 1)
    eye = jnp.where(row_i == col_i, 1.0, 0.0).astype(jnp.float32)
    obs_i = lax.broadcasted_iota(jnp.int32, (1, obs), 1)

    def cells_of(q, var):
        return state[var, q * half_rows : (q + 1) * half_rows, 0:16, :].reshape(cells, members)

    roots, fros, weights, innos = [], [], [], []
    for q in range(2):
        predicted = jnp.zeros((members, obs), jnp.float32)
        for var in range(3):
            predicted += dot(
                cells_of(q, var), stencil[q, var * cells : (var + 1) * cells, :], ((0,), (0,))
            )
        mean_obs = jnp.sum(predicted, axis=0, keepdims=True) / members
        obs_spread = predicted - mean_obs
        active = jnp.where(obs_i < cnt_ref[q], 1.0, 0.0)
        weighted = obs_spread * (active / var_ref[q : q + 1, :])
        scaled = eye + dot(weighted, obs_spread, ((1,), (1,))) / (members - 1)
        fro = jnp.sqrt(all_sum(scaled * scaled))
        iterate = scaled / fro
        factor = 1.5 * eye - 0.5 * iterate
        roots.append((dot(iterate, factor), factor))
        fros.append(fro)
        innos.append(
            jnp.sum(weighted * (val_ref[q : q + 1, :] - mean_obs), axis=1, keepdims=True)
        )

    def sweep(s, carry):
        new = []
        for iterate, root in carry:
            factor = 1.5 * eye - 0.5 * dot(root, iterate)
            new.append((dot(iterate, factor), dot(factor, root)))
        return tuple(new)

    roots = lax.fori_loop(1, NEWTON - 1, sweep, tuple(roots))

    for q in range(2):
        iterate, root = roots[q]
        factor = 1.5 * eye - 0.5 * dot(root, iterate)
        transform = dot(factor, root) / jnp.sqrt(fros[q])
        halfway = jnp.sum(transform * innos[q], axis=0, keepdims=True)
        mean_weights = jnp.sum(transform * halfway, axis=1, keepdims=True) / (members - 1)
        both = jnp.concatenate(
            [transform + mean_weights, jnp.broadcast_to(mean_weights, (members, LANES))], axis=1
        )
        for var in range(3):
            x = cells_of(q, var)
            mean_state = jnp.sum(x, axis=1, keepdims=True) / members
            moved = dot(x - mean_state, both)
            ana[var, :, 0:members] = moved[:, 0:members] + mean_state
            ana[var, :, members:] = moved[:, members:]

        def unload(i, carry):
            lo = pl.multiple_of(i * COLS, 8)
            hi = pl.multiple_of(i * COLS + 8, 8)
            row = q * half_rows + i
            for t in range(lane_tiles):
                at = slice(t * LANES, (t + 1) * LANES)
                for var in range(3):
                    x, y = ana[var, pl.ds(lo, 8), at], ana[var, pl.ds(hi, 8), at]
                    back_out[2 * t * n_reg + row, var] = jnp.where(
                        left, x, pltpu.roll(y, MEMS, axis=1)
                    )
                    back_out[(2 * t + 1) * n_reg + row, var] = jnp.where(
                        left, pltpu.roll(x, MEMS, axis=1), y
                    )
            packed = jnp.zeros((8, LANES), jnp.float32)
            for var in range(3):
                x = ana[var, pl.ds(lo, 8), members:]
                y = ana[var, pl.ds(hi, 8), members:]
                packed = jnp.where(lax.rem(lane, MEMS) // 16 == var, jnp.where(left, x, y), packed)
            inc_out[row] = packed
            return carry

        lax.fori_loop(0, half_rows, unload, 0)

        def send_inc(i, carry):
            p = q * half_rows + lax.rem(b + i, half_rows)

            @pl.when(p != b)
            def _():
                pltpu.make_async_remote_copy(
                    src_ref=inc_out.at[p], dst_ref=inc_in.at[b], send_sem=inc_out_sem,
                    recv_sem=inc_in_sem, device_id=(a, p, f), device_id_type=MESH,
                ).start()

            return carry

        def send_back(i, carry):
            p_mem = lax.rem(a + i, n_mem)
            p_row = q * half_rows + lax.rem(b + lax.div(i, n_mem), half_rows)
            p = p_mem * n_reg + p_row

            @pl.when(p != me)
            def _():
                pltpu.make_async_remote_copy(
                    src_ref=back_out.at[p], dst_ref=back_in.at[me], send_sem=back_out_sem,
                    recv_sem=back_in_sem, device_id=(p_mem, p_row, f), device_id_type=MESH,
                ).start()

            return carry

        lax.fori_loop(0, half_rows, send_inc, 0)
        lax.fori_loop(0, n_mem * half_rows, send_back, 0)

    inc_in[b] = inc_out[b]
    back_in[me] = back_out[me]
    wait_bytes(inc_in.at[pl.ds(0, n_reg - 1)], inc_in_sem)

    def straight(blocks):
        rolled = pltpu.roll(blocks, MEMS, axis=2)
        return jnp.stack([blocks, rolled], axis=1).reshape(LANES, LANES).T

    fine_i = lax.broadcasted_iota(jnp.int32, (LANES, 2 * LANES), 1)
    coarse_i = lax.broadcasted_iota(jnp.int32, (LANES, 2 * LANES), 0)
    widen = jnp.where(lax.div(fine_i, 2) == coarse_i, 1.0, 0.0).astype(jnp.float32)
    for j in range(own_tiles):
        at = slice(2 * j * LANES, 2 * (j + 1) * LANES)
        wide = dot(straight(inc_in[8 * j : 8 * j + 8])[0:64], widen)
        for var in range(3):
            for e in range(2):
                fo_ref[var, e, 0:1, at] = fc_ref[var, e, 0:1, at] + wide[16 * var : 16 * var + 1]

    wait_bytes(back_in.at[pl.ds(0, peers - 1)], back_in_sem)

    def unpack(j, carry):
        for var, ref in enumerate((ah_ref, au_ref, av_ref)):
            start = pl.multiple_of(j * 8, 8)
            blocks = back_in[pl.ds(start, 8), var]
            ref[pl.ds(j, MEMS, stride=tiles), :] = straight(blocks)[0:MEMS]
        return carry

    lax.fori_loop(0, tiles, unpack, 0)

    wait_bytes(c_out.at[pl.ds(0, n_reg - 1)], c_out_sem)
    wait_bytes(out_box.at[pl.ds(0, peers - 1)], out_sem)
    wait_bytes(inc_out.at[pl.ds(0, n_reg - 1)], inc_out_sem)
    wait_bytes(back_out.at[pl.ds(0, peers - 1)], back_out_sem)
    go_west.wait_send()
    go_east.wait_send()


def step(n_mem, n_reg, h, u, v, cu, cv, obs_index, obs_weight, obs_value, obs_var, obs_count, fine):
    peers = n_mem * n_reg
    members = n_mem * MEMS
    tiles = peers * COLS // LANES
    obs = obs_value.shape[1]
    cells = n_reg // 2 * COLS
    f32 = jnp.float32
    flat = (MEMS * tiles, LANES)
    vmem = pl.BlockSpec(memory_space=pltpu.VMEM)
    dma = pltpu.SemaphoreType.DMA
    outs = pl.pallas_call(
        functools.partial(kernel, (n_mem, n_reg)),
        out_shape=[jax.ShapeDtypeStruct(flat, f32)] * 3 + [jax.ShapeDtypeStruct(fine.shape, f32)],
        in_specs=[vmem] * 9 + [pl.BlockSpec(memory_space=pltpu.SMEM), vmem],
        out_specs=[vmem] * 4,
        scratch_shapes=[
            pltpu.VMEM((peers, 3, 8, LANES), f32),
            pltpu.VMEM((peers, 3, 8, LANES), f32),
            pltpu.VMEM((n_reg, 8, LANES), f32),
            pltpu.VMEM((n_reg, 8, LANES), f32),
            pltpu.VMEM((n_reg, 2, 8, members), f32),
            pltpu.VMEM((n_reg, 2, 8, members), f32),
            pltpu.VMEM((n_reg, 2, 8, members), f32),
            pltpu.VMEM((n_reg, 2, 8, members), f32),
            pltpu.VMEM((3, n_reg, 24, members), f32),
            pltpu.VMEM((n_reg, 24, LANES), f32),
            pltpu.VMEM((n_reg, 24, LANES), f32),
            pltpu.VMEM((2, 3 * cells, obs), f32),
            pltpu.VMEM((3, cells, members + LANES), f32),
            pltpu.VMEM((peers, 3, 8, LANES), f32),
            pltpu.VMEM((peers, 3, 8, LANES), f32),
            pltpu.VMEM((n_reg, 8, LANES), f32),
            pltpu.VMEM((n_reg, 8, LANES), f32),
            dma, dma, dma, dma, dma((4,)), dma, dma, dma, dma,
        ],
        compiler_params=pltpu.CompilerParams(
            collective_id=0, has_side_effects=True, vmem_limit_bytes=56 * 1024 * 1024
        ),
    )(
        h.reshape(flat), u.reshape(flat), v.reshape(flat),
        cu.reshape(tiles, LANES), cv.reshape(tiles, LANES),
        obs_index.transpose(0, 2, 1), obs_weight.transpose(0, 2, 1),
        obs_value, obs_var, obs_count, fine,
    )
    return tuple(x.reshape(h.shape) for x in outs[:3]) + (outs[3],)


def solution(mesh):
    fields = P("member", "region", "fine")
    regions = ("member", "region", "fine")
    fine = P(None, "region", "fine", "member")
    return jax.shard_map(
        functools.partial(step, mesh.shape["member"], mesh.shape["region"]),
        mesh=mesh,
        in_specs=(
            fields, fields, fields,
            P("region", "fine"), P("region", "fine"),
            P(regions, None, None), P(regions, None, None),
            P(regions, None), P(regions, None), P(regions),
            fine,
        ),
        out_specs=(fields, fields, fields, fine),
        check_vma=False,
    )
```

```python
import functools

import jax
import jax.numpy as jnp
from jax import lax
from jax.experimental import pallas as pl
from jax.experimental.pallas import tpu as pltpu
from jax.sharding import PartitionSpec as P

MESH = pl.DeviceIdType.MESH
STEPS = 4
NEWTON = 8
HIGHEST = lax.Precision.HIGHEST
LANES = 128
MEMS = 64
COLS = 16


ROWS_COLS = ((1,), (0,))


def dot(x, y, contract=ROWS_COLS, precision=None):
    return lax.dot_general(
        x, y, (contract, ((), ())), precision=precision, preferred_element_type=jnp.float32
    )


def split(x):
    high = x.astype(jnp.bfloat16)
    return high, (x - high.astype(jnp.float32)).astype(jnp.bfloat16)


def dot3(x, y, contract=ROWS_COLS):
    small = dot(x[0], y[1], contract) + dot(x[1], y[0], contract)
    return dot(x[0], y[0], contract) + small


def all_sum(x):
    return jnp.sum(jnp.sum(x, axis=1, keepdims=True), axis=0, keepdims=True)


def kernel(
    dims,
    h_ref, u_ref, v_ref, cu_ref, cv_ref, idx_ref, wt_ref, val_ref, var_ref, cnt_ref, fc_ref,
    ah_ref, au_ref, av_ref, fo_ref,
    out_box, in_box, c_out, c_in, to_west, to_east, from_east, from_west,
    window, cour_u, cour_v, state, stencil, stencil_hi, stencil_lo, ana,
    back_out, back_in, inc_out, inc_in,
    out_sem, in_sem, c_out_sem, c_in_sem, halo_out_sem, halo_in_sem,
    back_out_sem, back_in_sem, inc_out_sem, inc_in_sem,
):
    n_mem, n_reg = dims
    peers = n_mem * n_reg
    tiles = peers * COLS // LANES
    lane_tiles = n_mem * MEMS // LANES
    members = n_mem * MEMS
    half_rows = n_reg // 2
    cells = half_rows * COLS
    own_tiles = n_reg * COLS // LANES
    phases = [[0], [1, 3], [2]] if n_mem == 4 else [[s] for s in range(n_mem)]
    order = [s for phase in phases for s in phase]
    a = lax.axis_index("member")
    b = lax.axis_index("region")
    f = lax.axis_index("fine")
    me = a * n_reg + b

    def place(p):
        return (lax.div(p, n_reg), lax.rem(p, n_reg), f)

    ring = f * peers + me
    east = lax.rem(ring + 1, 2 * peers)
    west = lax.rem(ring + 2 * peers - 1, 2 * peers)

    def ring_place(n):
        p = lax.rem(n, peers)
        return (lax.div(p, n_reg), lax.rem(p, n_reg), lax.div(n, peers))

    barrier = pltpu.get_barrier_semaphore()

    def greet(i, carry):
        pl.semaphore_signal(
            barrier, inc=1, device_id=place(lax.rem(me + i, peers)), device_id_type=MESH
        )
        return carry

    lax.fori_loop(1, peers, greet, 0)
    pl.semaphore_signal(barrier, inc=1, device_id=ring_place(east), device_id_type=MESH)
    pl.semaphore_signal(barrier, inc=1, device_id=ring_place(west), device_id_type=MESH)

    lane = lax.broadcasted_iota(jnp.int32, (8, LANES), 1)
    left = lane < MEMS
    low = lax.broadcasted_iota(jnp.int32, (8, LANES), 0) < 4
    crossed = (low & ~left) | (~low & left)

    def across(x):
        return pltpu.roll(x, MEMS, axis=1)

    def up(x):
        return pltpu.roll(x, 4, axis=0)

    def turned(block):
        pair = jnp.concatenate([block, pltpu.roll(block, LANES - 8, axis=1)], axis=0)
        return pair.T

    def pack(j, carry):
        for var, ref in enumerate((h_ref, u_ref, v_ref)):
            t = turned(ref[pl.ds(j, MEMS, stride=tiles), :])
            for k in range(8):
                out_box[j * 8 + k, var] = t[COLS * k : COLS * k + 8]
        return carry

    lax.fori_loop(0, tiles, pack, 0)
    for j in range(own_tiles):
        cu = jnp.broadcast_to(cu_ref[pl.ds(a * own_tiles + j, 1), :], (32, LANES))
        cv = jnp.broadcast_to(cv_ref[pl.ds(a * own_tiles + j, 1), :], (32, LANES))
        t = turned(jnp.concatenate([cu, cv], axis=0))
        for k in range(8):
            c_out[j * 8 + k] = t[COLS * k : COLS * k + 8]

    pl.semaphore_wait(barrier, peers + 1)

    def send_courant(i, carry):
        p = lax.rem(b + i, n_reg)
        pltpu.make_async_remote_copy(
            src_ref=c_out.at[p], dst_ref=c_in.at[b], send_sem=c_out_sem, recv_sem=c_in_sem,
            device_id=(a, p, f), device_id_type=MESH,
        ).start()
        return carry

    lax.fori_loop(1, n_reg, send_courant, 0)
    c_in[b] = c_out[b]
    in_box[0, b] = out_box[me]

    for phase in phases:

        def send_state(i, carry):
            p_row = lax.rem(b + i, n_reg)
            for s in phase:
                p_mem = lax.rem(a + s, n_mem)
                slot = (n_mem - s) % n_mem
                pltpu.make_async_remote_copy(
                    src_ref=out_box.at[p_mem * n_reg + p_row], dst_ref=in_box.at[slot, b],
                    send_sem=out_sem, recv_sem=in_sem.at[slot],
                    device_id=(p_mem, p_row, f), device_id_type=MESH,
                ).start()
            return carry

        lax.fori_loop(1 if phase == [0] else 0, n_reg, send_state, 0)

    obs = idx_ref.shape[2]
    for q in range(2):

        def spread_weights(g, carry):
            start = pl.multiple_of(g * 16, 16)
            cell = lax.broadcasted_iota(jnp.int32, (16, obs), 0) + g * 16
            total = jnp.zeros((16, obs), jnp.float32)
            for j in range(4):
                total += jnp.where(idx_ref[q, j : j + 1, :] == cell, wt_ref[q, j : j + 1, :], 0.0)
            high, rest = split(total)
            stencil[q, pl.ds(start, 16), :] = total
            stencil_hi[q, pl.ds(start, 16), :] = high
            stencil_lo[q, pl.ds(start, 16), :] = rest
            return carry

        lax.fori_loop(0, 3 * cells // 16, spread_weights, 0)

    def wait_bytes(ref, sem):
        pltpu.make_async_copy(ref, ref, sem).wait()

    wait_bytes(c_in.at[pl.ds(0, n_reg - 1)], c_in_sem)

    def halo_copies(s):
        there_west = lax.rem(s + a - ring_place(west)[0] + n_mem, n_mem)
        there_east = lax.rem(s + a - ring_place(east)[0] + n_mem, n_mem)
        go_west = pltpu.make_async_remote_copy(
            src_ref=to_west.at[s], dst_ref=from_east.at[there_west],
            send_sem=halo_out_sem.at[0, s], recv_sem=halo_in_sem.at[0, there_west],
            device_id=ring_place(west), device_id_type=MESH,
        )
        go_east = pltpu.make_async_remote_copy(
            src_ref=to_east.at[s], dst_ref=from_west.at[there_east],
            send_sem=halo_out_sem.at[1, s], recv_sem=halo_in_sem.at[1, there_east],
            device_id=ring_place(east), device_id_type=MESH,
        )
        return go_west, go_east

    def send_rim(s):
        wait_bytes(in_box.at[s, pl.ds(0, n_reg - 1 if s == 0 else n_reg)], in_sem.at[s])

        def quarter(r, carry):
            h, u, v = in_box[s, r, 0], in_box[s, r, 1], in_box[s, r, 2]
            c, u = across(c_in[r]), across(u)
            to_west[s, r] = jnp.where(low, jnp.where(left, h, u), up(jnp.where(left, v, c)))
            to_east[s, r] = jnp.where(low, up(jnp.where(left, c, v)), jnp.where(left, u, h))
            return carry

        lax.fori_loop(0, n_reg, quarter, 0, unroll=2)
        for copy in halo_copies(s):
            copy.start()

    def broad(c, at):
        shape = (8, LANES)
        return jnp.where(
            left,
            jnp.broadcast_to(c[:, at : at + 1], shape),
            jnp.broadcast_to(c[:, at + MEMS : at + MEMS + 1], shape),
        )

    def forecast(s):
        wait_bytes(from_east.at[s], halo_in_sem.at[0, s])
        wait_bytes(from_west.at[s], halo_in_sem.at[1, s])

        def rim(r, carry):
            e, w = from_east[s, r], from_west[s, r]
            p, q = jnp.where(low, e, w), up(jnp.where(low, w, e))
            h, u, v = in_box[s, r, 0], in_box[s, r, 1], in_box[s, r, 2]
            window[0, r, 0:8] = h
            window[1, r, 0:8] = u
            window[2, r, 0:8] = v
            window[0, r, 8:16] = across(jnp.where(crossed, h, p))
            window[1, r, 8:16] = jnp.where(crossed, p, across(u))
            window[2, r, 8:16] = across(jnp.where(crossed, v, q))
            if s == 0:
                c = c_in[r]
                cour_u[r, 0:8] = broad(c, 0)
                cour_v[r, 0:8] = broad(c, 32)
                c = jnp.where(crossed, q, across(c))
                cour_u[r, 8:16] = broad(c, 0)
                cour_v[r, 8:16] = broad(c, 32)
            return carry

        lax.fori_loop(0, n_reg, rim, 0, unroll=2)

        def advance(r, carry):
            flux_below, h_below, v_below = carry
            h, u, v = window[0, r], window[1, r], window[2, r]
            flux_u, flux_v = cour_u[r] * u, cour_v[r] * v
            h = h - (flux_u - pltpu.roll(flux_u, 1, axis=0) + flux_v - flux_below)
            window[0, r] = h
            window[1, r] = u - (pltpu.roll(h, 15, axis=0) - h)
            window[2, jnp.maximum(r - 1, 0)] = v_below - (h - h_below)
            return flux_v, h, v

        def one_step(i, carry):
            zero = jnp.zeros((16, LANES), jnp.float32)
            _, h, v = lax.fori_loop(0, n_reg, advance, (zero, zero, zero), unroll=4)
            window[2, n_reg - 1] = v + h
            return carry

        lax.fori_loop(0, STEPS, one_step, 0)
        at = slice(s // 2 * LANES, (s // 2 + 1) * LANES)
        keep = left if s % 2 else ~left

        def place_cells(r, carry):
            for var in range(3):
                x = window[var, r, 0:8]
                y = across(x)
                x, y = (y, x) if s % 2 else (x, y)
                state[var, r, 0:8, at] = jnp.where(keep, state[var, r, 0:8, at], x)
                state[var, r, 8:16, at] = jnp.where(keep, state[var, r, 8:16, at], y)
            return carry

        lax.fori_loop(0, n_reg, place_cells, 0, unroll=2)

    for i, s in enumerate(order):
        send_rim(s)
        if i > 0:
            forecast(order[i - 1])
    forecast(order[-1])

    row_i = lax.broadcasted_iota(jnp.int32, (members, members), 0)
    col_i = lax.broadcasted_iota(jnp.int32, (members, members), 1)
    eye = jnp.where(row_i == col_i, 1.0, 0.0).astype(jnp.float32)
    obs_i = lax.broadcasted_iota(jnp.int32, (1, obs), 1)

    for q in range(2):
        spreads, means = [], []
        obs_spread = jnp.zeros((members, obs), jnp.float32)
        mean_obs = jnp.zeros((1, obs), jnp.float32)
        for var in range(3):
            x = state[var, q * half_rows : (q + 1) * half_rows].reshape(cells, members)
            mean = jnp.sum(x, axis=1, keepdims=True) / members
            spread = split(x - mean)
            block = slice(var * cells, (var + 1) * cells)
            weights = (stencil_hi[q, block, :], stencil_lo[q, block, :])
            obs_spread += dot3(spread, weights, ((0,), (0,)))
            mean_obs += jnp.sum(stencil[q, block, :] * mean, axis=0, keepdims=True)
            spreads.append(spread)
            means.append(mean)
        active = jnp.where(obs_i < cnt_ref[q], 1.0, 0.0)
        weighted = obs_spread * (active / var_ref[q : q + 1, :])
        gram_sum = dot3(split(weighted), split(obs_spread), ((1,), (1,)))
        scaled = eye + gram_sum / (members - 1)
        fro = jnp.sqrt(all_sum(scaled * scaled))
        innovation = jnp.sum(weighted * (val_ref[q : q + 1, :] - mean_obs), axis=1, keepdims=True)
        iterate = scaled / fro
        factor = split(1.5 * eye - 0.5 * iterate)

        def sweep(i, carry):
            iterate, root = carry
            factor = split(1.5 * eye - 0.5 * dot3(root, iterate))
            return split(dot3(iterate, factor)), split(dot3(factor, root))

        iterate, root = lax.fori_loop(
            1, NEWTON - 1, sweep, (split(dot3(split(iterate), factor)), factor)
        )
        factor = split(1.5 * eye - 0.5 * dot3(root, iterate))
        transform = dot3(factor, root) / jnp.sqrt(fro)
        halfway = jnp.sum(transform * innovation, axis=0, keepdims=True)
        mean_weights = jnp.sum(transform * halfway, axis=1, keepdims=True) / (members - 1)
        both = split(jnp.concatenate(
            [transform + mean_weights, jnp.broadcast_to(mean_weights, (members, LANES))], axis=1
        ))
        for var in range(3):
            moved = dot3(spreads[var], both)
            ana[var, :, 0:members] = moved[:, 0:members] + means[var]
            ana[var, :, members:] = moved[:, members:]

        def unload(i, carry):
            lo = pl.multiple_of(i * COLS, 8)
            hi = pl.multiple_of(i * COLS + 8, 8)
            row = q * half_rows + i
            for t in range(lane_tiles):
                at = slice(t * LANES, (t + 1) * LANES)
                for var in range(3):
                    x, y = ana[var, pl.ds(lo, 8), at], ana[var, pl.ds(hi, 8), at]
                    back_out[2 * t, row, var] = jnp.where(left, x, across(y))
                    back_out[2 * t + 1, row, var] = jnp.where(left, across(x), y)
            packed = jnp.zeros((8, LANES), jnp.float32)
            for var in range(3):
                x = ana[var, pl.ds(lo, 8), members:]
                y = ana[var, pl.ds(hi, 8), members:]
                packed = jnp.where(lax.div(lax.rem(lane, MEMS), 16) == var, jnp.where(left, x, y), packed)
            inc_out[row] = packed
            return carry

        lax.fori_loop(0, half_rows, unload, 0, unroll=2)

        def send_inc(i, carry):
            p = q * half_rows + lax.rem(b + i, half_rows)

            @pl.when(p != b)
            def _():
                pltpu.make_async_remote_copy(
                    src_ref=inc_out.at[p], dst_ref=inc_in.at[b], send_sem=inc_out_sem,
                    recv_sem=inc_in_sem, device_id=(a, p, f), device_id_type=MESH,
                ).start()

            return carry

        lax.fori_loop(0, half_rows, send_inc, 0)
        for phase in phases:

            def send_back(i, carry):
                p_row = q * half_rows + lax.rem(b + i, half_rows)
                for s in phase:
                    slot = (n_mem - s) % n_mem
                    copy = pltpu.make_async_remote_copy(
                        src_ref=back_out.at[s, p_row], dst_ref=back_in.at[slot, b],
                        send_sem=back_out_sem, recv_sem=back_in_sem.at[slot],
                        device_id=(lax.rem(a + s, n_mem), p_row, f), device_id_type=MESH,
                    )
                    if s == 0:
                        pl.when(p_row != b)(copy.start)
                    else:
                        copy.start()
                return carry

            lax.fori_loop(0, half_rows, send_back, 0)

    inc_in[b] = inc_out[b]
    back_in[0, b] = back_out[0, b]
    wait_bytes(inc_in.at[pl.ds(0, n_reg - 1)], inc_in_sem)

    def straight(blocks):
        return jnp.stack([blocks, pltpu.roll(blocks, MEMS, axis=2)], axis=1).reshape(LANES, LANES).T

    fine_i = lax.broadcasted_iota(jnp.int32, (LANES, 2 * LANES), 1)
    coarse_i = lax.broadcasted_iota(jnp.int32, (LANES, 2 * LANES), 0)
    widen = jnp.where(lax.div(fine_i, 2) == coarse_i, 1.0, 0.0).astype(jnp.float32)
    for j in range(own_tiles):
        at = slice(2 * j * LANES, 2 * (j + 1) * LANES)
        wide = dot(straight(inc_in[8 * j : 8 * j + 8])[0:64], widen, precision=HIGHEST)
        for var in range(3):
            for e in range(2):
                fo_ref[var, e, 0:1, at] = fc_ref[var, e, 0:1, at] + wide[16 * var : 16 * var + 1]

    for s in order:
        wait_bytes(back_in.at[s, pl.ds(0, n_reg - 1 if s == 0 else n_reg)], back_in_sem.at[s])
        first = lax.rem(a + s, n_mem) * own_tiles

        def unpack(j, carry):
            for var, ref in enumerate((ah_ref, au_ref, av_ref)):
                start = pl.multiple_of(j * 8, 8)
                blocks = back_in[s, pl.ds(start, 8), var]
                ref[pl.ds(first + j, MEMS, stride=tiles), :] = straight(blocks)[0:MEMS]
            return carry

        lax.fori_loop(0, own_tiles, unpack, 0)

    wait_bytes(c_out.at[pl.ds(0, n_reg - 1)], c_out_sem)
    wait_bytes(out_box.at[pl.ds(0, peers - 1)], out_sem)
    wait_bytes(inc_out.at[pl.ds(0, n_reg - 1)], inc_out_sem)
    wait_bytes(out_box.at[pl.ds(0, peers - 1)], back_out_sem)
    for s in order:
        for copy in halo_copies(s):
            copy.wait_send()


def step(n_mem, n_reg, h, u, v, cu, cv, obs_index, obs_weight, obs_value, obs_var, obs_count, fine):
    peers = n_mem * n_reg
    members = n_mem * MEMS
    tiles = peers * COLS // LANES
    obs = obs_value.shape[1]
    cells = n_reg // 2 * COLS
    f32 = jnp.float32
    flat = (MEMS * tiles, LANES)
    vmem = pl.BlockSpec(memory_space=pltpu.VMEM)
    dma = pltpu.SemaphoreType.DMA
    outs = pl.pallas_call(
        functools.partial(kernel, (n_mem, n_reg)),
        out_shape=[jax.ShapeDtypeStruct(flat, f32)] * 3 + [jax.ShapeDtypeStruct(fine.shape, f32)],
        in_specs=[vmem] * 9 + [pl.BlockSpec(memory_space=pltpu.SMEM), vmem],
        out_specs=[vmem] * 4,
        scratch_shapes=[
            pltpu.VMEM((peers, 3, 8, LANES), f32),
            pltpu.VMEM((n_mem, n_reg, 3, 8, LANES), f32),
            pltpu.VMEM((n_reg, 8, LANES), f32),
            pltpu.VMEM((n_reg, 8, LANES), f32),
            pltpu.VMEM((n_mem, n_reg, 8, LANES), f32),
            pltpu.VMEM((n_mem, n_reg, 8, LANES), f32),
            pltpu.VMEM((n_mem, n_reg, 8, LANES), f32),
            pltpu.VMEM((n_mem, n_reg, 8, LANES), f32),
            pltpu.VMEM((3, n_reg, 16, LANES), f32),
            pltpu.VMEM((n_reg, 16, LANES), f32),
            pltpu.VMEM((n_reg, 16, LANES), f32),
            pltpu.VMEM((3, n_reg, 16, members), f32),
            pltpu.VMEM((2, 3 * cells, obs), f32),
            pltpu.VMEM((2, 3 * cells, obs), jnp.bfloat16),
            pltpu.VMEM((2, 3 * cells, obs), jnp.bfloat16),
            pltpu.VMEM((3, cells, members + LANES), f32),
            pltpu.VMEM((n_mem, n_reg, 3, 8, LANES), f32),
            pltpu.VMEM((n_mem, n_reg, 3, 8, LANES), f32),
            pltpu.VMEM((n_reg, 8, LANES), f32),
            pltpu.VMEM((n_reg, 8, LANES), f32),
            dma, dma((n_mem,)), dma, dma, dma((2, n_mem)), dma((2, n_mem)),
            dma, dma((n_mem,)), dma, dma,
        ],
        compiler_params=pltpu.CompilerParams(
            collective_id=0, has_side_effects=True, vmem_limit_bytes=56 * 1024 * 1024
        ),
    )(
        h.reshape(flat), u.reshape(flat), v.reshape(flat),
        cu.reshape(tiles, LANES), cv.reshape(tiles, LANES),
        obs_index.transpose(0, 2, 1), obs_weight.transpose(0, 2, 1),
        obs_value, obs_var, obs_count, fine,
    )
    return tuple(x.reshape(h.shape) for x in outs[:3]) + (outs[3],)


def solution(mesh):
    fields = P("member", "region", "fine")
    regions = ("member", "region", "fine")
    fine = P(None, "region", "fine", "member")
    return jax.shard_map(
        functools.partial(step, mesh.shape["member"], mesh.shape["region"]),
        mesh=mesh,
        in_specs=(
            fields, fields, fields,
            P("region", "fine"), P("region", "fine"),
            P(regions, None, None), P(regions, None, None),
            P(regions, None), P(regions, None), P(regions),
            fine,
        ),
        out_specs=(fields, fields, fields, fine),
        check_vma=False,
    )
```

```python
import functools

import jax
import jax.numpy as jnp
from jax import lax
from jax.experimental import pallas as pl
from jax.experimental.pallas import tpu as pltpu
from jax.sharding import PartitionSpec as P

MESH = pl.DeviceIdType.MESH
STEPS = 4
NEWTON = 8
HIGHEST = lax.Precision.HIGHEST
LANES = 128
MEMS = 64
COLS = 16


ROWS_COLS = ((1,), (0,))


def dot(x, y, contract=ROWS_COLS, precision=None):
    return lax.dot_general(
        x, y, (contract, ((), ())), precision=precision, preferred_element_type=jnp.float32
    )


def split(x):
    high = x.astype(jnp.bfloat16)
    return high, (x - high.astype(jnp.float32)).astype(jnp.bfloat16)


def dot3(x, y, contract=ROWS_COLS):
    rows = 1 - contract[0][0]
    size = x[0].shape[rows]
    both = dot(jnp.concatenate(x, axis=rows), y[0], contract)
    return both[:size] + (both[size:] + dot(x[0], y[1], contract))


def all_sum(x):
    return jnp.sum(jnp.sum(x, axis=1, keepdims=True), axis=0, keepdims=True)


def kernel(
    dims,
    h_ref, u_ref, v_ref, cu_ref, cv_ref, idx_ref, wt_ref, val_ref, var_ref, cnt_ref, fc_ref,
    ah_ref, au_ref, av_ref, fo_ref,
    out_box, in_box, c_out, c_in, to_west, to_east, from_east, from_west,
    window, cour_u, cour_v, state, stencil, stencil_hi, stencil_lo, ana,
    back_out, back_in, inc_out, inc_in,
    out_sem, in_sem, c_out_sem, c_in_sem, halo_out_sem, halo_in_sem,
    back_out_sem, back_in_sem, inc_out_sem, inc_in_sem,
):
    n_mem, n_reg = dims
    peers = n_mem * n_reg
    tiles = peers * COLS // LANES
    lane_tiles = n_mem * MEMS // LANES
    members = n_mem * MEMS
    half_rows = n_reg // 2
    cells = half_rows * COLS
    own_tiles = n_reg * COLS // LANES
    phases = [[0], [1, 3], [2]] if n_mem == 4 else [[s] for s in range(n_mem)]
    order = [s for phase in phases for s in phase]
    a = lax.axis_index("member")
    b = lax.axis_index("region")
    f = lax.axis_index("fine")
    me = a * n_reg + b

    def place(p):
        return (lax.div(p, n_reg), lax.rem(p, n_reg), f)

    ring = f * peers + me
    east = lax.rem(ring + 1, 2 * peers)
    west = lax.rem(ring + 2 * peers - 1, 2 * peers)

    def ring_place(n):
        p = lax.rem(n, peers)
        return (lax.div(p, n_reg), lax.rem(p, n_reg), lax.div(n, peers))

    barrier = pltpu.get_barrier_semaphore()

    def greet(i):
        pl.semaphore_signal(
            barrier, inc=1, device_id=place(lax.rem(me + i, peers)), device_id_type=MESH
        )

    pl.semaphore_signal(barrier, inc=1, device_id=ring_place(east), device_id_type=MESH)
    pl.semaphore_signal(barrier, inc=1, device_id=ring_place(west), device_id_type=MESH)

    lane = lax.broadcasted_iota(jnp.int32, (8, LANES), 1)
    left = lane < MEMS
    low = lax.broadcasted_iota(jnp.int32, (8, LANES), 0) < 4
    crossed = (low & ~left) | (~low & left)

    def across(x):
        return pltpu.roll(x, MEMS, axis=x.ndim - 1)

    def up(x):
        return pltpu.roll(x, 4, axis=x.ndim - 2)

    def turned(block):
        pair = jnp.concatenate([block, pltpu.roll(block, LANES - 8, axis=1)], axis=0)
        return pair.T

    def pack_tile(j):
        for var, ref in enumerate((h_ref, u_ref, v_ref)):
            t = turned(ref[pl.ds(j, MEMS, stride=tiles), :])
            for k in range(8):
                out_box[j * 8 + k, var] = t[COLS * k : COLS * k + 8]

    def pack(j, carry):
        for k in range(8):
            greet(j * 8 + k + 1)
        pack_tile(j)
        return carry

    lax.fori_loop(0, tiles - 1, pack, 0)
    for k in range(7):
        greet(peers - 7 + k)
    pack_tile(tiles - 1)
    for j in range(own_tiles):
        cu = jnp.broadcast_to(cu_ref[pl.ds(a * own_tiles + j, 1), :], (32, LANES))
        cv = jnp.broadcast_to(cv_ref[pl.ds(a * own_tiles + j, 1), :], (32, LANES))
        t = turned(jnp.concatenate([cu, cv], axis=0))
        for k in range(8):
            c_out[j * 8 + k] = t[COLS * k : COLS * k + 8]

    pl.semaphore_wait(barrier, peers + 1)

    def send_courant(i, carry):
        p = lax.rem(b + i, n_reg)
        pltpu.make_async_remote_copy(
            src_ref=c_out.at[p], dst_ref=c_in.at[b], send_sem=c_out_sem, recv_sem=c_in_sem,
            device_id=(a, p, f), device_id_type=MESH,
        ).start()
        return carry

    lax.fori_loop(1, n_reg, send_courant, 0)
    c_in[b] = c_out[b]
    in_box[0, b] = out_box[me]

    for phase in phases:

        def send_state(i, carry):
            p_row = lax.rem(b + i, n_reg)
            for s in phase:
                p_mem = lax.rem(a + s, n_mem)
                slot = (n_mem - s) % n_mem
                pltpu.make_async_remote_copy(
                    src_ref=out_box.at[p_mem * n_reg + p_row], dst_ref=in_box.at[slot, b],
                    send_sem=out_sem, recv_sem=in_sem.at[slot],
                    device_id=(p_mem, p_row, f), device_id_type=MESH,
                ).start()
            return carry

        lax.fori_loop(1 if phase == [0] else 0, n_reg, send_state, 0)

    obs = idx_ref.shape[2]
    for q in range(2):

        def spread_weights(g, carry):
            start = pl.multiple_of(g * 16, 16)
            cell = lax.broadcasted_iota(jnp.int32, (16, obs), 0) + g * 16
            total = jnp.zeros((16, obs), jnp.float32)
            for j in range(4):
                total += jnp.where(idx_ref[q, j : j + 1, :] == cell, wt_ref[q, j : j + 1, :], 0.0)
            high, rest = split(total)
            stencil[q, pl.ds(start, 16), :] = total
            stencil_hi[q, pl.ds(start, 16), :] = high
            stencil_lo[q, pl.ds(start, 16), :] = rest
            return carry

        lax.fori_loop(0, 3 * cells // 16, spread_weights, 0)

    def wait_bytes(ref, sem):
        pltpu.make_async_copy(ref, ref, sem).wait()

    wait_bytes(c_in.at[pl.ds(0, n_reg - 1)], c_in_sem)

    def halo_copies(s):
        there_west = lax.rem(s + a - ring_place(west)[0] + n_mem, n_mem)
        there_east = lax.rem(s + a - ring_place(east)[0] + n_mem, n_mem)
        go_west = pltpu.make_async_remote_copy(
            src_ref=to_west.at[s], dst_ref=from_east.at[there_west],
            send_sem=halo_out_sem.at[0, s], recv_sem=halo_in_sem.at[0, there_west],
            device_id=ring_place(west), device_id_type=MESH,
        )
        go_east = pltpu.make_async_remote_copy(
            src_ref=to_east.at[s], dst_ref=from_west.at[there_east],
            send_sem=halo_out_sem.at[1, s], recv_sem=halo_in_sem.at[1, there_east],
            device_id=ring_place(east), device_id_type=MESH,
        )
        return go_west, go_east

    def send_rim(s):
        wait_bytes(in_box.at[s, pl.ds(0, n_reg - 1 if s == 0 else n_reg)], in_sem.at[s])

        def quarter(i, carry):
            at = pl.ds(i * 8, 8)
            h, u, v = in_box[s, at, 0], in_box[s, at, 1], in_box[s, at, 2]
            c, u = across(c_in[at]), across(u)
            to_west[s, at] = jnp.where(low, jnp.where(left, h, u), up(jnp.where(left, v, c)))
            to_east[s, at] = jnp.where(low, up(jnp.where(left, c, v)), jnp.where(left, u, h))
            return carry

        lax.fori_loop(0, n_reg // 8, quarter, 0)
        for copy in halo_copies(s):
            copy.start()

    def broad(c, at):
        return jnp.where(
            left,
            jnp.broadcast_to(c[:, :, at : at + 1], c.shape),
            jnp.broadcast_to(c[:, :, at + MEMS : at + MEMS + 1], c.shape),
        )

    def forecast(s):
        wait_bytes(from_east.at[s], halo_in_sem.at[0, s])
        wait_bytes(from_west.at[s], halo_in_sem.at[1, s])

        def rim(i, carry):
            at, to = pl.ds(i * 8, 8), pl.ds(i * 8 + 1, 8)
            e, w = from_east[s, at], from_west[s, at]
            p, q = jnp.where(low, e, w), up(jnp.where(low, w, e))
            h, u, v = in_box[s, at, 0], in_box[s, at, 1], in_box[s, at, 2]
            window[0, to, 0:8] = h
            window[1, to, 0:8] = u
            window[2, to, 0:8] = v
            window[0, to, 8:16] = across(jnp.where(crossed, h, p))
            window[1, to, 8:16] = jnp.where(crossed, p, across(u))
            window[2, to, 8:16] = across(jnp.where(crossed, v, q))
            if s == 0:
                c = c_in[at]
                cour_u[to, 0:8] = broad(c, 0)
                cour_v[to, 0:8] = broad(c, 32)
                c = jnp.where(crossed, q, across(c))
                cour_u[to, 8:16] = broad(c, 0)
                cour_v[to, 8:16] = broad(c, 32)
            return carry

        lax.fori_loop(0, n_reg // 8, rim, 0)

        def heights(i, carry):
            at = pl.ds(i * 8 + 1, 8)
            flux_u = cour_u[at] * window[1, at]
            flux_v = cour_v[pl.ds(i * 8, 9)] * window[2, pl.ds(i * 8, 9)]
            gain = flux_u - pltpu.roll(flux_u, 1, axis=1) + flux_v[1:] - flux_v[:-1]
            window[0, at] = window[0, at] - gain
            return carry

        def currents(i, carry):
            at = pl.ds(i * 8 + 1, 8)
            h = window[0, pl.ds(i * 8 + 1, 9)]
            window[1, at] = window[1, at] - (pltpu.roll(h[:-1], 15, axis=1) - h[:-1])
            window[2, at] = window[2, at] - (h[1:] - h[:-1])
            return carry

        def one_step(i, carry):
            lax.fori_loop(0, n_reg // 8, heights, 0, unroll=True)
            lax.fori_loop(0, n_reg // 8, currents, 0, unroll=True)
            return carry

        lax.fori_loop(0, STEPS, one_step, 0)
        tile = slice(s // 2 * LANES, (s // 2 + 1) * LANES)
        keep = left if s % 2 else ~left

        def place_cells(i, carry):
            at = pl.ds(i * 8, 8)
            for var in range(3):
                x = window[var, pl.ds(i * 8 + 1, 8), 0:8]
                y = across(x)
                x, y = (y, x) if s % 2 else (x, y)
                state[var, at, 0:8, tile] = jnp.where(keep, state[var, at, 0:8, tile], x)
                state[var, at, 8:16, tile] = jnp.where(keep, state[var, at, 8:16, tile], y)
            return carry

        lax.fori_loop(0, n_reg // 8, place_cells, 0)

    blank = jnp.zeros((16, LANES), jnp.float32)
    window[0, n_reg + 1] = blank
    window[2, 0] = blank
    cour_v[0] = blank

    early = order[:-1] if n_mem > 2 else order
    for s in early:
        send_rim(s)
    forecast(order[0])
    for s in order[len(early) :]:
        send_rim(s)
    for s in order[1:]:
        forecast(s)

    row_i = lax.broadcasted_iota(jnp.int32, (members, members), 0)
    col_i = lax.broadcasted_iota(jnp.int32, (members, members), 1)
    eye = jnp.where(row_i == col_i, 1.0, 0.0).astype(jnp.float32)
    obs_i = lax.broadcasted_iota(jnp.int32, (1, obs), 1)

    for q in range(2):
        spreads, means = [], []
        obs_spread = jnp.zeros((members, obs), jnp.float32)
        mean_obs = jnp.zeros((1, obs), jnp.float32)
        for var in range(3):
            x = state[var, q * half_rows : (q + 1) * half_rows].reshape(cells, members)
            mean = jnp.sum(x, axis=1, keepdims=True) / members
            spread = split(x - mean)
            block = slice(var * cells, (var + 1) * cells)
            weights = (stencil_hi[q, block, :], stencil_lo[q, block, :])
            obs_spread += dot3(spread, weights, ((0,), (0,)))
            mean_obs += jnp.sum(stencil[q, block, :] * mean, axis=0, keepdims=True)
            spreads.append(spread)
            means.append(mean)
        active = jnp.where(obs_i < cnt_ref[q], 1.0, 0.0)
        weighted = obs_spread * (active / var_ref[q : q + 1, :])
        gram_sum = dot3(split(weighted), split(obs_spread), ((1,), (1,)))
        scaled = eye + gram_sum / (members - 1)
        fro = jnp.sqrt(all_sum(scaled * scaled))
        innovation = jnp.sum(weighted * (val_ref[q : q + 1, :] - mean_obs), axis=1, keepdims=True)
        iterate = scaled / fro
        factor = split(1.5 * eye - 0.5 * iterate)

        def sweep(i, carry):
            iterate, root = carry
            factor = split(1.5 * eye - 0.5 * dot3(root, iterate))
            return split(dot3(iterate, factor)), split(dot3(factor, root))

        iterate, root = lax.fori_loop(
            1, NEWTON - 1, sweep, (split(dot3(split(iterate), factor)), factor)
        )
        factor = split(1.5 * eye - 0.5 * dot3(root, iterate))
        transform = dot3(factor, root) / jnp.sqrt(fro)
        halfway = jnp.sum(transform * innovation, axis=0, keepdims=True)
        mean_weights = jnp.sum(transform * halfway, axis=1, keepdims=True) / (members - 1)
        both = split(jnp.concatenate(
            [transform + mean_weights, jnp.broadcast_to(mean_weights, (members, LANES))], axis=1
        ))
        for var in range(3):
            moved = dot3(spreads[var], both)
            ana[var, :, 0:members] = moved[:, 0:members] + means[var]
            ana[var, :, members:] = moved[:, members:]

        def unload(i, carry):
            lo = pl.multiple_of(i * COLS, 8)
            hi = pl.multiple_of(i * COLS + 8, 8)
            row = q * half_rows + i
            for t in range(lane_tiles):
                at = slice(t * LANES, (t + 1) * LANES)
                for var in range(3):
                    x, y = ana[var, pl.ds(lo, 8), at], ana[var, pl.ds(hi, 8), at]
                    back_out[2 * t, row, var] = jnp.where(left, x, across(y))
                    back_out[2 * t + 1, row, var] = jnp.where(left, across(x), y)
            packed = jnp.zeros((8, LANES), jnp.float32)
            for var in range(3):
                x = ana[var, pl.ds(lo, 8), members:]
                y = ana[var, pl.ds(hi, 8), members:]
                packed = jnp.where(lax.div(lax.rem(lane, MEMS), 16) == var, jnp.where(left, x, y), packed)
            inc_out[row] = packed
            return carry

        lax.fori_loop(0, half_rows, unload, 0, unroll=2)

        def send_inc(i, carry):
            p = q * half_rows + lax.rem(b + i, half_rows)

            @pl.when(p != b)
            def _():
                pltpu.make_async_remote_copy(
                    src_ref=inc_out.at[p], dst_ref=inc_in.at[b], send_sem=inc_out_sem,
                    recv_sem=inc_in_sem, device_id=(a, p, f), device_id_type=MESH,
                ).start()

            return carry

        lax.fori_loop(0, half_rows, send_inc, 0)
        for phase in phases:

            def send_back(i, carry):
                p_row = q * half_rows + lax.rem(b + i, half_rows)
                for s in phase:
                    slot = (n_mem - s) % n_mem
                    copy = pltpu.make_async_remote_copy(
                        src_ref=back_out.at[s, p_row], dst_ref=back_in.at[slot, b],
                        send_sem=back_out_sem, recv_sem=back_in_sem.at[slot],
                        device_id=(lax.rem(a + s, n_mem), p_row, f), device_id_type=MESH,
                    )
                    if s == 0:
                        pl.when(p_row != b)(copy.start)
                    else:
                        copy.start()
                return carry

            lax.fori_loop(0, half_rows, send_back, 0)

    inc_in[b] = inc_out[b]
    back_in[0, b] = back_out[0, b]
    wait_bytes(inc_in.at[pl.ds(0, n_reg - 1)], inc_in_sem)

    def straight(blocks):
        return jnp.stack([blocks, pltpu.roll(blocks, MEMS, axis=2)], axis=1).reshape(LANES, LANES).T

    fine_i = lax.broadcasted_iota(jnp.int32, (LANES, 2 * LANES), 1)
    coarse_i = lax.broadcasted_iota(jnp.int32, (LANES, 2 * LANES), 0)
    widen = jnp.where(lax.div(fine_i, 2) == coarse_i, 1.0, 0.0).astype(jnp.float32)
    for j in range(own_tiles):
        at = slice(2 * j * LANES, 2 * (j + 1) * LANES)
        wide = dot(straight(inc_in[8 * j : 8 * j + 8])[0:64], widen, precision=HIGHEST)
        for var in range(3):
            for e in range(2):
                fo_ref[var, e, 0:1, at] = fc_ref[var, e, 0:1, at] + wide[16 * var : 16 * var + 1]

    for s in order:
        wait_bytes(back_in.at[s, pl.ds(0, n_reg - 1 if s == 0 else n_reg)], back_in_sem.at[s])
        first = lax.rem(a + s, n_mem) * own_tiles

        def unpack(j, carry):
            for var, ref in enumerate((ah_ref, au_ref, av_ref)):
                start = pl.multiple_of(j * 8, 8)
                blocks = back_in[s, pl.ds(start, 8), var]
                ref[pl.ds(first + j, MEMS, stride=tiles), :] = straight(blocks)[0:MEMS]
            return carry

        lax.fori_loop(0, own_tiles, unpack, 0)

    wait_bytes(c_out.at[pl.ds(0, n_reg - 1)], c_out_sem)
    wait_bytes(out_box.at[pl.ds(0, peers - 1)], out_sem)
    wait_bytes(inc_out.at[pl.ds(0, n_reg - 1)], inc_out_sem)
    wait_bytes(out_box.at[pl.ds(0, peers - 1)], back_out_sem)
    for s in order:
        for copy in halo_copies(s):
            copy.wait_send()


def step(n_mem, n_reg, h, u, v, cu, cv, obs_index, obs_weight, obs_value, obs_var, obs_count, fine):
    peers = n_mem * n_reg
    members = n_mem * MEMS
    tiles = peers * COLS // LANES
    obs = obs_value.shape[1]
    cells = n_reg // 2 * COLS
    f32 = jnp.float32
    flat = (MEMS * tiles, LANES)
    vmem = pl.BlockSpec(memory_space=pltpu.VMEM)
    dma = pltpu.SemaphoreType.DMA
    outs = pl.pallas_call(
        functools.partial(kernel, (n_mem, n_reg)),
        out_shape=[jax.ShapeDtypeStruct(flat, f32)] * 3 + [jax.ShapeDtypeStruct(fine.shape, f32)],
        in_specs=[vmem] * 9 + [pl.BlockSpec(memory_space=pltpu.SMEM), vmem],
        out_specs=[vmem] * 4,
        scratch_shapes=[
            pltpu.VMEM((peers, 3, 8, LANES), f32),
            pltpu.VMEM((n_mem, n_reg, 3, 8, LANES), f32),
            pltpu.VMEM((n_reg, 8, LANES), f32),
            pltpu.VMEM((n_reg, 8, LANES), f32),
            pltpu.VMEM((n_mem, n_reg, 8, LANES), f32),
            pltpu.VMEM((n_mem, n_reg, 8, LANES), f32),
            pltpu.VMEM((n_mem, n_reg, 8, LANES), f32),
            pltpu.VMEM((n_mem, n_reg, 8, LANES), f32),
            pltpu.VMEM((3, n_reg + 2, 16, LANES), f32),
            pltpu.VMEM((n_reg + 2, 16, LANES), f32),
            pltpu.VMEM((n_reg + 2, 16, LANES), f32),
            pltpu.VMEM((3, n_reg, 16, members), f32),
            pltpu.VMEM((2, 3 * cells, obs), f32),
            pltpu.VMEM((2, 3 * cells, obs), jnp.bfloat16),
            pltpu.VMEM((2, 3 * cells, obs), jnp.bfloat16),
            pltpu.VMEM((3, cells, members + LANES), f32),
            pltpu.VMEM((n_mem, n_reg, 3, 8, LANES), f32),
            pltpu.VMEM((n_mem, n_reg, 3, 8, LANES), f32),
            pltpu.VMEM((n_reg, 8, LANES), f32),
            pltpu.VMEM((n_reg, 8, LANES), f32),
            dma, dma((n_mem,)), dma, dma, dma((2, n_mem)), dma((2, n_mem)),
            dma, dma((n_mem,)), dma, dma,
        ],
        compiler_params=pltpu.CompilerParams(
            collective_id=0, has_side_effects=True, vmem_limit_bytes=56 * 1024 * 1024
        ),
    )(
        h.reshape(flat), u.reshape(flat), v.reshape(flat),
        cu.reshape(tiles, LANES), cv.reshape(tiles, LANES),
        obs_index.transpose(0, 2, 1), obs_weight.transpose(0, 2, 1),
        obs_value, obs_var, obs_count, fine,
    )
    return tuple(x.reshape(h.shape) for x in outs[:3]) + (outs[3],)


def solution(mesh):
    fields = P("member", "region", "fine")
    regions = ("member", "region", "fine")
    fine = P(None, "region", "fine", "member")
    return jax.shard_map(
        functools.partial(step, mesh.shape["member"], mesh.shape["region"]),
        mesh=mesh,
        in_specs=(
            fields, fields, fields,
            P("region", "fine"), P("region", "fine"),
            P(regions, None, None), P(regions, None, None),
            P(regions, None), P(regions, None), P(regions),
            fine,
        ),
        out_specs=(fields, fields, fields, fine),
        check_vma=False,
    )
```

```python
import functools

import jax
import jax.numpy as jnp
from jax import lax
from jax.experimental import pallas as pl
from jax.experimental.pallas import tpu as pltpu
from jax.sharding import PartitionSpec as P

MESH = pl.DeviceIdType.MESH
STEPS = 4
NEWTON = 8
HIGHEST = lax.Precision.HIGHEST
LANES = 128
MEMS = 64
COLS = 16


ROWS_COLS = ((1,), (0,))


def dot(x, y, contract=ROWS_COLS, precision=None):
    return lax.dot_general(
        x, y, (contract, ((), ())), precision=precision, preferred_element_type=jnp.float32
    )


def split(x):
    high = x.astype(jnp.bfloat16)
    return high, (x - high.astype(jnp.float32)).astype(jnp.bfloat16)


def dot3(x, y, contract=ROWS_COLS):
    rows = 1 - contract[0][0]
    size = x[0].shape[rows]
    both = dot(jnp.concatenate(x, axis=rows), y[0], contract)
    return both[:size] + (both[size:] + dot(x[0], y[1], contract))


def all_sum(x):
    return jnp.sum(jnp.sum(x, axis=1, keepdims=True), axis=0, keepdims=True)


def kernel(
    dims,
    h_ref, u_ref, v_ref, cu_ref, cv_ref, idx_ref, wt_ref, val_ref, var_ref, cnt_ref, fc_ref,
    ah_ref, au_ref, av_ref, fo_ref,
    out_box, in_box, c_out, c_in, to_west, to_east, from_east, from_west,
    window, cour_u, cour_v, state, stencil, stencil_hi, stencil_lo, ana,
    back_out, back_in, inc_out, inc_in, h_in, u_in, v_in, c_edge, edges,
    out_sem, in_sem, c_out_sem, c_in_sem, halo_out_sem, halo_in_sem,
    back_out_sem, back_in_sem, inc_out_sem, inc_in_sem, load_sem, edge_sem,
):
    n_mem, n_reg = dims
    peers = n_mem * n_reg
    tiles = peers * COLS // LANES
    lane_tiles = n_mem * MEMS // LANES
    members = n_mem * MEMS
    half_rows = n_reg // 2
    cells = half_rows * COLS
    own_tiles = n_reg * COLS // LANES
    plane = n_reg // 2
    phases = [[0], [1, 3], [2]] if n_mem == 4 else [[s] for s in range(n_mem)]
    order = [s for phase in phases for s in phase]
    a = lax.axis_index("member")
    b = lax.axis_index("region")
    f = lax.axis_index("fine")
    me = a * n_reg + b

    def place(p):
        return (lax.div(p, n_reg), lax.rem(p, n_reg), f)

    loads = [
        pltpu.make_async_copy(ref, box, load_sem.at[i])
        for i, (ref, box) in enumerate(((h_ref, h_in), (u_ref, u_in), (v_ref, v_in)))
    ]
    for load in loads:
        load.start()

    barrier = pltpu.get_barrier_semaphore()

    def greet(i, carry):
        pl.semaphore_signal(
            barrier, inc=1, device_id=place(lax.rem(me + i, peers)), device_id_type=MESH
        )
        return carry

    def greet_other_half(i, carry):
        p_mem, p_row, _ = place(i)
        pl.semaphore_signal(barrier, inc=1, device_id=(p_mem, p_row, 1 - f), device_id_type=MESH)
        return carry

    @pl.when((me == 0) | (me == peers - 1))
    def _():
        lax.fori_loop(0, peers, greet_other_half, 0)

    lax.fori_loop(1, peers, greet, 0)
    for load in loads:
        load.wait()

    lane = lax.broadcasted_iota(jnp.int32, (8, LANES), 1)
    left = lane < MEMS
    low = lax.broadcasted_iota(jnp.int32, (8, LANES), 0) < 4
    crossed = (low & ~left) | (~low & left)

    def across(x):
        return pltpu.roll(x, MEMS, axis=x.ndim - 1)

    def up(x):
        return pltpu.roll(x, 4, axis=x.ndim - 2)

    def turned(block):
        pair = jnp.concatenate([block, pltpu.roll(block, LANES - 8, axis=1)], axis=0)
        return pair.T

    def pack(j, carry):
        for var, ref in enumerate((h_in, u_in, v_in)):
            t = turned(ref[pl.ds(j, MEMS, stride=tiles), :])
            for k in range(8):
                out_box[j * 8 + k, var] = t[COLS * k : COLS * k + 8]
        return carry

    lax.fori_loop(0, tiles, pack, 0)

    def courant(j):
        cu = jnp.broadcast_to(cu_ref[pl.ds(j, 1), :], (32, LANES))
        cv = jnp.broadcast_to(cv_ref[pl.ds(j, 1), :], (32, LANES))
        return turned(jnp.concatenate([cu, cv], axis=0))

    def west_going(h, u, v, c):
        c, u = across(c), across(u)
        return jnp.where(low, jnp.where(left, h, u), up(jnp.where(left, v, c)))

    def east_going(h, u, v, c):
        c, u = across(c), across(u)
        return jnp.where(low, up(jnp.where(left, c, v)), jnp.where(left, u, h))

    for j in range(own_tiles):
        t = courant(a * own_tiles + j)
        for k in range(8):
            c_out[j * 8 + k] = t[COLS * k : COLS * k + 8]

    c_edge[0] = courant(lax.rem(a + 1, n_mem) * own_tiles)[0:8]
    c_edge[1] = courant(lax.rem(a * own_tiles + tiles - 1, tiles))[7 * COLS : 7 * COLS + 8]
    for k in range(n_mem):
        for kind, (m, c, going) in enumerate((
            (k * n_reg + plane, c_out[plane], west_going),
            ((k + 1) % n_mem * n_reg, c_edge[0], west_going),
            (k * n_reg + plane - 1, c_out[plane - 1], east_going),
            ((k * n_reg + peers - 1) % peers, c_edge[1], east_going),
        )):
            edges[k, kind] = going(out_box[m, 0], out_box[m, 1], out_box[m, 2], c)

    pl.semaphore_wait(barrier, peers + 1)

    def send_courant(i, carry):
        p = lax.rem(b + i, n_reg)
        pltpu.make_async_remote_copy(
            src_ref=c_out.at[p], dst_ref=c_in.at[b], send_sem=c_out_sem, recv_sem=c_in_sem,
            device_id=(a, p, f), device_id_type=MESH,
        ).start()
        return carry

    lax.fori_loop(1, n_reg, send_courant, 0)
    c_in[b] = c_out[b]
    in_box[0, b] = out_box[me]

    for phase in phases:

        def send_state(i, carry):
            p_row = lax.rem(b + i, n_reg)
            for s in phase:
                p_mem = lax.rem(a + s, n_mem)
                slot = (n_mem - s) % n_mem
                pltpu.make_async_remote_copy(
                    src_ref=out_box.at[p_mem * n_reg + p_row], dst_ref=in_box.at[slot, b],
                    send_sem=out_sem, recv_sem=in_sem.at[slot],
                    device_id=(p_mem, p_row, f), device_id_type=MESH,
                ).start()
            return carry

        lax.fori_loop(1 if phase == [0] else 0, n_reg, send_state, 0)
        for s in phase:
            p_mem = lax.rem(a + s, n_mem)
            slot = (n_mem - s) % n_mem
            for kind, (p_row, box, other) in enumerate((
                (plane - 1, from_east, None),
                (n_reg - 1, from_east, n_mem - 1),
                (plane, from_west, None),
                (0, from_west, 0),
            )):
                here = f if other is None else jnp.where(p_mem == other, 1 - f, f)
                sem = halo_in_sem.at[kind // 2, slot]
                go = pltpu.make_async_remote_copy(
                    src_ref=edges.at[p_mem, kind], dst_ref=box.at[slot, b],
                    send_sem=edge_sem, recv_sem=sem,
                    device_id=(p_mem, p_row, here), device_id_type=MESH,
                )
                if s:
                    go.start()
                else:
                    own = (b == p_row) if other is None else (b == p_row) & (a != other)
                    stay = pltpu.make_async_copy(edges.at[p_mem, kind], box.at[slot, b], sem)
                    pl.when(own)(stay.start)
                    pl.when(jnp.logical_not(own))(go.start)

    obs = idx_ref.shape[2]
    for q in range(2):

        def spread_weights(g, carry):
            start = pl.multiple_of(g * 16, 16)
            cell = lax.broadcasted_iota(jnp.int32, (16, obs), 0) + g * 16
            total = jnp.zeros((16, obs), jnp.float32)
            for j in range(4):
                total += jnp.where(idx_ref[q, j : j + 1, :] == cell, wt_ref[q, j : j + 1, :], 0.0)
            high, rest = split(total)
            stencil[q, pl.ds(start, 16), :] = total
            stencil_hi[q, pl.ds(start, 16), :] = high
            stencil_lo[q, pl.ds(start, 16), :] = rest
            return carry

        lax.fori_loop(0, 3 * cells // 16, spread_weights, 0)

    def wait_bytes(ref, sem):
        pltpu.make_async_copy(ref, ref, sem).wait()

    wait_bytes(c_in.at[pl.ds(0, n_reg - 1)], c_in_sem)

    inside_west = lax.rem(b, plane) != 0
    inside_east = lax.rem(b, plane) != plane - 1

    def halo_copies(s):
        go_west = pltpu.make_async_remote_copy(
            src_ref=to_west.at[s], dst_ref=from_east.at[s],
            send_sem=halo_out_sem.at[0, s], recv_sem=halo_in_sem.at[0, s],
            device_id=(a, lax.rem(b + n_reg - 1, n_reg), f), device_id_type=MESH,
        )
        go_east = pltpu.make_async_remote_copy(
            src_ref=to_east.at[s], dst_ref=from_west.at[s],
            send_sem=halo_out_sem.at[1, s], recv_sem=halo_in_sem.at[1, s],
            device_id=(a, lax.rem(b + 1, n_reg), f), device_id_type=MESH,
        )
        return (inside_west, go_west), (inside_east, go_east)

    def send_rim(s):
        wait_bytes(in_box.at[s, pl.ds(0, n_reg - 1 if s == 0 else n_reg)], in_sem.at[s])

        def quarter(i, carry):
            at = pl.ds(i * 8, 8)
            h, u, v = in_box[s, at, 0], in_box[s, at, 1], in_box[s, at, 2]
            c = c_in[at]
            to_west[s, at] = west_going(h, u, v, c)
            to_east[s, at] = east_going(h, u, v, c)
            return carry

        lax.fori_loop(0, n_reg // 8, quarter, 0)
        for inside, copy in halo_copies(s):
            pl.when(inside)(copy.start)

    def broad(c, at):
        return jnp.where(
            left,
            jnp.broadcast_to(c[:, :, at : at + 1], c.shape),
            jnp.broadcast_to(c[:, :, at + MEMS : at + MEMS + 1], c.shape),
        )

    def forecast(s):
        wait_bytes(from_east.at[s], halo_in_sem.at[0, s])
        wait_bytes(from_west.at[s], halo_in_sem.at[1, s])

        def rim(i, carry):
            at, to = pl.ds(i * 8, 8), pl.ds(i * 8 + 1, 8)
            e, w = from_east[s, at], from_west[s, at]
            p, q = jnp.where(low, e, w), up(jnp.where(low, w, e))
            h, u, v = in_box[s, at, 0], in_box[s, at, 1], in_box[s, at, 2]
            window[0, to, 0:8] = h
            window[1, to, 0:8] = u
            window[2, to, 0:8] = v
            window[0, to, 8:16] = across(jnp.where(crossed, h, p))
            window[1, to, 8:16] = jnp.where(crossed, p, across(u))
            window[2, to, 8:16] = across(jnp.where(crossed, v, q))
            if s == 0:
                c = c_in[at]
                cour_u[to, 0:8] = broad(c, 0)
                cour_v[to, 0:8] = broad(c, 32)
                c = jnp.where(crossed, q, across(c))
                cour_u[to, 8:16] = broad(c, 0)
                cour_v[to, 8:16] = broad(c, 32)
            return carry

        lax.fori_loop(0, n_reg // 8, rim, 0)

        def heights(i, carry):
            at = pl.ds(i * 8 + 1, 8)
            flux_u = cour_u[at] * window[1, at]
            flux_v = cour_v[pl.ds(i * 8, 9)] * window[2, pl.ds(i * 8, 9)]
            gain = flux_u - pltpu.roll(flux_u, 1, axis=1) + flux_v[1:] - flux_v[:-1]
            window[0, at] = window[0, at] - gain
            return carry

        def currents(i, carry):
            at = pl.ds(i * 8 + 1, 8)
            h = window[0, pl.ds(i * 8 + 1, 9)]
            window[1, at] = window[1, at] - (pltpu.roll(h[:-1], 15, axis=1) - h[:-1])
            window[2, at] = window[2, at] - (h[1:] - h[:-1])
            return carry

        def one_step(i, carry):
            lax.fori_loop(0, n_reg // 8, heights, 0, unroll=True)
            lax.fori_loop(0, n_reg // 8, currents, 0, unroll=True)
            return carry

        lax.fori_loop(0, STEPS, one_step, 0)
        tile = slice(s // 2 * LANES, (s // 2 + 1) * LANES)
        keep = left if s % 2 else ~left

        def place_cells(i, carry):
            at = pl.ds(i * 8, 8)
            for var in range(3):
                x = window[var, pl.ds(i * 8 + 1, 8), 0:8]
                y = across(x)
                x, y = (y, x) if s % 2 else (x, y)
                state[var, at, 0:8, tile] = jnp.where(keep, state[var, at, 0:8, tile], x)
                state[var, at, 8:16, tile] = jnp.where(keep, state[var, at, 8:16, tile], y)
            return carry

        lax.fori_loop(0, n_reg // 8, place_cells, 0)

    blank = jnp.zeros((16, LANES), jnp.float32)
    window[0, n_reg + 1] = blank
    window[2, 0] = blank
    cour_v[0] = blank

    for s in order[:-1]:
        send_rim(s)
    forecast(order[0])
    send_rim(order[-1])
    for s in order[1:]:
        forecast(s)

    row_i = lax.broadcasted_iota(jnp.int32, (members, members), 0)
    col_i = lax.broadcasted_iota(jnp.int32, (members, members), 1)
    eye = jnp.where(row_i == col_i, 1.0, 0.0).astype(jnp.float32)
    obs_i = lax.broadcasted_iota(jnp.int32, (1, obs), 1)

    for q in range(2):
        spreads, means = [], []
        obs_spread = jnp.zeros((members, obs), jnp.float32)
        mean_obs = jnp.zeros((1, obs), jnp.float32)
        for var in range(3):
            x = state[var, q * half_rows : (q + 1) * half_rows].reshape(cells, members)
            mean = jnp.sum(x, axis=1, keepdims=True) / members
            spread = split(x - mean)
            block = slice(var * cells, (var + 1) * cells)
            weights = (stencil_hi[q, block, :], stencil_lo[q, block, :])
            obs_spread += dot3(spread, weights, ((0,), (0,)))
            mean_obs += jnp.sum(stencil[q, block, :] * mean, axis=0, keepdims=True)
            spreads.append(spread)
            means.append(mean)
        active = jnp.where(obs_i < cnt_ref[q], 1.0, 0.0)
        weighted = obs_spread * (active / var_ref[q : q + 1, :])
        gram_sum = dot3(split(weighted), split(obs_spread), ((1,), (1,)))
        scaled = eye + gram_sum / (members - 1)
        fro = jnp.sqrt(all_sum(scaled * scaled))
        innovation = jnp.sum(weighted * (val_ref[q : q + 1, :] - mean_obs), axis=1, keepdims=True)
        iterate = scaled / fro
        factor = split(1.5 * eye - 0.5 * iterate)

        def sweep(i, carry):
            iterate, root = carry
            factor = split(1.5 * eye - 0.5 * dot3(root, iterate))
            return split(dot3(iterate, factor)), split(dot3(factor, root))

        iterate, root = lax.fori_loop(
            1, NEWTON - 1, sweep, (split(dot3(split(iterate), factor)), factor), unroll=2
        )
        factor = split(1.5 * eye - 0.5 * dot3(root, iterate))
        transform = dot3(factor, root) / jnp.sqrt(fro)
        halfway = jnp.sum(transform * innovation, axis=0, keepdims=True)
        mean_weights = jnp.sum(transform * halfway, axis=1, keepdims=True) / (members - 1)
        both = split(jnp.concatenate(
            [transform + mean_weights, jnp.broadcast_to(mean_weights, (members, LANES))], axis=1
        ))
        for var in range(3):
            moved = dot3(spreads[var], both)
            ana[var, :, 0:members] = moved[:, 0:members] + means[var]
            ana[var, :, members:] = moved[:, members:]

        def unload(i, carry):
            i = lax.rem(b + i, half_rows)
            lo = pl.multiple_of(i * COLS, 8)
            hi = pl.multiple_of(i * COLS + 8, 8)
            row = q * half_rows + i
            for t in range(lane_tiles):
                at = slice(t * LANES, (t + 1) * LANES)
                for var in range(3):
                    x, y = ana[var, pl.ds(lo, 8), at], ana[var, pl.ds(hi, 8), at]
                    back_out[2 * t, row, var] = jnp.where(left, x, across(y))
                    back_out[2 * t + 1, row, var] = jnp.where(left, across(x), y)
            packed = jnp.zeros((8, LANES), jnp.float32)
            for var in range(3):
                x = ana[var, pl.ds(lo, 8), members:]
                y = ana[var, pl.ds(hi, 8), members:]
                packed = jnp.where(lax.div(lax.rem(lane, MEMS), 16) == var, jnp.where(left, x, y), packed)
            inc_out[row] = packed
            if q == 0:
                send_inc(row)
                for s in order:
                    send_back(s, row)
            return carry

        def send_inc(row):
            go = pltpu.make_async_remote_copy(
                src_ref=inc_out.at[row], dst_ref=inc_in.at[b], send_sem=inc_out_sem,
                recv_sem=inc_in_sem, device_id=(a, row, f), device_id_type=MESH,
            )
            pl.when(row != b)(go.start)

        def send_back(s, row):
            slot = (n_mem - s) % n_mem
            go = pltpu.make_async_remote_copy(
                src_ref=back_out.at[s, row], dst_ref=back_in.at[slot, b],
                send_sem=back_out_sem, recv_sem=back_in_sem.at[slot],
                device_id=(lax.rem(a + s, n_mem), row, f), device_id_type=MESH,
            )
            if s:
                go.start()
            else:
                pl.when(row != b)(go.start)

        lax.fori_loop(0, half_rows, unload, 0)
        if q:
            for phase in phases:

                def send_phase(i, carry):
                    row = q * half_rows + lax.rem(b + i, half_rows)
                    if phase == phases[0]:
                        send_inc(row)
                    for s in phase:
                        send_back(s, row)
                    return carry

                lax.fori_loop(0, half_rows, send_phase, 0)

    inc_in[b] = inc_out[b]
    back_in[0, b] = back_out[0, b]
    wait_bytes(inc_in.at[pl.ds(0, n_reg - 1)], inc_in_sem)

    def straight(blocks):
        return jnp.stack([blocks, pltpu.roll(blocks, MEMS, axis=2)], axis=1).reshape(LANES, LANES).T

    fine_i = lax.broadcasted_iota(jnp.int32, (LANES, 2 * LANES), 1)
    coarse_i = lax.broadcasted_iota(jnp.int32, (LANES, 2 * LANES), 0)
    widen = jnp.where(lax.div(fine_i, 2) == coarse_i, 1.0, 0.0).astype(jnp.float32)
    for j in range(own_tiles):
        at = slice(2 * j * LANES, 2 * (j + 1) * LANES)
        wide = dot(straight(inc_in[8 * j : 8 * j + 8])[0:64], widen, precision=HIGHEST)
        for var in range(3):
            for e in range(2):
                fo_ref[var, e, 0:1, at] = fc_ref[var, e, 0:1, at] + wide[16 * var : 16 * var + 1]

    for s in order:
        wait_bytes(back_in.at[s, pl.ds(0, n_reg - 1 if s == 0 else n_reg)], back_in_sem.at[s])
        first = lax.rem(a + s, n_mem) * own_tiles

        def unpack(j, carry):
            for var, ref in enumerate((ah_ref, au_ref, av_ref)):
                start = pl.multiple_of(j * 8, 8)
                blocks = back_in[s, pl.ds(start, 8), var]
                ref[pl.ds(first + j, MEMS, stride=tiles), :] = straight(blocks)[0:MEMS]
            return carry

        lax.fori_loop(0, own_tiles, unpack, 0)

    wait_bytes(c_out.at[pl.ds(0, n_reg - 1)], c_out_sem)
    wait_bytes(out_box.at[pl.ds(0, peers - 1)], out_sem)
    wait_bytes(inc_out.at[pl.ds(0, n_reg - 1)], inc_out_sem)
    wait_bytes(out_box.at[pl.ds(0, peers - 1)], back_out_sem)
    for s in order:
        for inside, copy in halo_copies(s):
            pl.when(inside)(copy.wait_send)

    own_edge = (b == plane - 1) | (b == plane)
    own_edge |= ((b == n_reg - 1) & (a != n_mem - 1)) | ((b == 0) & (a != 0))

    @pl.when(own_edge)
    def _():
        wait_bytes(c_out.at[pl.ds(0, 4 * n_mem - 1)], edge_sem)

    @pl.when(jnp.logical_not(own_edge))
    def _():
        wait_bytes(c_out.at[pl.ds(0, 4 * n_mem)], edge_sem)


def step(n_mem, n_reg, h, u, v, cu, cv, obs_index, obs_weight, obs_value, obs_var, obs_count, fine):
    peers = n_mem * n_reg
    members = n_mem * MEMS
    tiles = peers * COLS // LANES
    obs = obs_value.shape[1]
    cells = n_reg // 2 * COLS
    f32 = jnp.float32
    flat = (MEMS * tiles, LANES)
    vmem = pl.BlockSpec(memory_space=pltpu.VMEM)
    dma = pltpu.SemaphoreType.DMA
    outs = pl.pallas_call(
        functools.partial(kernel, (n_mem, n_reg)),
        out_shape=[jax.ShapeDtypeStruct(flat, f32)] * 3 + [jax.ShapeDtypeStruct(fine.shape, f32)],
        in_specs=[pl.BlockSpec(memory_space=pl.ANY)] * 3 + [vmem] * 6 + [pl.BlockSpec(memory_space=pltpu.SMEM), vmem],
        out_specs=[vmem] * 4,
        scratch_shapes=[
            pltpu.VMEM((peers, 3, 8, LANES), f32),
            pltpu.VMEM((n_mem, n_reg, 3, 8, LANES), f32),
            pltpu.VMEM((n_reg, 8, LANES), f32),
            pltpu.VMEM((n_reg, 8, LANES), f32),
            pltpu.VMEM((n_mem, n_reg, 8, LANES), f32),
            pltpu.VMEM((n_mem, n_reg, 8, LANES), f32),
            pltpu.VMEM((n_mem, n_reg, 8, LANES), f32),
            pltpu.VMEM((n_mem, n_reg, 8, LANES), f32),
            pltpu.VMEM((3, n_reg + 2, 16, LANES), f32),
            pltpu.VMEM((n_reg + 2, 16, LANES), f32),
            pltpu.VMEM((n_reg + 2, 16, LANES), f32),
            pltpu.VMEM((3, n_reg, 16, members), f32),
            pltpu.VMEM((2, 3 * cells, obs), f32),
            pltpu.VMEM((2, 3 * cells, obs), jnp.bfloat16),
            pltpu.VMEM((2, 3 * cells, obs), jnp.bfloat16),
            pltpu.VMEM((3, cells, members + LANES), f32),
            pltpu.VMEM((n_mem, n_reg, 3, 8, LANES), f32),
            pltpu.VMEM((n_mem, n_reg, 3, 8, LANES), f32),
            pltpu.VMEM((n_reg, 8, LANES), f32),
            pltpu.VMEM((n_reg, 8, LANES), f32),
            pltpu.VMEM(flat, f32), pltpu.VMEM(flat, f32), pltpu.VMEM(flat, f32),
            pltpu.VMEM((2, 8, LANES), f32),
            pltpu.VMEM((n_mem, 4, 8, LANES), f32),
            dma, dma((n_mem,)), dma, dma, dma((2, n_mem)), dma((2, n_mem)),
            dma, dma((n_mem,)), dma, dma, dma((3,)), dma,
        ],
        compiler_params=pltpu.CompilerParams(
            collective_id=0, has_side_effects=True, vmem_limit_bytes=56 * 1024 * 1024
        ),
    )(
        h.reshape(flat), u.reshape(flat), v.reshape(flat),
        cu.reshape(tiles, LANES), cv.reshape(tiles, LANES),
        obs_index.transpose(0, 2, 1), obs_weight.transpose(0, 2, 1),
        obs_value, obs_var, obs_count, fine,
    )
    return tuple(x.reshape(h.shape) for x in outs[:3]) + (outs[3],)


def solution(mesh):
    fields = P("member", "region", "fine")
    regions = ("member", "region", "fine")
    fine = P(None, "region", "fine", "member")
    return jax.shard_map(
        functools.partial(step, mesh.shape["member"], mesh.shape["region"]),
        mesh=mesh,
        in_specs=(
            fields, fields, fields,
            P("region", "fine"), P("region", "fine"),
            P(regions, None, None), P(regions, None, None),
            P(regions, None), P(regions, None), P(regions),
            fine,
        ),
        out_specs=(fields, fields, fields, fine),
        check_vma=False,
    )
```

```python
import functools

import jax
import jax.numpy as jnp
from jax import lax
from jax.experimental import pallas as pl
from jax.experimental.pallas import tpu as pltpu
from jax.sharding import PartitionSpec as P

MESH = pl.DeviceIdType.MESH
STEPS = 4
NEWTON = 8
HIGHEST = lax.Precision.HIGHEST
LANES = 128
MEMS = 64
COLS = 16


ROWS_COLS = ((1,), (0,))


def dot(x, y, contract=ROWS_COLS, precision=None):
    return lax.dot_general(
        x, y, (contract, ((), ())), precision=precision, preferred_element_type=jnp.float32
    )


def split(x):
    high = x.astype(jnp.bfloat16)
    return high, (x - high.astype(jnp.float32)).astype(jnp.bfloat16)


def dot3(x, y, contract=ROWS_COLS):
    rows = 1 - contract[0][0]
    size = x[0].shape[rows]
    both = dot(jnp.concatenate(x, axis=rows), y[0], contract)
    return both[:size] + (both[size:] + dot(x[0], y[1], contract))


def all_sum(x):
    return jnp.sum(jnp.sum(x, axis=1, keepdims=True), axis=0, keepdims=True)


def kernel(
    dims,
    h_ref, u_ref, v_ref, cu_ref, cv_ref, idx_ref, wt_ref, val_ref, var_ref, cnt_ref, fc_ref,
    ana_ref, fo_ref,
    out_box, in_box, c_out, c_in, to_west, to_east, from_east, from_west,
    window, cour_u, cour_v, state, stencil, stencil_hi, stencil_lo, ana,
    back_out, back_in, inc_out, inc_in, h_in, u_in, v_in, c_edge, edges,
    out_sem, in_sem, c_out_sem, c_in_sem, halo_out_sem, halo_in_sem,
    back_out_sem, back_in_sem, inc_out_sem, inc_in_sem, load_sem, edge_sem,
):
    n_mem, n_reg = dims
    peers = n_mem * n_reg
    tiles = peers * COLS // LANES
    lane_tiles = n_mem * MEMS // LANES
    members = n_mem * MEMS
    half_rows = n_reg // 2
    cells = half_rows * COLS
    own_tiles = n_reg * COLS // LANES
    plane = n_reg // 2
    phases = [[0], [1, 3], [2]] if n_mem == 4 else [[s] for s in range(n_mem)]
    order = [s for phase in phases for s in phase]
    a = lax.axis_index("member")
    b = lax.axis_index("region")
    f = lax.axis_index("fine")
    me = a * n_reg + b

    def place(p):
        return (lax.div(p, n_reg), lax.rem(p, n_reg), f)

    loads = [
        pltpu.make_async_copy(ref, box, load_sem.at[i])
        for i, (ref, box) in enumerate(((h_ref, h_in), (u_ref, u_in), (v_ref, v_in)))
    ]
    for load in loads:
        load.start()

    barrier = pltpu.get_barrier_semaphore()

    def greet(i, carry):
        pl.semaphore_signal(
            barrier, inc=1, device_id=place(lax.rem(me + i, peers)), device_id_type=MESH
        )
        return carry

    def greet_other_half(i, carry):
        p_mem, p_row, _ = place(i)
        pl.semaphore_signal(barrier, inc=1, device_id=(p_mem, p_row, 1 - f), device_id_type=MESH)
        return carry

    @pl.when((me == 0) | (me == peers - 1))
    def _():
        lax.fori_loop(0, peers, greet_other_half, 0)

    lax.fori_loop(1, peers, greet, 0)
    for load in loads:
        load.wait()

    lane = lax.broadcasted_iota(jnp.int32, (8, LANES), 1)
    left = lane < MEMS
    low = lax.broadcasted_iota(jnp.int32, (8, LANES), 0) < 4
    crossed = (low & ~left) | (~low & left)

    def across(x):
        return pltpu.roll(x, MEMS, axis=x.ndim - 1)

    def up(x):
        return pltpu.roll(x, 4, axis=x.ndim - 2)

    def turned(block):
        pair = jnp.concatenate([block, pltpu.roll(block, LANES - 8, axis=1)], axis=0)
        return pair.T

    def pack(j, carry):
        for var, ref in enumerate((h_in, u_in, v_in)):
            t = turned(ref[pl.ds(j, MEMS, stride=tiles), :])
            for k in range(8):
                out_box[j * 8 + k, var] = t[COLS * k : COLS * k + 8]
        return carry

    lax.fori_loop(0, tiles, pack, 0)

    def courant(j):
        cu = jnp.broadcast_to(cu_ref[pl.ds(j, 1), :], (32, LANES))
        cv = jnp.broadcast_to(cv_ref[pl.ds(j, 1), :], (32, LANES))
        return turned(jnp.concatenate([cu, cv], axis=0))

    def west_going(h, u, v, c):
        c, u = across(c), across(u)
        return jnp.where(low, jnp.where(left, h, u), up(jnp.where(left, v, c)))

    def east_going(h, u, v, c):
        c, u = across(c), across(u)
        return jnp.where(low, up(jnp.where(left, c, v)), jnp.where(left, u, h))

    for j in range(own_tiles):
        t = courant(a * own_tiles + j)
        for k in range(8):
            c_out[j * 8 + k] = t[COLS * k : COLS * k + 8]

    c_edge[0] = courant(lax.rem(a + 1, n_mem) * own_tiles)[0:8]
    c_edge[1] = courant(lax.rem(a * own_tiles + tiles - 1, tiles))[7 * COLS : 7 * COLS + 8]
    for k in range(n_mem):
        for kind, (m, c, going) in enumerate((
            (k * n_reg + plane, c_out[plane], west_going),
            ((k + 1) % n_mem * n_reg, c_edge[0], west_going),
            (k * n_reg + plane - 1, c_out[plane - 1], east_going),
            ((k * n_reg + peers - 1) % peers, c_edge[1], east_going),
        )):
            edges[k, kind] = going(out_box[m, 0], out_box[m, 1], out_box[m, 2], c)

    pl.semaphore_wait(barrier, peers + 1)

    def send_courant(i, carry):
        p = lax.rem(b + i, n_reg)
        pltpu.make_async_remote_copy(
            src_ref=c_out.at[p], dst_ref=c_in.at[b], send_sem=c_out_sem, recv_sem=c_in_sem,
            device_id=(a, p, f), device_id_type=MESH,
        ).start()
        return carry

    lax.fori_loop(1, n_reg, send_courant, 0)
    c_in[b] = c_out[b]
    in_box[0, b] = out_box[me]

    for phase in phases:

        def send_state(i, carry):
            p_row = lax.rem(b + i, n_reg)
            for s in phase:
                p_mem = lax.rem(a + s, n_mem)
                slot = (n_mem - s) % n_mem
                pltpu.make_async_remote_copy(
                    src_ref=out_box.at[p_mem * n_reg + p_row], dst_ref=in_box.at[slot, b],
                    send_sem=out_sem, recv_sem=in_sem.at[slot],
                    device_id=(p_mem, p_row, f), device_id_type=MESH,
                ).start()
            return carry

        lax.fori_loop(1 if phase == [0] else 0, n_reg, send_state, 0)
        for s in phase:
            p_mem = lax.rem(a + s, n_mem)
            slot = (n_mem - s) % n_mem
            for kind, (p_row, box, other) in enumerate((
                (plane - 1, from_east, None),
                (n_reg - 1, from_east, n_mem - 1),
                (plane, from_west, None),
                (0, from_west, 0),
            )):
                here = f if other is None else jnp.where(p_mem == other, 1 - f, f)
                sem = halo_in_sem.at[kind // 2, slot]
                go = pltpu.make_async_remote_copy(
                    src_ref=edges.at[p_mem, kind], dst_ref=box.at[slot, b],
                    send_sem=edge_sem, recv_sem=sem,
                    device_id=(p_mem, p_row, here), device_id_type=MESH,
                )
                if s:
                    go.start()
                else:
                    own = (b == p_row) if other is None else (b == p_row) & (a != other)
                    stay = pltpu.make_async_copy(edges.at[p_mem, kind], box.at[slot, b], sem)
                    pl.when(own)(stay.start)
                    pl.when(jnp.logical_not(own))(go.start)

    obs = idx_ref.shape[2]
    for q in range(2):

        def spread_weights(g, carry):
            start = pl.multiple_of(g * 16, 16)
            cell = lax.broadcasted_iota(jnp.int32, (16, obs), 0) + g * 16
            total = jnp.zeros((16, obs), jnp.float32)
            for j in range(4):
                total += jnp.where(idx_ref[q, j : j + 1, :] == cell, wt_ref[q, j : j + 1, :], 0.0)
            high, rest = split(total)
            stencil[q, pl.ds(start, 16), :] = total
            stencil_hi[q, pl.ds(start, 16), :] = high
            stencil_lo[q, pl.ds(start, 16), :] = rest
            return carry

        lax.fori_loop(0, 3 * cells // 16, spread_weights, 0)

    def wait_bytes(ref, sem):
        pltpu.make_async_copy(ref, ref, sem).wait()

    wait_bytes(c_in.at[pl.ds(0, n_reg - 1)], c_in_sem)

    inside_west = lax.rem(b, plane) != 0
    inside_east = lax.rem(b, plane) != plane - 1

    def halo_copies(s):
        go_west = pltpu.make_async_remote_copy(
            src_ref=to_west.at[s], dst_ref=from_east.at[s],
            send_sem=halo_out_sem.at[0, s], recv_sem=halo_in_sem.at[0, s],
            device_id=(a, lax.rem(b + n_reg - 1, n_reg), f), device_id_type=MESH,
        )
        go_east = pltpu.make_async_remote_copy(
            src_ref=to_east.at[s], dst_ref=from_west.at[s],
            send_sem=halo_out_sem.at[1, s], recv_sem=halo_in_sem.at[1, s],
            device_id=(a, lax.rem(b + 1, n_reg), f), device_id_type=MESH,
        )
        return (inside_west, go_west), (inside_east, go_east)

    def send_rim(s):
        wait_bytes(in_box.at[s, pl.ds(0, n_reg - 1 if s == 0 else n_reg)], in_sem.at[s])

        def quarter(i, carry):
            at = pl.ds(i * 8, 8)
            h, u, v = in_box[s, at, 0], in_box[s, at, 1], in_box[s, at, 2]
            c = c_in[at]
            to_west[s, at] = west_going(h, u, v, c)
            to_east[s, at] = east_going(h, u, v, c)
            return carry

        lax.fori_loop(0, n_reg // 8, quarter, 0)
        for inside, copy in halo_copies(s):
            pl.when(inside)(copy.start)

    def broad(c, at):
        return jnp.where(
            left,
            jnp.broadcast_to(c[:, :, at : at + 1], c.shape),
            jnp.broadcast_to(c[:, :, at + MEMS : at + MEMS + 1], c.shape),
        )

    def forecast(s):
        wait_bytes(from_east.at[s], halo_in_sem.at[0, s])
        wait_bytes(from_west.at[s], halo_in_sem.at[1, s])

        def rim(i, carry):
            at, to = pl.ds(i * 8, 8), pl.ds(i * 8 + 1, 8)
            e, w = from_east[s, at], from_west[s, at]
            p, q = jnp.where(low, e, w), up(jnp.where(low, w, e))
            h, u, v = in_box[s, at, 0], in_box[s, at, 1], in_box[s, at, 2]
            window[0, to, 0:8] = h
            window[1, to, 0:8] = u
            window[2, to, 0:8] = v
            window[0, to, 8:16] = across(jnp.where(crossed, h, p))
            window[1, to, 8:16] = jnp.where(crossed, p, across(u))
            window[2, to, 8:16] = across(jnp.where(crossed, v, q))
            if s == 0:
                c = c_in[at]
                cour_u[to, 0:8] = broad(c, 0)
                cour_v[to, 0:8] = broad(c, 32)
                c = jnp.where(crossed, q, across(c))
                cour_u[to, 8:16] = broad(c, 0)
                cour_v[to, 8:16] = broad(c, 32)
            return carry

        lax.fori_loop(0, n_reg // 8, rim, 0)

        def heights(i, carry):
            at = pl.ds(i * 8 + 1, 8)
            flux_u = cour_u[at] * window[1, at]
            flux_v = cour_v[pl.ds(i * 8, 9)] * window[2, pl.ds(i * 8, 9)]
            gain = flux_u - pltpu.roll(flux_u, 1, axis=1) + flux_v[1:] - flux_v[:-1]
            window[0, at] = window[0, at] - gain
            return carry

        def currents(i, carry):
            at = pl.ds(i * 8 + 1, 8)
            h = window[0, pl.ds(i * 8 + 1, 9)]
            window[1, at] = window[1, at] - (pltpu.roll(h[:-1], 15, axis=1) - h[:-1])
            window[2, at] = window[2, at] - (h[1:] - h[:-1])
            return carry

        def one_step(i, carry):
            lax.fori_loop(0, n_reg // 8, heights, 0, unroll=True)
            lax.fori_loop(0, n_reg // 8, currents, 0, unroll=True)
            return carry

        lax.fori_loop(0, STEPS, one_step, 0)
        tile = slice(s // 2 * LANES, (s // 2 + 1) * LANES)
        keep = left if s % 2 else ~left

        def place_cells(i, carry):
            at = pl.ds(i * 8, 8)
            for var in range(3):
                x = window[var, pl.ds(i * 8 + 1, 8), 0:8]
                y = across(x)
                x, y = (y, x) if s % 2 else (x, y)
                state[var, at, 0:8, tile] = jnp.where(keep, state[var, at, 0:8, tile], x)
                state[var, at, 8:16, tile] = jnp.where(keep, state[var, at, 8:16, tile], y)
            return carry

        lax.fori_loop(0, n_reg // 8, place_cells, 0)

    blank = jnp.zeros((16, LANES), jnp.float32)
    window[0, n_reg + 1] = blank
    window[2, 0] = blank
    cour_v[0] = blank

    for s in order[:-1]:
        send_rim(s)
    forecast(order[0])
    send_rim(order[-1])
    for s in order[1:]:
        forecast(s)

    row_i = lax.broadcasted_iota(jnp.int32, (members, members), 0)
    col_i = lax.broadcasted_iota(jnp.int32, (members, members), 1)
    eye = jnp.where(row_i == col_i, 1.0, 0.0).astype(jnp.float32)
    obs_i = lax.broadcasted_iota(jnp.int32, (1, obs), 1)

    for q in range(2):
        spreads, means = [], []
        obs_spread = jnp.zeros((members, obs), jnp.float32)
        mean_obs = jnp.zeros((1, obs), jnp.float32)
        for var in range(3):
            x = state[var, q * half_rows : (q + 1) * half_rows].reshape(cells, members)
            mean = jnp.sum(x, axis=1, keepdims=True) / members
            spread = split(x - mean)
            block = slice(var * cells, (var + 1) * cells)
            weights = (stencil_hi[q, block, :], stencil_lo[q, block, :])
            obs_spread += dot3(spread, weights, ((0,), (0,)))
            mean_obs += jnp.sum(stencil[q, block, :] * mean, axis=0, keepdims=True)
            spreads.append(spread)
            means.append(mean)
        active = jnp.where(obs_i < cnt_ref[q], 1.0, 0.0)
        weighted = obs_spread * (active / var_ref[q : q + 1, :])
        gram_sum = dot3(split(weighted), split(obs_spread), ((1,), (1,)))
        scaled = eye + gram_sum / (members - 1)
        fro = jnp.sqrt(all_sum(scaled * scaled))
        innovation = jnp.sum(weighted * (val_ref[q : q + 1, :] - mean_obs), axis=1, keepdims=True)
        iterate = scaled / fro
        factor = split(1.5 * eye - 0.5 * iterate)

        def sweep(i, carry):
            iterate, root = carry
            factor = split(1.5 * eye - 0.5 * dot3(root, iterate))
            return split(dot3(iterate, factor)), split(dot3(factor, root))

        iterate, root = lax.fori_loop(
            1, NEWTON - 1, sweep, (split(dot3(split(iterate), factor)), factor), unroll=2
        )
        factor = split(1.5 * eye - 0.5 * dot3(root, iterate))
        transform = dot3(factor, root) / jnp.sqrt(fro)
        halfway = jnp.sum(transform * innovation, axis=0, keepdims=True)
        mean_weights = jnp.sum(transform * halfway, axis=1, keepdims=True) / (members - 1)
        both = split(jnp.concatenate(
            [transform + mean_weights, jnp.broadcast_to(mean_weights, (members, LANES))], axis=1
        ))
        for var in range(3):
            moved = dot3(spreads[var], both)
            ana[var, :, 0:members] = moved[:, 0:members] + means[var]
            ana[var, :, members:] = moved[:, members:]

        def unload(i, carry):
            i = lax.rem(b + i, half_rows)
            lo = pl.multiple_of(i * COLS, 8)
            hi = pl.multiple_of(i * COLS + 8, 8)
            row = q * half_rows + i
            for t in range(lane_tiles):
                at = slice(t * LANES, (t + 1) * LANES)
                for var in range(3):
                    x, y = ana[var, pl.ds(lo, 8), at], ana[var, pl.ds(hi, 8), at]
                    back_out[2 * t, row, var] = jnp.where(left, x, across(y))
                    back_out[2 * t + 1, row, var] = jnp.where(left, across(x), y)
            packed = jnp.zeros((8, LANES), jnp.float32)
            for var in range(3):
                x = ana[var, pl.ds(lo, 8), members:]
                y = ana[var, pl.ds(hi, 8), members:]
                packed = jnp.where(lax.div(lax.rem(lane, MEMS), 16) == var, jnp.where(left, x, y), packed)
            inc_out[row] = packed
            if q == 0:
                send_inc(row)
                for s in order:
                    send_back(s, row)
            return carry

        def send_inc(row):
            go = pltpu.make_async_remote_copy(
                src_ref=inc_out.at[row], dst_ref=inc_in.at[b], send_sem=inc_out_sem,
                recv_sem=inc_in_sem, device_id=(a, row, f), device_id_type=MESH,
            )
            pl.when(row != b)(go.start)

        def send_back(s, row):
            slot = (n_mem - s) % n_mem
            go = pltpu.make_async_remote_copy(
                src_ref=back_out.at[s, row], dst_ref=back_in.at[slot, b],
                send_sem=back_out_sem, recv_sem=back_in_sem.at[slot],
                device_id=(lax.rem(a + s, n_mem), row, f), device_id_type=MESH,
            )
            if s:
                go.start()
            else:
                pl.when(row != b)(go.start)

        lax.fori_loop(0, half_rows, unload, 0)
        if q:
            for phase in phases:

                def send_phase(i, carry):
                    row = q * half_rows + lax.rem(b + i, half_rows)
                    if phase == phases[0]:
                        send_inc(row)
                    for s in phase:
                        send_back(s, row)
                    return carry

                lax.fori_loop(0, half_rows, send_phase, 0)

    inc_in[b] = inc_out[b]
    back_in[0, b] = back_out[0, b]
    wait_bytes(inc_in.at[pl.ds(0, n_reg - 1)], inc_in_sem)

    def straight(blocks):
        return jnp.stack([blocks, pltpu.roll(blocks, MEMS, axis=2)], axis=1).reshape(LANES, LANES).T

    fine_i = lax.broadcasted_iota(jnp.int32, (LANES, 2 * LANES), 1)
    coarse_i = lax.broadcasted_iota(jnp.int32, (LANES, 2 * LANES), 0)
    widen = jnp.where(lax.div(fine_i, 2) == coarse_i, 1.0, 0.0).astype(jnp.float32)
    for j in range(own_tiles):
        wide = dot(straight(inc_in[8 * j : 8 * j + 8])[0:64], widen, precision=HIGHEST)
        for var in range(3):
            for e in range(2):
                for k in range(2):
                    at = (2 * var + e) * 2 * own_tiles + 2 * j + k
                    part = wide[16 * var : 16 * var + 1, k * LANES : (k + 1) * LANES]
                    fo_ref[at : at + 1, :] = fc_ref[at : at + 1, :] + part

    for s in order:
        wait_bytes(back_in.at[s, pl.ds(0, n_reg - 1 if s == 0 else n_reg)], back_in_sem.at[s])
        first = lax.rem(a + s, n_mem) * own_tiles

        def unpack(j, carry):
            for var in range(3):
                start = pl.multiple_of(j * 8, 8)
                blocks = back_in[s, pl.ds(start, 8), var]
                ana_ref[var, pl.ds(first + j, MEMS, stride=tiles), :] = straight(blocks)[0:MEMS]
            return carry

        lax.fori_loop(0, own_tiles, unpack, 0)

    wait_bytes(c_out.at[pl.ds(0, n_reg - 1)], c_out_sem)
    wait_bytes(out_box.at[pl.ds(0, peers - 1)], out_sem)
    wait_bytes(inc_out.at[pl.ds(0, n_reg - 1)], inc_out_sem)
    wait_bytes(out_box.at[pl.ds(0, peers - 1)], back_out_sem)
    for s in order:
        for inside, copy in halo_copies(s):
            pl.when(inside)(copy.wait_send)

    own_edge = (b == plane - 1) | (b == plane)
    own_edge |= ((b == n_reg - 1) & (a != n_mem - 1)) | ((b == 0) & (a != 0))

    @pl.when(own_edge)
    def _():
        wait_bytes(c_out.at[pl.ds(0, 4 * n_mem - 1)], edge_sem)

    @pl.when(jnp.logical_not(own_edge))
    def _():
        wait_bytes(c_out.at[pl.ds(0, 4 * n_mem)], edge_sem)


def step(n_mem, n_reg, h, u, v, cu, cv, obs_index, obs_weight, obs_value, obs_var, obs_count, fine):
    peers = n_mem * n_reg
    members = n_mem * MEMS
    tiles = peers * COLS // LANES
    obs = obs_value.shape[1]
    cells = n_reg // 2 * COLS
    f32 = jnp.float32
    flat = (MEMS * tiles, LANES)
    flat_fine = (fine.size // LANES, LANES)
    vmem = pl.BlockSpec(memory_space=pltpu.VMEM)
    dma = pltpu.SemaphoreType.DMA
    outs = pl.pallas_call(
        functools.partial(kernel, (n_mem, n_reg)),
        out_shape=[
            jax.ShapeDtypeStruct((3, *flat), f32), jax.ShapeDtypeStruct(flat_fine, f32),
        ],
        in_specs=[pl.BlockSpec(memory_space=pl.ANY)] * 3 + [vmem] * 6 + [pl.BlockSpec(memory_space=pltpu.SMEM), vmem],
        out_specs=[vmem] * 2,
        scratch_shapes=[
            pltpu.VMEM((peers, 3, 8, LANES), f32),
            pltpu.VMEM((n_mem, n_reg, 3, 8, LANES), f32),
            pltpu.VMEM((n_reg, 8, LANES), f32),
            pltpu.VMEM((n_reg, 8, LANES), f32),
            pltpu.VMEM((n_mem, n_reg, 8, LANES), f32),
            pltpu.VMEM((n_mem, n_reg, 8, LANES), f32),
            pltpu.VMEM((n_mem, n_reg, 8, LANES), f32),
            pltpu.VMEM((n_mem, n_reg, 8, LANES), f32),
            pltpu.VMEM((3, n_reg + 2, 16, LANES), f32),
            pltpu.VMEM((n_reg + 2, 16, LANES), f32),
            pltpu.VMEM((n_reg + 2, 16, LANES), f32),
            pltpu.VMEM((3, n_reg, 16, members), f32),
            pltpu.VMEM((2, 3 * cells, obs), f32),
            pltpu.VMEM((2, 3 * cells, obs), jnp.bfloat16),
            pltpu.VMEM((2, 3 * cells, obs), jnp.bfloat16),
            pltpu.VMEM((3, cells, members + LANES), f32),
            pltpu.VMEM((n_mem, n_reg, 3, 8, LANES), f32),
            pltpu.VMEM((n_mem, n_reg, 3, 8, LANES), f32),
            pltpu.VMEM((n_reg, 8, LANES), f32),
            pltpu.VMEM((n_reg, 8, LANES), f32),
            pltpu.VMEM(flat, f32), pltpu.VMEM(flat, f32), pltpu.VMEM(flat, f32),
            pltpu.VMEM((2, 8, LANES), f32),
            pltpu.VMEM((n_mem, 4, 8, LANES), f32),
            dma, dma((n_mem,)), dma, dma, dma((2, n_mem)), dma((2, n_mem)),
            dma, dma((n_mem,)), dma, dma, dma((3,)), dma,
        ],
        compiler_params=pltpu.CompilerParams(
            collective_id=0, has_side_effects=True, vmem_limit_bytes=56 * 1024 * 1024
        ),
    )(
        h.reshape(flat), u.reshape(flat), v.reshape(flat),
        cu.reshape(tiles, LANES), cv.reshape(tiles, LANES),
        obs_index.transpose(0, 2, 1), obs_weight.transpose(0, 2, 1),
        obs_value, obs_var, obs_count, fine.reshape(flat_fine),
    )
    return tuple(outs[0][var].reshape(h.shape) for var in range(3)) + (outs[1].reshape(fine.shape),)


def solution(mesh):
    fields = P("member", "region", "fine")
    regions = ("member", "region", "fine")
    fine = P(None, "region", "fine", "member")
    return jax.shard_map(
        functools.partial(step, mesh.shape["member"], mesh.shape["region"]),
        mesh=mesh,
        in_specs=(
            fields, fields, fields,
            P("region", "fine"), P("region", "fine"),
            P(regions, None, None), P(regions, None, None),
            P(regions, None), P(regions, None), P(regions),
            fine,
        ),
        out_specs=(fields, fields, fields, fine),
        check_vma=False,
    )
```

```python
import functools

import jax
import jax.numpy as jnp
from jax import lax
from jax.experimental import pallas as pl
from jax.experimental.pallas import tpu as pltpu
from jax.sharding import PartitionSpec as P

MESH = pl.DeviceIdType.MESH
STEPS = 4
NEWTON = 8
HIGHEST = lax.Precision.HIGHEST
LANES = 128
MEMS = 64
COLS = 16


ROWS_COLS = ((1,), (0,))


def dot(x, y, contract=ROWS_COLS, precision=None):
    return lax.dot_general(
        x, y, (contract, ((), ())), precision=precision, preferred_element_type=jnp.float32
    )


def split(x):
    high = x.astype(jnp.bfloat16)
    return high, (x - high.astype(jnp.float32)).astype(jnp.bfloat16)


def dot3(x, y, contract=ROWS_COLS):
    rows = 1 - contract[0][0]
    size = x[0].shape[rows]
    both = dot(jnp.concatenate(x, axis=rows), y[0], contract)
    return both[:size] + (both[size:] + dot(x[0], y[1], contract))


def all_sum(x):
    return jnp.sum(jnp.sum(x, axis=1, keepdims=True), axis=0, keepdims=True)


def kernel(
    dims,
    h_src, u_src, v_src, cu_src, cv_src, idx_src, wt_src, val_src, var_src, cnt_src, fc_src,
    ana_ref, fo_ref,
    out_box, in_box, c_out, c_in, to_west, to_east, from_east, from_west,
    window, cour_u, cour_v, state, stencil, stencil_hi, stencil_lo, ana,
    back_out, back_in, inc_out, inc_in, h_in, u_in, v_in, c_edge, edges,
    cu_ref, cv_ref, idx_ref, wt_ref, val_ref, var_ref, cnt_ref, fc_ref,
    out_sem, in_sem, c_out_sem, c_in_sem, halo_out_sem, halo_in_sem,
    back_out_sem, back_in_sem, inc_out_sem, inc_in_sem, load_sem, edge_sem,
):
    n_mem, n_reg = dims
    peers = n_mem * n_reg
    tiles = peers * COLS // LANES
    lane_tiles = n_mem * MEMS // LANES
    members = n_mem * MEMS
    half_rows = n_reg // 2
    cells = half_rows * COLS
    own_tiles = n_reg * COLS // LANES
    plane = n_reg // 2
    phases = [[0], [1, 3], [2]] if n_mem == 4 else [[s] for s in range(n_mem)]
    order = [s for phase in phases for s in phase]
    a = lax.axis_index("member")
    b = lax.axis_index("region")
    f = lax.axis_index("fine")
    me = a * n_reg + b

    def place(p):
        return (lax.div(p, n_reg), lax.rem(p, n_reg), f)

    loads = [
        pltpu.make_async_copy(ref, box, load_sem.at[i])
        for i, (ref, box) in enumerate((
            (h_src, h_in), (u_src, u_in), (v_src, v_in), (cu_src, cu_ref), (cv_src, cv_ref),
            (idx_src, idx_ref), (wt_src, wt_ref), (val_src, val_ref), (var_src, var_ref),
            (cnt_src, cnt_ref), (fc_src, fc_ref),
        ))
    ]
    for load in loads:
        load.start()

    barrier = pltpu.get_barrier_semaphore()

    def greet(i, carry):
        pl.semaphore_signal(
            barrier, inc=1, device_id=place(lax.rem(me + i, peers)), device_id_type=MESH
        )
        return carry

    def greet_other_half(i, carry):
        p_mem, p_row, _ = place(i)
        pl.semaphore_signal(barrier, inc=1, device_id=(p_mem, p_row, 1 - f), device_id_type=MESH)
        return carry

    @pl.when((me == 0) | (me == peers - 1))
    def _():
        lax.fori_loop(0, peers, greet_other_half, 0)

    lax.fori_loop(1, peers, greet, 0)
    for load in loads[:3]:
        load.wait()

    lane = lax.broadcasted_iota(jnp.int32, (8, LANES), 1)
    left = lane < MEMS
    low = lax.broadcasted_iota(jnp.int32, (8, LANES), 0) < 4
    crossed = (low & ~left) | (~low & left)

    def across(x):
        return pltpu.roll(x, MEMS, axis=x.ndim - 1)

    def up(x):
        return pltpu.roll(x, 4, axis=x.ndim - 2)

    def turned(block):
        pair = jnp.concatenate([block, pltpu.roll(block, LANES - 8, axis=1)], axis=0)
        return pair.T

    def pack(j, carry):
        for var, ref in enumerate((h_in, u_in, v_in)):
            pair = [ref[pl.ds(2 * j + k, MEMS, stride=tiles), :] for k in range(2)]
            t = jnp.concatenate(pair, axis=0).T
            for k in range(8):
                x, y = t[COLS * k : COLS * k + 8], t[COLS * k + 8 : COLS * k + 16]
                out_box[16 * j + k, var] = jnp.where(left, x, across(y))
                out_box[16 * j + 8 + k, var] = jnp.where(left, across(x), y)
        return carry

    lax.fori_loop(0, tiles // 2, pack, 0)

    def courant(j):
        cu = jnp.broadcast_to(cu_ref[pl.ds(j, 1), :], (32, LANES))
        cv = jnp.broadcast_to(cv_ref[pl.ds(j, 1), :], (32, LANES))
        return turned(jnp.concatenate([cu, cv], axis=0))

    def west_going(h, u, v, c):
        c, u = across(c), across(u)
        return jnp.where(low, jnp.where(left, h, u), up(jnp.where(left, v, c)))

    def east_going(h, u, v, c):
        c, u = across(c), across(u)
        return jnp.where(low, up(jnp.where(left, c, v)), jnp.where(left, u, h))

    pl.semaphore_wait(barrier, peers + 1)

    def send_rest():
        for load in loads[3:]:
            load.wait()
        for j in range(own_tiles):
            t = courant(a * own_tiles + j)
            for k in range(8):
                c_out[j * 8 + k] = t[COLS * k : COLS * k + 8]

        c_edge[0] = courant(lax.rem(a + 1, n_mem) * own_tiles)[0:8]
        c_edge[1] = courant(lax.rem(a * own_tiles + tiles - 1, tiles))[7 * COLS : 7 * COLS + 8]
        for k in range(n_mem):
            for kind, (m, c, going) in enumerate((
                (k * n_reg + plane, c_out[plane], west_going),
                ((k + 1) % n_mem * n_reg, c_edge[0], west_going),
                (k * n_reg + plane - 1, c_out[plane - 1], east_going),
                ((k * n_reg + peers - 1) % peers, c_edge[1], east_going),
            )):
                edges[k, kind] = going(out_box[m, 0], out_box[m, 1], out_box[m, 2], c)

        def send_courant(i, carry):
            p = lax.rem(b + i, n_reg)
            pltpu.make_async_remote_copy(
                src_ref=c_out.at[p], dst_ref=c_in.at[b], send_sem=c_out_sem, recv_sem=c_in_sem,
                device_id=(a, p, f), device_id_type=MESH,
            ).start()
            return carry

        lax.fori_loop(1, n_reg, send_courant, 0)
        c_in[b] = c_out[b]
        for s in order:
            p_mem = lax.rem(a + s, n_mem)
            slot = (n_mem - s) % n_mem
            for kind, (p_row, box, other) in enumerate((
                (plane - 1, from_east, None),
                (n_reg - 1, from_east, n_mem - 1),
                (plane, from_west, None),
                (0, from_west, 0),
            )):
                here = f if other is None else jnp.where(p_mem == other, 1 - f, f)
                sem = halo_in_sem.at[kind // 2, slot]
                go = pltpu.make_async_remote_copy(
                    src_ref=edges.at[p_mem, kind], dst_ref=box.at[slot, b],
                    send_sem=edge_sem, recv_sem=sem,
                    device_id=(p_mem, p_row, here), device_id_type=MESH,
                )
                if s:
                    go.start()
                else:
                    own = (b == p_row) if other is None else (b == p_row) & (a != other)
                    stay = pltpu.make_async_copy(edges.at[p_mem, kind], box.at[slot, b], sem)
                    pl.when(own)(stay.start)
                    pl.when(jnp.logical_not(own))(go.start)

    in_box[0, b] = out_box[me]

    for phase in phases:
        if phase == phases[-1]:
            send_rest()

        def send_state(i, carry):
            p_row = lax.rem(b + i, n_reg)
            for s in phase:
                p_mem = lax.rem(a + s, n_mem)
                slot = (n_mem - s) % n_mem
                pltpu.make_async_remote_copy(
                    src_ref=out_box.at[p_mem * n_reg + p_row], dst_ref=in_box.at[slot, b],
                    send_sem=out_sem, recv_sem=in_sem.at[slot],
                    device_id=(p_mem, p_row, f), device_id_type=MESH,
                ).start()
            return carry

        lax.fori_loop(1 if phase == [0] else 0, n_reg, send_state, 0)
    obs = idx_ref.shape[2]
    for q in range(2):

        def spread_weights(g, carry):
            start = pl.multiple_of(g * 16, 16)
            cell = lax.broadcasted_iota(jnp.int32, (16, obs), 0) + g * 16
            total = jnp.zeros((16, obs), jnp.float32)
            for j in range(4):
                total += jnp.where(idx_ref[q, j : j + 1, :] == cell, wt_ref[q, j : j + 1, :], 0.0)
            high, rest = split(total)
            stencil[q, pl.ds(start, 16), :] = total
            stencil_hi[q, pl.ds(start, 16), :] = high
            stencil_lo[q, pl.ds(start, 16), :] = rest
            return carry

        lax.fori_loop(0, 3 * cells // 16, spread_weights, 0)

    def wait_bytes(ref, sem):
        pltpu.make_async_copy(ref, ref, sem).wait()

    wait_bytes(c_in.at[pl.ds(0, n_reg - 1)], c_in_sem)

    inside_west = lax.rem(b, plane) != 0
    inside_east = lax.rem(b, plane) != plane - 1

    def halo_copies(s):
        go_west = pltpu.make_async_remote_copy(
            src_ref=to_west.at[s], dst_ref=from_east.at[s],
            send_sem=halo_out_sem.at[0, s], recv_sem=halo_in_sem.at[0, s],
            device_id=(a, lax.rem(b + n_reg - 1, n_reg), f), device_id_type=MESH,
        )
        go_east = pltpu.make_async_remote_copy(
            src_ref=to_east.at[s], dst_ref=from_west.at[s],
            send_sem=halo_out_sem.at[1, s], recv_sem=halo_in_sem.at[1, s],
            device_id=(a, lax.rem(b + 1, n_reg), f), device_id_type=MESH,
        )
        return (inside_west, go_west), (inside_east, go_east)

    def send_rim(s):
        wait_bytes(in_box.at[s, pl.ds(0, n_reg - 1 if s == 0 else n_reg)], in_sem.at[s])

        def quarter(i, carry):
            at = pl.ds(i * 8, 8)
            h, u, v = in_box[s, at, 0], in_box[s, at, 1], in_box[s, at, 2]
            c = c_in[at]
            to_west[s, at] = west_going(h, u, v, c)
            to_east[s, at] = east_going(h, u, v, c)
            return carry

        lax.fori_loop(0, n_reg // 8, quarter, 0)
        for inside, copy in halo_copies(s):
            pl.when(inside)(copy.start)

    def broad(c, at):
        return jnp.where(
            left,
            jnp.broadcast_to(c[:, :, at : at + 1], c.shape),
            jnp.broadcast_to(c[:, :, at + MEMS : at + MEMS + 1], c.shape),
        )

    def forecast(s):
        wait_bytes(from_east.at[s], halo_in_sem.at[0, s])
        wait_bytes(from_west.at[s], halo_in_sem.at[1, s])

        def rim(i, carry):
            at, to = pl.ds(i * 8, 8), pl.ds(i * 8 + 1, 8)
            e, w = from_east[s, at], from_west[s, at]
            p, q = jnp.where(low, e, w), up(jnp.where(low, w, e))
            h, u, v = in_box[s, at, 0], in_box[s, at, 1], in_box[s, at, 2]
            window[0, to, 0:8] = h
            window[1, to, 0:8] = u
            window[2, to, 0:8] = v
            window[0, to, 8:16] = across(jnp.where(crossed, h, p))
            window[1, to, 8:16] = jnp.where(crossed, p, across(u))
            window[2, to, 8:16] = across(jnp.where(crossed, v, q))
            if s == 0:
                c = c_in[at]
                cour_u[to, 0:8] = broad(c, 0)
                cour_v[to, 0:8] = broad(c, 32)
                c = jnp.where(crossed, q, across(c))
                cour_u[to, 8:16] = broad(c, 0)
                cour_v[to, 8:16] = broad(c, 32)
            return carry

        lax.fori_loop(0, n_reg // 8, rim, 0)

        def heights(i, carry):
            at = pl.ds(i * 8 + 1, 8)
            flux_u = cour_u[at] * window[1, at]
            flux_v = cour_v[pl.ds(i * 8, 9)] * window[2, pl.ds(i * 8, 9)]
            gain = flux_u - pltpu.roll(flux_u, 1, axis=1) + flux_v[1:] - flux_v[:-1]
            window[0, at] = window[0, at] - gain
            return carry

        def currents(i, carry):
            at = pl.ds(i * 8 + 1, 8)
            h = window[0, pl.ds(i * 8 + 1, 9)]
            window[1, at] = window[1, at] - (pltpu.roll(h[:-1], 15, axis=1) - h[:-1])
            window[2, at] = window[2, at] - (h[1:] - h[:-1])
            return carry

        def one_step(i, carry):
            lax.fori_loop(0, n_reg // 8, heights, 0, unroll=True)
            lax.fori_loop(0, n_reg // 8, currents, 0, unroll=True)
            return carry

        lax.fori_loop(0, STEPS, one_step, 0)
        tile = slice(s // 2 * LANES, (s // 2 + 1) * LANES)
        keep = left if s % 2 else ~left

        def place_cells(i, carry):
            at = pl.ds(i * 8, 8)
            for var in range(3):
                x = window[var, pl.ds(i * 8 + 1, 8), 0:8]
                y = across(x)
                x, y = (y, x) if s % 2 else (x, y)
                state[var, at, 0:8, tile] = jnp.where(keep, state[var, at, 0:8, tile], x)
                state[var, at, 8:16, tile] = jnp.where(keep, state[var, at, 8:16, tile], y)
            return carry

        lax.fori_loop(0, n_reg // 8, place_cells, 0)

    blank = jnp.zeros((16, LANES), jnp.float32)
    window[0, n_reg + 1] = blank
    window[2, 0] = blank
    cour_v[0] = blank

    for s in order[:-1]:
        send_rim(s)
    forecast(order[0])
    send_rim(order[-1])
    for s in order[1:]:
        forecast(s)

    row_i = lax.broadcasted_iota(jnp.int32, (members, members), 0)
    col_i = lax.broadcasted_iota(jnp.int32, (members, members), 1)
    eye = jnp.where(row_i == col_i, 1.0, 0.0).astype(jnp.float32)
    obs_i = lax.broadcasted_iota(jnp.int32, (1, obs), 1)

    for q in range(2):
        spreads, means = [], []
        obs_spread = jnp.zeros((members, obs), jnp.float32)
        mean_obs = jnp.zeros((1, obs), jnp.float32)
        for var in range(3):
            x = state[var, q * half_rows : (q + 1) * half_rows].reshape(cells, members)
            mean = jnp.sum(x, axis=1, keepdims=True) / members
            spread = split(x - mean)
            block = slice(var * cells, (var + 1) * cells)
            weights = (stencil_hi[q, block, :], stencil_lo[q, block, :])
            obs_spread += dot3(spread, weights, ((0,), (0,)))
            mean_obs += jnp.sum(stencil[q, block, :] * mean, axis=0, keepdims=True)
            spreads.append(spread)
            means.append(mean)
        active = jnp.where(obs_i < cnt_ref[q], 1.0, 0.0)
        weighted = obs_spread * (active / var_ref[q : q + 1, :])
        gram_sum = dot3(split(weighted), split(obs_spread), ((1,), (1,)))
        scaled = eye + gram_sum / (members - 1)
        fro = jnp.sqrt(all_sum(scaled * scaled))
        innovation = jnp.sum(weighted * (val_ref[q : q + 1, :] - mean_obs), axis=1, keepdims=True)
        iterate = scaled / fro
        factor = split(1.5 * eye - 0.5 * iterate)

        def sweep(i, carry):
            iterate, root = carry
            factor = split(1.5 * eye - 0.5 * dot3(root, iterate))
            return split(dot3(iterate, factor)), split(dot3(factor, root))

        iterate, root = lax.fori_loop(
            1, NEWTON - 1, sweep, (split(dot3(split(iterate), factor)), factor), unroll=2
        )
        factor = split(1.5 * eye - 0.5 * dot3(root, iterate))
        transform = dot3(factor, root) / jnp.sqrt(fro)
        halfway = jnp.sum(transform * innovation, axis=0, keepdims=True)
        mean_weights = jnp.sum(transform * halfway, axis=1, keepdims=True) / (members - 1)
        both = split(jnp.concatenate(
            [transform + mean_weights, jnp.broadcast_to(mean_weights, (members, LANES))], axis=1
        ))
        for var in range(3):
            moved = dot3(spreads[var], both)
            ana[var, :, 0:members] = moved[:, 0:members] + means[var]
            ana[var, :, members:] = moved[:, members:]

        def unload(i, carry):
            i = lax.rem(b + i, half_rows)
            lo = pl.multiple_of(i * COLS, 8)
            hi = pl.multiple_of(i * COLS + 8, 8)
            row = q * half_rows + i
            for t in range(lane_tiles):
                at = slice(t * LANES, (t + 1) * LANES)
                for var in range(3):
                    x, y = ana[var, pl.ds(lo, 8), at], ana[var, pl.ds(hi, 8), at]
                    back_out[2 * t, row, var] = jnp.where(left, x, across(y))
                    back_out[2 * t + 1, row, var] = jnp.where(left, across(x), y)
            packed = jnp.zeros((8, LANES), jnp.float32)
            for var in range(3):
                x = ana[var, pl.ds(lo, 8), members:]
                y = ana[var, pl.ds(hi, 8), members:]
                packed = jnp.where(lax.div(lax.rem(lane, MEMS), 16) == var, jnp.where(left, x, y), packed)
            inc_out[row] = packed
            if q == 0:
                send_inc(row)
                for s in order:
                    send_back(s, row)
            return carry

        def send_inc(row):
            go = pltpu.make_async_remote_copy(
                src_ref=inc_out.at[row], dst_ref=inc_in.at[b], send_sem=inc_out_sem,
                recv_sem=inc_in_sem, device_id=(a, row, f), device_id_type=MESH,
            )
            pl.when(row != b)(go.start)

        def send_back(s, row):
            slot = (n_mem - s) % n_mem
            go = pltpu.make_async_remote_copy(
                src_ref=back_out.at[s, row], dst_ref=back_in.at[slot, b],
                send_sem=back_out_sem, recv_sem=back_in_sem.at[slot],
                device_id=(lax.rem(a + s, n_mem), row, f), device_id_type=MESH,
            )
            if s:
                go.start()
            else:
                pl.when(row != b)(go.start)

        lax.fori_loop(0, half_rows, unload, 0)
        if q:
            for phase in phases:

                def send_phase(i, carry):
                    row = q * half_rows + lax.rem(b + i, half_rows)
                    if phase == phases[0]:
                        send_inc(row)
                    for s in phase:
                        send_back(s, row)
                    return carry

                lax.fori_loop(0, half_rows, send_phase, 0)

    inc_in[b] = inc_out[b]
    back_in[0, b] = back_out[0, b]
    wait_bytes(inc_in.at[pl.ds(0, n_reg - 1)], inc_in_sem)

    def straight(blocks):
        return jnp.stack([blocks, pltpu.roll(blocks, MEMS, axis=2)], axis=1).reshape(LANES, LANES).T

    fine_i = lax.broadcasted_iota(jnp.int32, (LANES, 2 * LANES), 1)
    coarse_i = lax.broadcasted_iota(jnp.int32, (LANES, 2 * LANES), 0)
    widen = jnp.where(lax.div(fine_i, 2) == coarse_i, 1.0, 0.0).astype(jnp.float32)
    for j in range(own_tiles):
        wide = dot(straight(inc_in[8 * j : 8 * j + 8])[0:64], widen, precision=HIGHEST)
        for var in range(3):
            for e in range(2):
                for k in range(2):
                    at = (2 * var + e) * 2 * own_tiles + 2 * j + k
                    part = wide[16 * var : 16 * var + 1, k * LANES : (k + 1) * LANES]
                    fo_ref[at : at + 1, :] = fc_ref[at : at + 1, :] + part

    for s in order:
        wait_bytes(back_in.at[s, pl.ds(0, n_reg - 1 if s == 0 else n_reg)], back_in_sem.at[s])
        first = lax.rem(a + s, n_mem) * own_tiles

        def unpack(j, carry):
            for var in range(3):
                x = back_in[s, pl.ds(pl.multiple_of(j * 16, 8), 8), var]
                y = back_in[s, pl.ds(pl.multiple_of(j * 16 + 8, 8), 8), var]
                rows = [jnp.where(left, x, across(y)), jnp.where(left, across(x), y)]
                t = jnp.stack(rows, axis=1).reshape(LANES, LANES).T
                for k in range(2):
                    at = pl.ds(first + 2 * j + k, MEMS, stride=tiles)
                    ana_ref[var, at, :] = t[k * MEMS : (k + 1) * MEMS]
            return carry

        lax.fori_loop(0, own_tiles // 2, unpack, 0)

    wait_bytes(c_out.at[pl.ds(0, n_reg - 1)], c_out_sem)
    wait_bytes(out_box.at[pl.ds(0, peers - 1)], out_sem)
    wait_bytes(inc_out.at[pl.ds(0, n_reg - 1)], inc_out_sem)
    wait_bytes(out_box.at[pl.ds(0, peers - 1)], back_out_sem)
    for s in order:
        for inside, copy in halo_copies(s):
            pl.when(inside)(copy.wait_send)

    own_edge = (b == plane - 1) | (b == plane)
    own_edge |= ((b == n_reg - 1) & (a != n_mem - 1)) | ((b == 0) & (a != 0))

    @pl.when(own_edge)
    def _():
        wait_bytes(c_out.at[pl.ds(0, 4 * n_mem - 1)], edge_sem)

    @pl.when(jnp.logical_not(own_edge))
    def _():
        wait_bytes(c_out.at[pl.ds(0, 4 * n_mem)], edge_sem)


def step(n_mem, n_reg, h, u, v, cu, cv, obs_index, obs_weight, obs_value, obs_var, obs_count, fine):
    peers = n_mem * n_reg
    members = n_mem * MEMS
    tiles = peers * COLS // LANES
    obs = obs_value.shape[1]
    cells = n_reg // 2 * COLS
    f32 = jnp.float32
    flat = (MEMS * tiles, LANES)
    flat_fine = (fine.size // LANES, LANES)
    vmem = pl.BlockSpec(memory_space=pltpu.VMEM)
    dma = pltpu.SemaphoreType.DMA
    outs = pl.pallas_call(
        functools.partial(kernel, (n_mem, n_reg)),
        out_shape=[
            jax.ShapeDtypeStruct((3, *flat), f32), jax.ShapeDtypeStruct(flat_fine, f32),
        ],
        in_specs=[pl.BlockSpec(memory_space=pl.ANY)] * 11,
        out_specs=[vmem] * 2,
        scratch_shapes=[
            pltpu.VMEM((peers, 3, 8, LANES), f32),
            pltpu.VMEM((n_mem, n_reg, 3, 8, LANES), f32),
            pltpu.VMEM((n_reg, 8, LANES), f32),
            pltpu.VMEM((n_reg, 8, LANES), f32),
            pltpu.VMEM((n_mem, n_reg, 8, LANES), f32),
            pltpu.VMEM((n_mem, n_reg, 8, LANES), f32),
            pltpu.VMEM((n_mem, n_reg, 8, LANES), f32),
            pltpu.VMEM((n_mem, n_reg, 8, LANES), f32),
            pltpu.VMEM((3, n_reg + 2, 16, LANES), f32),
            pltpu.VMEM((n_reg + 2, 16, LANES), f32),
            pltpu.VMEM((n_reg + 2, 16, LANES), f32),
            pltpu.VMEM((3, n_reg, 16, members), f32),
            pltpu.VMEM((2, 3 * cells, obs), f32),
            pltpu.VMEM((2, 3 * cells, obs), jnp.bfloat16),
            pltpu.VMEM((2, 3 * cells, obs), jnp.bfloat16),
            pltpu.VMEM((3, cells, members + LANES), f32),
            pltpu.VMEM((n_mem, n_reg, 3, 8, LANES), f32),
            pltpu.VMEM((n_mem, n_reg, 3, 8, LANES), f32),
            pltpu.VMEM((n_reg, 8, LANES), f32),
            pltpu.VMEM((n_reg, 8, LANES), f32),
            pltpu.VMEM(flat, f32), pltpu.VMEM(flat, f32), pltpu.VMEM(flat, f32),
            pltpu.VMEM((2, 8, LANES), f32),
            pltpu.VMEM((n_mem, 4, 8, LANES), f32),
            pltpu.VMEM((tiles, LANES), f32), pltpu.VMEM((tiles, LANES), f32),
            pltpu.VMEM((2, 4, obs), jnp.int32), pltpu.VMEM((2, 4, obs), f32),
            pltpu.VMEM((2, obs), f32), pltpu.VMEM((2, obs), f32),
            pltpu.SMEM((2,), jnp.int32), pltpu.VMEM(flat_fine, f32),
            dma, dma((n_mem,)), dma, dma, dma((2, n_mem)), dma((2, n_mem)),
            dma, dma((n_mem,)), dma, dma, dma((11,)), dma,
        ],
        compiler_params=pltpu.CompilerParams(
            collective_id=0, has_side_effects=True, vmem_limit_bytes=56 * 1024 * 1024
        ),
    )(
        h.reshape(flat), u.reshape(flat), v.reshape(flat),
        cu.reshape(tiles, LANES), cv.reshape(tiles, LANES),
        obs_index.transpose(0, 2, 1), obs_weight.transpose(0, 2, 1),
        obs_value, obs_var, obs_count, fine.reshape(flat_fine),
    )
    return tuple(outs[0][var].reshape(h.shape) for var in range(3)) + (outs[1].reshape(fine.shape),)


def solution(mesh):
    fields = P("member", "region", "fine")
    regions = ("member", "region", "fine")
    fine = P(None, "region", "fine", "member")
    return jax.shard_map(
        functools.partial(step, mesh.shape["member"], mesh.shape["region"]),
        mesh=mesh,
        in_specs=(
            fields, fields, fields,
            P("region", "fine"), P("region", "fine"),
            P(regions, None, None), P(regions, None, None),
            P(regions, None), P(regions, None), P(regions),
            fine,
        ),
        out_specs=(fields, fields, fields, fine),
        check_vma=False,
    )
```

```python
import functools

import jax
import jax.numpy as jnp
from jax import lax
from jax.experimental import pallas as pl
from jax.experimental.pallas import tpu as pltpu
from jax.sharding import PartitionSpec as P

MESH = pl.DeviceIdType.MESH
STEPS = 4
NEWTON = 8
HIGHEST = lax.Precision.HIGHEST
LANES = 128
MEMS = 64
COLS = 16


ROWS_COLS = ((1,), (0,))


def dot(x, y, contract=ROWS_COLS, precision=None):
    return lax.dot_general(
        x, y, (contract, ((), ())), precision=precision, preferred_element_type=jnp.float32
    )


def split(x):
    high = x.astype(jnp.bfloat16)
    return high, (x - high.astype(jnp.float32)).astype(jnp.bfloat16)


def dot3(x, y, contract=ROWS_COLS):
    rows = 1 - contract[0][0]
    size = x[0].shape[rows]
    both = dot(jnp.concatenate(x, axis=rows), y[0], contract)
    return both[:size] + (both[size:] + dot(x[0], y[1], contract))


def all_sum(x):
    return jnp.sum(jnp.sum(x, axis=1, keepdims=True), axis=0, keepdims=True)


def kernel(
    dims,
    h_src, u_src, v_src, cu_src, cv_src, idx_src, wt_src, val_src, var_src, cnt_src, fc_src,
    ana_ref, fo_ref,
    out_box, in_box, c_out, c_in, to_west, to_east, from_east, from_west,
    window, cour_u, cour_v, state, stencil, stencil_hi, stencil_lo, ana,
    back_out, back_in, inc_out, inc_in, h_in, u_in, v_in, c_edge, edges,
    cu_ref, cv_ref, idx_ref, wt_ref, val_ref, var_ref, cnt_ref, fc_ref,
    out_sem, in_sem, c_out_sem, c_in_sem, halo_out_sem, halo_in_sem,
    back_out_sem, back_in_sem, inc_out_sem, inc_in_sem, load_sem, edge_sem,
):
    n_mem, n_reg = dims
    peers = n_mem * n_reg
    tiles = peers * COLS // LANES
    lane_tiles = n_mem * MEMS // LANES
    members = n_mem * MEMS
    half_rows = n_reg // 2
    cells = half_rows * COLS
    own_tiles = n_reg * COLS // LANES
    plane = n_reg // 2
    phases = [[0], [1, 3], [2]] if n_mem == 4 else [[s] for s in range(n_mem)]
    order = [s for phase in phases for s in phase]
    a = lax.axis_index("member")
    b = lax.axis_index("region")
    f = lax.axis_index("fine")
    me = a * n_reg + b

    def place(p):
        return (lax.div(p, n_reg), lax.rem(p, n_reg), f)

    loads = [
        pltpu.make_async_copy(ref, box, load_sem.at[i])
        for i, (ref, box) in enumerate((
            (h_src, h_in), (u_src, u_in), (v_src, v_in), (cu_src, cu_ref), (cv_src, cv_ref),
            (idx_src, idx_ref), (wt_src, wt_ref), (val_src, val_ref), (var_src, var_ref),
            (cnt_src, cnt_ref), (fc_src, fc_ref),
        ))
    ]
    for load in loads:
        load.start()

    barrier = pltpu.get_barrier_semaphore()

    def greet(i, carry):
        pl.semaphore_signal(
            barrier, inc=1, device_id=place(lax.rem(me + i, peers)), device_id_type=MESH
        )
        return carry

    def greet_other_half(i, carry):
        p_mem, p_row, _ = place(i)
        pl.semaphore_signal(barrier, inc=1, device_id=(p_mem, p_row, 1 - f), device_id_type=MESH)
        return carry

    @pl.when((me == 0) | (me == peers - 1))
    def _():
        lax.fori_loop(0, peers, greet_other_half, 0)

    lax.fori_loop(1, peers, greet, 0)
    for load in loads[:3]:
        load.wait()

    lane = lax.broadcasted_iota(jnp.int32, (8, LANES), 1)
    left = lane < MEMS
    low = lax.broadcasted_iota(jnp.int32, (8, LANES), 0) < 4
    crossed = (low & ~left) | (~low & left)

    def across(x):
        return pltpu.roll(x, MEMS, axis=x.ndim - 1)

    def up(x):
        return pltpu.roll(x, 4, axis=x.ndim - 2)

    def turned(block):
        pair = jnp.concatenate([block, pltpu.roll(block, LANES - 8, axis=1)], axis=0)
        return pair.T

    def pack(j, carry):
        for var, ref in enumerate((h_in, u_in, v_in)):
            pair = [ref[pl.ds(2 * j + k, MEMS, stride=tiles), :] for k in range(2)]
            t = jnp.concatenate(pair, axis=0).T
            for k in range(8):
                x, y = t[COLS * k : COLS * k + 8], t[COLS * k + 8 : COLS * k + 16]
                out_box[16 * j + k, var] = jnp.where(left, x, across(y))
                out_box[16 * j + 8 + k, var] = jnp.where(left, across(x), y)
        return carry

    lax.fori_loop(0, tiles // 2, pack, 0)

    def courant(j):
        cu = jnp.broadcast_to(cu_ref[pl.ds(j, 1), :], (32, LANES))
        cv = jnp.broadcast_to(cv_ref[pl.ds(j, 1), :], (32, LANES))
        return turned(jnp.concatenate([cu, cv], axis=0))

    def west_going(h, u, v, c):
        c, u = across(c), across(u)
        return jnp.where(low, jnp.where(left, h, u), up(jnp.where(left, v, c)))

    def east_going(h, u, v, c):
        c, u = across(c), across(u)
        return jnp.where(low, up(jnp.where(left, c, v)), jnp.where(left, u, h))

    pl.semaphore_wait(barrier, peers + 1)

    def send_rest():
        for load in loads[3:]:
            load.wait()
        for j in range(own_tiles):
            t = courant(a * own_tiles + j)
            for k in range(8):
                c_out[j * 8 + k] = t[COLS * k : COLS * k + 8]

        c_edge[0] = courant(lax.rem(a + 1, n_mem) * own_tiles)[0:8]
        c_edge[1] = courant(lax.rem(a * own_tiles + tiles - 1, tiles))[7 * COLS : 7 * COLS + 8]
        for k in range(n_mem):
            for kind, (m, c, going) in enumerate((
                (k * n_reg + plane, c_out[plane], west_going),
                ((k + 1) % n_mem * n_reg, c_edge[0], west_going),
                (k * n_reg + plane - 1, c_out[plane - 1], east_going),
                ((k * n_reg + peers - 1) % peers, c_edge[1], east_going),
            )):
                edges[k, kind] = going(out_box[m, 0], out_box[m, 1], out_box[m, 2], c)

        def send_courant(i, carry):
            p = lax.rem(b + i, n_reg)
            pltpu.make_async_remote_copy(
                src_ref=c_out.at[p], dst_ref=c_in.at[b], send_sem=c_out_sem, recv_sem=c_in_sem,
                device_id=(a, p, f), device_id_type=MESH,
            ).start()
            return carry

        lax.fori_loop(1, n_reg, send_courant, 0)
        c_in[b] = c_out[b]
        for s in order:
            p_mem = lax.rem(a + s, n_mem)
            slot = (n_mem - s) % n_mem
            for kind, (p_row, box, other) in enumerate((
                (plane - 1, from_east, None),
                (n_reg - 1, from_east, n_mem - 1),
                (plane, from_west, None),
                (0, from_west, 0),
            )):
                here = f if other is None else jnp.where(p_mem == other, 1 - f, f)
                sem = halo_in_sem.at[kind // 2, slot]
                go = pltpu.make_async_remote_copy(
                    src_ref=edges.at[p_mem, kind], dst_ref=box.at[slot, b],
                    send_sem=edge_sem, recv_sem=sem,
                    device_id=(p_mem, p_row, here), device_id_type=MESH,
                )
                if s:
                    go.start()
                else:
                    own = (b == p_row) if other is None else (b == p_row) & (a != other)
                    stay = pltpu.make_async_copy(edges.at[p_mem, kind], box.at[slot, b], sem)
                    pl.when(own)(stay.start)
                    pl.when(jnp.logical_not(own))(go.start)

    in_box[0, b] = out_box[me]

    for phase in phases:
        if phase == phases[-1]:
            send_rest()

        def send_state(i, carry):
            p_row = lax.rem(b + i, n_reg)
            for s in phase:
                p_mem = lax.rem(a + s, n_mem)
                slot = (n_mem - s) % n_mem
                pltpu.make_async_remote_copy(
                    src_ref=out_box.at[p_mem * n_reg + p_row], dst_ref=in_box.at[slot, b],
                    send_sem=out_sem, recv_sem=in_sem.at[slot],
                    device_id=(p_mem, p_row, f), device_id_type=MESH,
                ).start()
            return carry

        lax.fori_loop(1 if phase == [0] else 0, n_reg, send_state, 0)
    obs = idx_ref.shape[2]
    for q in range(2):

        def spread_weights(g, carry):
            start = pl.multiple_of(g * 16, 16)
            cell = lax.broadcasted_iota(jnp.int32, (16, obs), 0) + g * 16
            total = jnp.zeros((16, obs), jnp.float32)
            for j in range(4):
                total += jnp.where(idx_ref[q, j : j + 1, :] == cell, wt_ref[q, j : j + 1, :], 0.0)
            high, rest = split(total)
            stencil[q, pl.ds(start, 16), :] = total
            stencil_hi[q, pl.ds(start, 16), :] = high
            stencil_lo[q, pl.ds(start, 16), :] = rest
            return carry

        lax.fori_loop(0, 3 * cells // 16, spread_weights, 0)

    def wait_bytes(ref, sem):
        pltpu.make_async_copy(ref, ref, sem).wait()

    wait_bytes(c_in.at[pl.ds(0, n_reg - 1)], c_in_sem)

    inside_west = lax.rem(b, plane) != 0
    inside_east = lax.rem(b, plane) != plane - 1

    def halo_copies(s):
        go_west = pltpu.make_async_remote_copy(
            src_ref=to_west.at[s], dst_ref=from_east.at[s],
            send_sem=halo_out_sem.at[0, s], recv_sem=halo_in_sem.at[0, s],
            device_id=(a, lax.rem(b + n_reg - 1, n_reg), f), device_id_type=MESH,
        )
        go_east = pltpu.make_async_remote_copy(
            src_ref=to_east.at[s], dst_ref=from_west.at[s],
            send_sem=halo_out_sem.at[1, s], recv_sem=halo_in_sem.at[1, s],
            device_id=(a, lax.rem(b + 1, n_reg), f), device_id_type=MESH,
        )
        return (inside_west, go_west), (inside_east, go_east)

    def send_rim(s):
        wait_bytes(in_box.at[s, pl.ds(0, n_reg - 1 if s == 0 else n_reg)], in_sem.at[s])

        def quarter(i, carry):
            at = pl.ds(i * 8, 8)
            h, u, v = in_box[s, at, 0], in_box[s, at, 1], in_box[s, at, 2]
            c = c_in[at]
            to_west[s, at] = west_going(h, u, v, c)
            to_east[s, at] = east_going(h, u, v, c)
            return carry

        lax.fori_loop(0, n_reg // 8, quarter, 0)
        for inside, copy in halo_copies(s):
            pl.when(inside)(copy.start)

    def broad(c, at):
        return jnp.where(
            left,
            jnp.broadcast_to(c[:, :, at : at + 1], c.shape),
            jnp.broadcast_to(c[:, :, at + MEMS : at + MEMS + 1], c.shape),
        )

    def forecast(s):
        wait_bytes(from_east.at[s], halo_in_sem.at[0, s])
        wait_bytes(from_west.at[s], halo_in_sem.at[1, s])

        def rim(i, carry):
            at, to = pl.ds(i * 8, 8), pl.ds(i * 8 + 1, 8)
            e, w = from_east[s, at], from_west[s, at]
            p, q = jnp.where(low, e, w), up(jnp.where(low, w, e))
            h, u, v = in_box[s, at, 0], in_box[s, at, 1], in_box[s, at, 2]
            window[0, to, 0:8] = h
            window[1, to, 0:8] = u
            window[2, to, 0:8] = v
            window[0, to, 8:16] = across(jnp.where(crossed, h, p))
            window[1, to, 8:16] = jnp.where(crossed, p, across(u))
            window[2, to, 8:16] = across(jnp.where(crossed, v, q))
            if s == 0:
                c = c_in[at]
                cour_u[to, 0:8] = broad(c, 0)
                cour_v[to, 0:8] = broad(c, 32)
                c = jnp.where(crossed, q, across(c))
                cour_u[to, 8:16] = broad(c, 0)
                cour_v[to, 8:16] = broad(c, 32)
            return carry

        lax.fori_loop(0, n_reg // 8, rim, 0)

        def heights(i, carry):
            at = pl.ds(i * 8 + 1, 8)
            flux_u = cour_u[at] * window[1, at]
            flux_v = cour_v[pl.ds(i * 8, 9)] * window[2, pl.ds(i * 8, 9)]
            gain = flux_u - pltpu.roll(flux_u, 1, axis=1) + flux_v[1:] - flux_v[:-1]
            window[0, at] = window[0, at] - gain
            return carry

        def currents(i, carry):
            at = pl.ds(i * 8 + 1, 8)
            h = window[0, pl.ds(i * 8 + 1, 9)]
            window[1, at] = window[1, at] - (pltpu.roll(h[:-1], 15, axis=1) - h[:-1])
            window[2, at] = window[2, at] - (h[1:] - h[:-1])
            return carry

        def one_step(i, carry):
            lax.fori_loop(0, n_reg // 8, heights, 0, unroll=True)
            lax.fori_loop(0, n_reg // 8, currents, 0, unroll=True)
            return carry

        lax.fori_loop(0, STEPS, one_step, 0)
        tile = slice(s // 2 * LANES, (s // 2 + 1) * LANES)
        keep = left if s % 2 else ~left

        def place_cells(i, carry):
            at = pl.ds(i * 8, 8)
            for var in range(3):
                x = window[var, pl.ds(i * 8 + 1, 8), 0:8]
                y = across(x)
                x, y = (y, x) if s % 2 else (x, y)
                state[var, at, 0:8, tile] = jnp.where(keep, state[var, at, 0:8, tile], x)
                state[var, at, 8:16, tile] = jnp.where(keep, state[var, at, 8:16, tile], y)
            return carry

        lax.fori_loop(0, n_reg // 8, place_cells, 0)

    blank = jnp.zeros((16, LANES), jnp.float32)
    window[0, n_reg + 1] = blank
    window[2, 0] = blank
    cour_v[0] = blank

    for s in order[:-1]:
        send_rim(s)
    forecast(order[0])
    send_rim(order[-1])
    for s in order[1:]:
        forecast(s)

    row_i = lax.broadcasted_iota(jnp.int32, (members, members), 0)
    col_i = lax.broadcasted_iota(jnp.int32, (members, members), 1)
    eye = jnp.where(row_i == col_i, 1.0, 0.0).astype(jnp.float32)
    obs_i = lax.broadcasted_iota(jnp.int32, (1, obs), 1)

    for turn in range(2):
        q = lax.rem(a + b + turn, 2)
        spreads, means = [], []
        obs_spread = jnp.zeros((members, obs), jnp.float32)
        mean_obs = jnp.zeros((1, obs), jnp.float32)
        for var in range(3):
            x = state[var, pl.ds(q * half_rows, half_rows)].reshape(cells, members)
            mean = jnp.sum(x, axis=1, keepdims=True) / members
            spread = split(x - mean)
            block = slice(var * cells, (var + 1) * cells)
            weights = (stencil_hi[q, block, :], stencil_lo[q, block, :])
            obs_spread += dot3(spread, weights, ((0,), (0,)))
            mean_obs += jnp.sum(stencil[q, block, :] * mean, axis=0, keepdims=True)
            spreads.append(spread)
            means.append(mean)
        active = jnp.where(obs_i < cnt_ref[q], 1.0, 0.0)
        weighted = obs_spread * (active / var_ref[pl.ds(q, 1), :])
        gram_sum = dot3(split(weighted), split(obs_spread), ((1,), (1,)))
        scaled = eye + gram_sum / (members - 1)
        fro = jnp.sqrt(all_sum(scaled * scaled))
        innovation = jnp.sum(weighted * (val_ref[pl.ds(q, 1), :] - mean_obs), axis=1, keepdims=True)
        iterate = scaled / fro
        factor = split(1.5 * eye - 0.5 * iterate)

        def sweep(i, carry):
            iterate, root = carry
            factor = split(1.5 * eye - 0.5 * dot3(root, iterate))
            return split(dot3(iterate, factor)), split(dot3(factor, root))

        iterate, root = lax.fori_loop(
            1, NEWTON - 1, sweep, (split(dot3(split(iterate), factor)), factor)
        )
        factor = split(1.5 * eye - 0.5 * dot3(root, iterate))
        transform = dot3(factor, root) / jnp.sqrt(fro)
        halfway = jnp.sum(transform * innovation, axis=0, keepdims=True)
        mean_weights = jnp.sum(transform * halfway, axis=1, keepdims=True) / (members - 1)
        both = split(jnp.concatenate(
            [transform + mean_weights, jnp.broadcast_to(mean_weights, (members, LANES))], axis=1
        ))
        for var in range(3):
            moved = dot3(spreads[var], both)
            ana[var, :, 0:members] = moved[:, 0:members] + means[var]
            ana[var, :, members:] = moved[:, members:]

        def unload(i, carry):
            i = lax.rem(b + i, half_rows)
            lo = pl.multiple_of(i * COLS, 8)
            hi = pl.multiple_of(i * COLS + 8, 8)
            row = q * half_rows + i
            for t in range(lane_tiles):
                at = slice(t * LANES, (t + 1) * LANES)
                for var in range(3):
                    x, y = ana[var, pl.ds(lo, 8), at], ana[var, pl.ds(hi, 8), at]
                    back_out[2 * t, row, var] = jnp.where(left, x, across(y))
                    back_out[2 * t + 1, row, var] = jnp.where(left, across(x), y)
            packed = jnp.zeros((8, LANES), jnp.float32)
            for var in range(3):
                x = ana[var, pl.ds(lo, 8), members:]
                y = ana[var, pl.ds(hi, 8), members:]
                packed = jnp.where(lax.div(lax.rem(lane, MEMS), 16) == var, jnp.where(left, x, y), packed)
            inc_out[row] = packed
            if turn == 0:
                send_inc(row)
                for s in order:
                    send_back(s, row)
            return carry

        def send_inc(row):
            go = pltpu.make_async_remote_copy(
                src_ref=inc_out.at[row], dst_ref=inc_in.at[b], send_sem=inc_out_sem,
                recv_sem=inc_in_sem, device_id=(a, row, f), device_id_type=MESH,
            )
            pl.when(row != b)(go.start)

        def send_back(s, row):
            slot = (n_mem - s) % n_mem
            go = pltpu.make_async_remote_copy(
                src_ref=back_out.at[s, row], dst_ref=back_in.at[slot, b],
                send_sem=back_out_sem, recv_sem=back_in_sem.at[slot],
                device_id=(lax.rem(a + s, n_mem), row, f), device_id_type=MESH,
            )
            if s:
                go.start()
            else:
                pl.when(row != b)(go.start)

        lax.fori_loop(0, half_rows, unload, 0)
        if turn:
            for phase in phases:

                def send_phase(i, carry):
                    row = q * half_rows + lax.rem(b + i, half_rows)
                    if phase == phases[0]:
                        send_inc(row)
                    for s in phase:
                        send_back(s, row)
                    return carry

                lax.fori_loop(0, half_rows, send_phase, 0)

    inc_in[b] = inc_out[b]
    back_in[0, b] = back_out[0, b]
    wait_bytes(inc_in.at[pl.ds(0, n_reg - 1)], inc_in_sem)

    def straight(blocks):
        return jnp.stack([blocks, pltpu.roll(blocks, MEMS, axis=2)], axis=1).reshape(LANES, LANES).T

    fine_i = lax.broadcasted_iota(jnp.int32, (LANES, 2 * LANES), 1)
    coarse_i = lax.broadcasted_iota(jnp.int32, (LANES, 2 * LANES), 0)
    widen = jnp.where(lax.div(fine_i, 2) == coarse_i, 1.0, 0.0).astype(jnp.float32)
    for j in range(own_tiles):
        wide = dot(straight(inc_in[8 * j : 8 * j + 8])[0:64], widen, precision=HIGHEST)
        for var in range(3):
            for e in range(2):
                for k in range(2):
                    at = (2 * var + e) * 2 * own_tiles + 2 * j + k
                    part = wide[16 * var : 16 * var + 1, k * LANES : (k + 1) * LANES]
                    fo_ref[at : at + 1, :] = fc_ref[at : at + 1, :] + part

    for s in order:
        wait_bytes(back_in.at[s, pl.ds(0, n_reg - 1 if s == 0 else n_reg)], back_in_sem.at[s])
        first = lax.rem(a + s, n_mem) * own_tiles

        def unpack(j, carry):
            for var in range(3):
                x = back_in[s, pl.ds(pl.multiple_of(j * 16, 8), 8), var]
                y = back_in[s, pl.ds(pl.multiple_of(j * 16 + 8, 8), 8), var]
                rows = [jnp.where(left, x, across(y)), jnp.where(left, across(x), y)]
                t = jnp.stack(rows, axis=1).reshape(LANES, LANES).T
                for k in range(2):
                    at = pl.ds(first + 2 * j + k, MEMS, stride=tiles)
                    ana_ref[var, at, :] = t[k * MEMS : (k + 1) * MEMS]
            return carry

        lax.fori_loop(0, own_tiles // 2, unpack, 0)

    wait_bytes(c_out.at[pl.ds(0, n_reg - 1)], c_out_sem)
    wait_bytes(out_box.at[pl.ds(0, peers - 1)], out_sem)
    wait_bytes(inc_out.at[pl.ds(0, n_reg - 1)], inc_out_sem)
    wait_bytes(out_box.at[pl.ds(0, peers - 1)], back_out_sem)
    for s in order:
        for inside, copy in halo_copies(s):
            pl.when(inside)(copy.wait_send)

    own_edge = (b == plane - 1) | (b == plane)
    own_edge |= ((b == n_reg - 1) & (a != n_mem - 1)) | ((b == 0) & (a != 0))

    @pl.when(own_edge)
    def _():
        wait_bytes(c_out.at[pl.ds(0, 4 * n_mem - 1)], edge_sem)

    @pl.when(jnp.logical_not(own_edge))
    def _():
        wait_bytes(c_out.at[pl.ds(0, 4 * n_mem)], edge_sem)


def step(n_mem, n_reg, h, u, v, cu, cv, obs_index, obs_weight, obs_value, obs_var, obs_count, fine):
    peers = n_mem * n_reg
    members = n_mem * MEMS
    tiles = peers * COLS // LANES
    obs = obs_value.shape[1]
    cells = n_reg // 2 * COLS
    f32 = jnp.float32
    flat = (MEMS * tiles, LANES)
    flat_fine = (fine.size // LANES, LANES)
    vmem = pl.BlockSpec(memory_space=pltpu.VMEM)
    dma = pltpu.SemaphoreType.DMA
    outs = pl.pallas_call(
        functools.partial(kernel, (n_mem, n_reg)),
        out_shape=[
            jax.ShapeDtypeStruct((3, *flat), f32), jax.ShapeDtypeStruct(flat_fine, f32),
        ],
        in_specs=[pl.BlockSpec(memory_space=pl.ANY)] * 11,
        out_specs=[vmem] * 2,
        scratch_shapes=[
            pltpu.VMEM((peers, 3, 8, LANES), f32),
            pltpu.VMEM((n_mem, n_reg, 3, 8, LANES), f32),
            pltpu.VMEM((n_reg, 8, LANES), f32),
            pltpu.VMEM((n_reg, 8, LANES), f32),
            pltpu.VMEM((n_mem, n_reg, 8, LANES), f32),
            pltpu.VMEM((n_mem, n_reg, 8, LANES), f32),
            pltpu.VMEM((n_mem, n_reg, 8, LANES), f32),
            pltpu.VMEM((n_mem, n_reg, 8, LANES), f32),
            pltpu.VMEM((3, n_reg + 2, 16, LANES), f32),
            pltpu.VMEM((n_reg + 2, 16, LANES), f32),
            pltpu.VMEM((n_reg + 2, 16, LANES), f32),
            pltpu.VMEM((3, n_reg, 16, members), f32),
            pltpu.VMEM((2, 3 * cells, obs), f32),
            pltpu.VMEM((2, 3 * cells, obs), jnp.bfloat16),
            pltpu.VMEM((2, 3 * cells, obs), jnp.bfloat16),
            pltpu.VMEM((3, cells, members + LANES), f32),
            pltpu.VMEM((n_mem, n_reg, 3, 8, LANES), f32),
            pltpu.VMEM((n_mem, n_reg, 3, 8, LANES), f32),
            pltpu.VMEM((n_reg, 8, LANES), f32),
            pltpu.VMEM((n_reg, 8, LANES), f32),
            pltpu.VMEM(flat, f32), pltpu.VMEM(flat, f32), pltpu.VMEM(flat, f32),
            pltpu.VMEM((2, 8, LANES), f32),
            pltpu.VMEM((n_mem, 4, 8, LANES), f32),
            pltpu.VMEM((tiles, LANES), f32), pltpu.VMEM((tiles, LANES), f32),
            pltpu.VMEM((2, 4, obs), jnp.int32), pltpu.VMEM((2, 4, obs), f32),
            pltpu.VMEM((2, obs), f32), pltpu.VMEM((2, obs), f32),
            pltpu.SMEM((2,), jnp.int32), pltpu.VMEM(flat_fine, f32),
            dma, dma((n_mem,)), dma, dma, dma((2, n_mem)), dma((2, n_mem)),
            dma, dma((n_mem,)), dma, dma, dma((11,)), dma,
        ],
        compiler_params=pltpu.CompilerParams(
            collective_id=0, has_side_effects=True, vmem_limit_bytes=56 * 1024 * 1024
        ),
    )(
        h.reshape(flat), u.reshape(flat), v.reshape(flat),
        cu.reshape(tiles, LANES), cv.reshape(tiles, LANES),
        obs_index.transpose(0, 2, 1), obs_weight.transpose(0, 2, 1),
        obs_value, obs_var, obs_count, fine.reshape(flat_fine),
    )
    return tuple(outs[0][var].reshape(h.shape) for var in range(3)) + (outs[1].reshape(fine.shape),)


def solution(mesh):
    fields = P("member", "region", "fine")
    regions = ("member", "region", "fine")
    fine = P(None, "region", "fine", "member")
    return jax.shard_map(
        functools.partial(step, mesh.shape["member"], mesh.shape["region"]),
        mesh=mesh,
        in_specs=(
            fields, fields, fields,
            P("region", "fine"), P("region", "fine"),
            P(regions, None, None), P(regions, None, None),
            P(regions, None), P(regions, None), P(regions),
            fine,
        ),
        out_specs=(fields, fields, fields, fine),
        check_vma=False,
    )
```

```python
import functools

import jax
import jax.numpy as jnp
from jax import lax
from jax.experimental import pallas as pl
from jax.experimental.pallas import tpu as pltpu
from jax.sharding import PartitionSpec as P

MESH = pl.DeviceIdType.MESH
STEPS = 4
NEWTON = 8
HIGHEST = lax.Precision.HIGHEST
LANES = 128
MEMS = 64
COLS = 16


ROWS_COLS = ((1,), (0,))


def dot(x, y, contract=ROWS_COLS, precision=None):
    return lax.dot_general(
        x, y, (contract, ((), ())), precision=precision, preferred_element_type=jnp.float32
    )


def split(x):
    high = x.astype(jnp.bfloat16)
    return high, (x - high.astype(jnp.float32)).astype(jnp.bfloat16)


def dot3(x, y, contract=ROWS_COLS):
    rows = 1 - contract[0][0]
    size = x[0].shape[rows]
    both = dot(jnp.concatenate(x, axis=rows), y[0], contract)
    return both[:size] + (both[size:] + dot(x[0], y[1], contract))


def all_sum(x):
    return jnp.sum(jnp.sum(x, axis=1, keepdims=True), axis=0, keepdims=True)


def kernel(
    dims,
    h_src, u_src, v_src, cu_src, cv_src, idx_src, wt_src, val_src, var_src, cnt_src, fc_src,
    ana_ref, fo_ref,
    out_box, in_box, c_out, c_in, to_west, to_east, from_east, from_west,
    window, cour_u, cour_v, state, stencil, stencil_hi, stencil_lo, ana,
    back_out, back_in, inc_out, inc_in, h_in, u_in, v_in, c_edge, edges,
    cu_ref, cv_ref, idx_ref, wt_ref, val_ref, var_ref, cnt_ref, fc_ref,
    out_sem, in_sem, c_out_sem, c_in_sem, halo_out_sem, halo_in_sem,
    back_out_sem, back_in_sem, inc_out_sem, inc_in_sem, load_sem, edge_sem,
):
    n_mem, n_reg = dims
    peers = n_mem * n_reg
    tiles = peers * COLS // LANES
    lane_tiles = n_mem * MEMS // LANES
    members = n_mem * MEMS
    half_rows = n_reg // 2
    cells = half_rows * COLS
    own_tiles = n_reg * COLS // LANES
    plane = n_reg // 2
    phases = [[0], [1, 3], [2]] if n_mem == 4 else [[s] for s in range(n_mem)]
    order = [s for phase in phases for s in phase]
    a = lax.axis_index("member")
    b = lax.axis_index("region")
    f = lax.axis_index("fine")
    me = a * n_reg + b

    def place(p):
        return (lax.div(p, n_reg), lax.rem(p, n_reg), f)

    loads = [
        pltpu.make_async_copy(ref, box, load_sem.at[i])
        for i, (ref, box) in enumerate((
            (h_src, h_in), (u_src, u_in), (v_src, v_in), (cu_src, cu_ref), (cv_src, cv_ref),
            (idx_src, idx_ref), (wt_src, wt_ref), (val_src, val_ref), (var_src, var_ref),
            (cnt_src, cnt_ref), (fc_src, fc_ref),
        ))
    ]
    for load in loads:
        load.start()

    barrier = pltpu.get_barrier_semaphore()

    def greet(i, carry):
        pl.semaphore_signal(
            barrier, inc=1, device_id=place(lax.rem(me + i, peers)), device_id_type=MESH
        )
        return carry

    def greet_other_half(i, carry):
        p_mem, p_row, _ = place(i)
        pl.semaphore_signal(barrier, inc=1, device_id=(p_mem, p_row, 1 - f), device_id_type=MESH)
        return carry

    @pl.when((me == 0) | (me == peers - 1))
    def _():
        lax.fori_loop(0, peers, greet_other_half, 0)

    lax.fori_loop(1, peers, greet, 0)
    for load in loads[:3]:
        load.wait()

    lane = lax.broadcasted_iota(jnp.int32, (8, LANES), 1)
    left = lane < MEMS
    low = lax.broadcasted_iota(jnp.int32, (8, LANES), 0) < 4
    crossed = (low & ~left) | (~low & left)

    def across(x):
        return pltpu.roll(x, MEMS, axis=x.ndim - 1)

    def up(x):
        return pltpu.roll(x, 4, axis=x.ndim - 2)

    def turned(block):
        pair = jnp.concatenate([block, pltpu.roll(block, LANES - 8, axis=1)], axis=0)
        return pair.T

    def pack(j, carry):
        for var, ref in enumerate((h_in, u_in, v_in)):
            pair = [ref[pl.ds(2 * j + k, MEMS, stride=tiles), :] for k in range(2)]
            t = jnp.concatenate(pair, axis=0).T
            for k in range(8):
                x, y = t[COLS * k : COLS * k + 8], t[COLS * k + 8 : COLS * k + 16]
                out_box[16 * j + k, var] = jnp.where(left, x, across(y))
                out_box[16 * j + 8 + k, var] = jnp.where(left, across(x), y)
        return carry

    lax.fori_loop(0, tiles // 2, pack, 0)

    def courant(j):
        cu = jnp.broadcast_to(cu_ref[pl.ds(j, 1), :], (32, LANES))
        cv = jnp.broadcast_to(cv_ref[pl.ds(j, 1), :], (32, LANES))
        return turned(jnp.concatenate([cu, cv], axis=0))

    def west_going(h, u, v, c):
        c, u = across(c), across(u)
        return jnp.where(low, jnp.where(left, h, u), up(jnp.where(left, v, c)))

    def east_going(h, u, v, c):
        c, u = across(c), across(u)
        return jnp.where(low, up(jnp.where(left, c, v)), jnp.where(left, u, h))

    pl.semaphore_wait(barrier, peers + 1)

    def send_rest():
        for load in loads[3:]:
            load.wait()
        for j in range(own_tiles):
            t = courant(a * own_tiles + j)
            for k in range(8):
                c_out[j * 8 + k] = t[COLS * k : COLS * k + 8]

        c_edge[0] = courant(lax.rem(a + 1, n_mem) * own_tiles)[0:8]
        c_edge[1] = courant(lax.rem(a * own_tiles + tiles - 1, tiles))[7 * COLS : 7 * COLS + 8]
        for k in range(n_mem):
            for kind, (m, c, going) in enumerate((
                (k * n_reg + plane, c_out[plane], west_going),
                ((k + 1) % n_mem * n_reg, c_edge[0], west_going),
                (k * n_reg + plane - 1, c_out[plane - 1], east_going),
                ((k * n_reg + peers - 1) % peers, c_edge[1], east_going),
            )):
                edges[k, kind] = going(out_box[m, 0], out_box[m, 1], out_box[m, 2], c)

        def send_courant(i, carry):
            p = lax.rem(b + i, n_reg)
            pltpu.make_async_remote_copy(
                src_ref=c_out.at[p], dst_ref=c_in.at[b], send_sem=c_out_sem, recv_sem=c_in_sem,
                device_id=(a, p, f), device_id_type=MESH,
            ).start()
            return carry

        lax.fori_loop(1, n_reg, send_courant, 0)
        c_in[b] = c_out[b]
        for s in order:
            p_mem = lax.rem(a + s, n_mem)
            slot = (n_mem - s) % n_mem
            for kind, (p_row, box, other) in enumerate((
                (plane - 1, from_east, None),
                (n_reg - 1, from_east, n_mem - 1),
                (plane, from_west, None),
                (0, from_west, 0),
            )):
                here = f if other is None else jnp.where(p_mem == other, 1 - f, f)
                sem = halo_in_sem.at[kind // 2, slot]
                go = pltpu.make_async_remote_copy(
                    src_ref=edges.at[p_mem, kind], dst_ref=box.at[slot, b],
                    send_sem=edge_sem, recv_sem=sem,
                    device_id=(p_mem, p_row, here), device_id_type=MESH,
                )
                if s:
                    go.start()
                else:
                    own = (b == p_row) if other is None else (b == p_row) & (a != other)
                    stay = pltpu.make_async_copy(edges.at[p_mem, kind], box.at[slot, b], sem)
                    pl.when(own)(stay.start)
                    pl.when(jnp.logical_not(own))(go.start)

    in_box[0, b] = out_box[me]

    for phase in phases:
        if phase == phases[-1]:
            send_rest()

        def send_state(i, carry):
            p_row = lax.rem(b + i, n_reg)
            for s in phase:
                p_mem = lax.rem(a + s, n_mem)
                slot = (n_mem - s) % n_mem
                pltpu.make_async_remote_copy(
                    src_ref=out_box.at[p_mem * n_reg + p_row], dst_ref=in_box.at[slot, b],
                    send_sem=out_sem, recv_sem=in_sem.at[slot],
                    device_id=(p_mem, p_row, f), device_id_type=MESH,
                ).start()
            return carry

        lax.fori_loop(1 if phase == [0] else 0, n_reg, send_state, 0)
    obs = idx_ref.shape[2]
    for q in range(2):

        def spread_weights(g, carry):
            start = pl.multiple_of(g * 16, 16)
            cell = lax.broadcasted_iota(jnp.int32, (16, obs), 0) + g * 16
            total = jnp.zeros((16, obs), jnp.float32)
            for j in range(4):
                total += jnp.where(idx_ref[q, j : j + 1, :] == cell, wt_ref[q, j : j + 1, :], 0.0)
            high, rest = split(total)
            stencil[q, pl.ds(start, 16), :] = total
            stencil_hi[q, pl.ds(start, 16), :] = high
            stencil_lo[q, pl.ds(start, 16), :] = rest
            return carry

        lax.fori_loop(0, 3 * cells // 16, spread_weights, 0)

    def wait_bytes(ref, sem):
        pltpu.make_async_copy(ref, ref, sem).wait()

    wait_bytes(c_in.at[pl.ds(0, n_reg - 1)], c_in_sem)

    inside_west = lax.rem(b, plane) != 0
    inside_east = lax.rem(b, plane) != plane - 1

    def halo_copies(s):
        go_west = pltpu.make_async_remote_copy(
            src_ref=to_west.at[s], dst_ref=from_east.at[s],
            send_sem=halo_out_sem.at[0, s], recv_sem=halo_in_sem.at[0, s],
            device_id=(a, lax.rem(b + n_reg - 1, n_reg), f), device_id_type=MESH,
        )
        go_east = pltpu.make_async_remote_copy(
            src_ref=to_east.at[s], dst_ref=from_west.at[s],
            send_sem=halo_out_sem.at[1, s], recv_sem=halo_in_sem.at[1, s],
            device_id=(a, lax.rem(b + 1, n_reg), f), device_id_type=MESH,
        )
        return (inside_west, go_west), (inside_east, go_east)

    def send_rim(s):
        wait_bytes(in_box.at[s, pl.ds(0, n_reg - 1 if s == 0 else n_reg)], in_sem.at[s])

        def quarter(i, carry):
            at = pl.ds(i * 8, 8)
            h, u, v = in_box[s, at, 0], in_box[s, at, 1], in_box[s, at, 2]
            c = c_in[at]
            to_west[s, at] = west_going(h, u, v, c)
            to_east[s, at] = east_going(h, u, v, c)
            return carry

        lax.fori_loop(0, n_reg // 8, quarter, 0)
        for inside, copy in halo_copies(s):
            pl.when(inside)(copy.start)

    def broad(c, at):
        return jnp.where(
            left,
            jnp.broadcast_to(c[:, :, at : at + 1], c.shape),
            jnp.broadcast_to(c[:, :, at + MEMS : at + MEMS + 1], c.shape),
        )

    def forecast(s):
        wait_bytes(from_east.at[s], halo_in_sem.at[0, s])
        wait_bytes(from_west.at[s], halo_in_sem.at[1, s])

        def rim(i, carry):
            at, to = pl.ds(i * 8, 8), pl.ds(i * 8 + 1, 8)
            e, w = from_east[s, at], from_west[s, at]
            p, q = jnp.where(low, e, w), up(jnp.where(low, w, e))
            h, u, v = in_box[s, at, 0], in_box[s, at, 1], in_box[s, at, 2]
            window[0, to, 0:8] = h
            window[1, to, 0:8] = u
            window[2, to, 0:8] = v
            window[0, to, 8:16] = across(jnp.where(crossed, h, p))
            window[1, to, 8:16] = jnp.where(crossed, p, across(u))
            window[2, to, 8:16] = across(jnp.where(crossed, v, q))
            if s == 0:
                c = c_in[at]
                cour_u[to, 0:8] = broad(c, 0)
                cour_v[to, 0:8] = broad(c, 32)
                c = jnp.where(crossed, q, across(c))
                cour_u[to, 8:16] = broad(c, 0)
                cour_v[to, 8:16] = broad(c, 32)
            return carry

        lax.fori_loop(0, n_reg // 8, rim, 0)

        def heights(i, carry):
            at = pl.ds(i * 8 + 1, 8)
            flux_u = cour_u[at] * window[1, at]
            flux_v = cour_v[pl.ds(i * 8, 9)] * window[2, pl.ds(i * 8, 9)]
            gain = flux_u - pltpu.roll(flux_u, 1, axis=1) + flux_v[1:] - flux_v[:-1]
            window[0, at] = window[0, at] - gain
            return carry

        def currents(i, carry):
            at = pl.ds(i * 8 + 1, 8)
            h = window[0, pl.ds(i * 8 + 1, 9)]
            window[1, at] = window[1, at] - (pltpu.roll(h[:-1], 15, axis=1) - h[:-1])
            window[2, at] = window[2, at] - (h[1:] - h[:-1])
            return carry

        def one_step(i, carry):
            lax.fori_loop(0, n_reg // 8, heights, 0, unroll=True)
            lax.fori_loop(0, n_reg // 8, currents, 0, unroll=True)
            return carry

        lax.fori_loop(0, STEPS, one_step, 0)
        tile = slice(s // 2 * LANES, (s // 2 + 1) * LANES)
        keep = left if s % 2 else ~left

        def place_cells(i, carry):
            at = pl.ds(i * 8, 8)
            for var in range(3):
                x = window[var, pl.ds(i * 8 + 1, 8), 0:8]
                y = across(x)
                x, y = (y, x) if s % 2 else (x, y)
                state[var, at, 0:8, tile] = jnp.where(keep, state[var, at, 0:8, tile], x)
                state[var, at, 8:16, tile] = jnp.where(keep, state[var, at, 8:16, tile], y)
            return carry

        lax.fori_loop(0, n_reg // 8, place_cells, 0)

    blank = jnp.zeros((16, LANES), jnp.float32)
    window[0, n_reg + 1] = blank
    window[2, 0] = blank
    cour_v[0] = blank

    for s in order[:-1]:
        send_rim(s)
    forecast(order[0])
    send_rim(order[-1])
    for s in order[1:]:
        forecast(s)

    row_i = lax.broadcasted_iota(jnp.int32, (members, members), 0)
    col_i = lax.broadcasted_iota(jnp.int32, (members, members), 1)
    eye = jnp.where(row_i == col_i, 1.0, 0.0).astype(jnp.float32)
    obs_i = lax.broadcasted_iota(jnp.int32, (1, obs), 1)

    for turn in range(2):
        q = lax.rem(a + b + turn, 2)
        spreads, means = [], []
        obs_spread = jnp.zeros((members, obs), jnp.float32)
        mean_obs = jnp.zeros((1, obs), jnp.float32)
        for var in range(3):
            x = state[var, pl.ds(q * half_rows, half_rows)].reshape(cells, members)
            mean = jnp.sum(x, axis=1, keepdims=True) / members
            spread = split(x - mean)
            block = slice(var * cells, (var + 1) * cells)
            weights = (stencil_hi[q, block, :], stencil_lo[q, block, :])
            obs_spread += dot3(spread, weights, ((0,), (0,)))
            mean_obs += jnp.sum(stencil[q, block, :] * mean, axis=0, keepdims=True)
            spreads.append(spread)
            means.append(mean)
        active = jnp.where(obs_i < cnt_ref[q], 1.0, 0.0)
        weighted = obs_spread * (active / var_ref[pl.ds(q, 1), :])
        gram_sum = dot3(split(weighted), split(obs_spread), ((1,), (1,)))
        scaled = eye + gram_sum / (members - 1)
        fro = jnp.sqrt(all_sum(scaled * scaled))
        innovation = jnp.sum(weighted * (val_ref[pl.ds(q, 1), :] - mean_obs), axis=1, keepdims=True)
        iterate = scaled / fro
        factor = split(1.5 * eye - 0.5 * iterate)

        def sweep(i, carry):
            iterate, root = carry
            factor = split(1.5 * eye - 0.5 * dot3(root, iterate))
            return split(dot3(iterate, factor)), split(dot3(factor, root))

        iterate, root = lax.fori_loop(
            1, NEWTON - 1, sweep, (split(dot3(split(iterate), factor)), factor)
        )
        factor = split(1.5 * eye - 0.5 * dot3(root, iterate))
        transform = dot3(factor, root) / jnp.sqrt(fro)
        halfway = jnp.sum(transform * innovation, axis=0, keepdims=True)
        mean_weights = jnp.sum(transform * halfway, axis=1, keepdims=True) / (members - 1)
        both = split(jnp.concatenate(
            [transform + mean_weights, jnp.broadcast_to(mean_weights, (members, LANES))], axis=1
        ))
        for var in range(3):
            moved = dot3(spreads[var], both)
            ana[var, :, 0:members] = moved[:, 0:members] + means[var]
            ana[var, :, members:] = moved[:, members:]

        def unload(i, carry):
            i = lax.rem(b + i, half_rows)
            lo = pl.multiple_of(i * COLS, 8)
            hi = pl.multiple_of(i * COLS + 8, 8)
            row = q * half_rows + i
            for t in range(lane_tiles):
                at = slice(t * LANES, (t + 1) * LANES)
                for var in range(3):
                    x, y = ana[var, pl.ds(lo, 8), at], ana[var, pl.ds(hi, 8), at]
                    back_out[2 * t, row, var] = jnp.where(left, x, across(y))
                    back_out[2 * t + 1, row, var] = jnp.where(left, across(x), y)
            packed = jnp.zeros((8, LANES), jnp.float32)
            for var in range(3):
                x = ana[var, pl.ds(lo, 8), members:]
                y = ana[var, pl.ds(hi, 8), members:]
                packed = jnp.where(lax.div(lax.rem(lane, MEMS), 16) == var, jnp.where(left, x, y), packed)
            inc_out[row] = packed
            if turn == 0:
                send_inc(row)
                for s in order:
                    send_back(s, row)
            return carry

        def send_inc(row):
            go = pltpu.make_async_remote_copy(
                src_ref=inc_out.at[row], dst_ref=inc_in.at[b], send_sem=inc_out_sem,
                recv_sem=inc_in_sem, device_id=(a, row, f), device_id_type=MESH,
            )
            pl.when(row != b)(go.start)

        def send_back(s, row):
            slot = (n_mem - s) % n_mem
            go = pltpu.make_async_remote_copy(
                src_ref=back_out.at[s, row], dst_ref=back_in.at[slot, b],
                send_sem=back_out_sem, recv_sem=back_in_sem.at[slot],
                device_id=(lax.rem(a + s, n_mem), row, f), device_id_type=MESH,
            )
            if s:
                go.start()
            else:
                pl.when(row != b)(go.start)

        lax.fori_loop(0, half_rows, unload, 0)
        if turn:
            for phase in phases[::-1]:

                def send_phase(i, carry):
                    row = q * half_rows + lax.rem(b + i, half_rows)
                    if phase == phases[-1]:
                        send_inc(row)
                    for s in phase:
                        send_back(s, row)
                    return carry

                lax.fori_loop(0, half_rows, send_phase, 0)

    inc_in[b] = inc_out[b]
    back_in[0, b] = back_out[0, b]
    wait_bytes(inc_in.at[pl.ds(0, n_reg - 1)], inc_in_sem)

    def straight(blocks):
        return jnp.stack([blocks, pltpu.roll(blocks, MEMS, axis=2)], axis=1).reshape(LANES, LANES).T

    fine_i = lax.broadcasted_iota(jnp.int32, (LANES, 2 * LANES), 1)
    coarse_i = lax.broadcasted_iota(jnp.int32, (LANES, 2 * LANES), 0)
    widen = jnp.where(lax.div(fine_i, 2) == coarse_i, 1.0, 0.0).astype(jnp.float32)
    for j in range(own_tiles):
        wide = dot(straight(inc_in[8 * j : 8 * j + 8])[0:64], widen, precision=HIGHEST)
        for var in range(3):
            for e in range(2):
                for k in range(2):
                    at = (2 * var + e) * 2 * own_tiles + 2 * j + k
                    part = wide[16 * var : 16 * var + 1, k * LANES : (k + 1) * LANES]
                    fo_ref[at : at + 1, :] = fc_ref[at : at + 1, :] + part

    for s in order[::-1]:
        wait_bytes(back_in.at[s, pl.ds(0, n_reg - 1 if s == 0 else n_reg)], back_in_sem.at[s])
        first = lax.rem(a + s, n_mem) * own_tiles

        def unpack(j, carry):
            for var in range(3):
                x = back_in[s, pl.ds(pl.multiple_of(j * 16, 8), 8), var]
                y = back_in[s, pl.ds(pl.multiple_of(j * 16 + 8, 8), 8), var]
                rows = [jnp.where(left, x, across(y)), jnp.where(left, across(x), y)]
                t = jnp.stack(rows, axis=1).reshape(LANES, LANES).T
                for k in range(2):
                    at = pl.ds(first + 2 * j + k, MEMS, stride=tiles)
                    ana_ref[var, at, :] = t[k * MEMS : (k + 1) * MEMS]
            return carry

        lax.fori_loop(0, own_tiles // 2, unpack, 0)

    wait_bytes(c_out.at[pl.ds(0, n_reg - 1)], c_out_sem)
    wait_bytes(out_box.at[pl.ds(0, peers - 1)], out_sem)
    wait_bytes(inc_out.at[pl.ds(0, n_reg - 1)], inc_out_sem)
    wait_bytes(out_box.at[pl.ds(0, peers - 1)], back_out_sem)
    for s in order:
        for inside, copy in halo_copies(s):
            pl.when(inside)(copy.wait_send)

    own_edge = (b == plane - 1) | (b == plane)
    own_edge |= ((b == n_reg - 1) & (a != n_mem - 1)) | ((b == 0) & (a != 0))

    @pl.when(own_edge)
    def _():
        wait_bytes(c_out.at[pl.ds(0, 4 * n_mem - 1)], edge_sem)

    @pl.when(jnp.logical_not(own_edge))
    def _():
        wait_bytes(c_out.at[pl.ds(0, 4 * n_mem)], edge_sem)


def step(n_mem, n_reg, h, u, v, cu, cv, obs_index, obs_weight, obs_value, obs_var, obs_count, fine):
    peers = n_mem * n_reg
    members = n_mem * MEMS
    tiles = peers * COLS // LANES
    obs = obs_value.shape[1]
    cells = n_reg // 2 * COLS
    f32 = jnp.float32
    flat = (MEMS * tiles, LANES)
    flat_fine = (fine.size // LANES, LANES)
    vmem = pl.BlockSpec(memory_space=pltpu.VMEM)
    dma = pltpu.SemaphoreType.DMA
    outs = pl.pallas_call(
        functools.partial(kernel, (n_mem, n_reg)),
        out_shape=[
            jax.ShapeDtypeStruct((3, *flat), f32), jax.ShapeDtypeStruct(flat_fine, f32),
        ],
        in_specs=[pl.BlockSpec(memory_space=pl.ANY)] * 11,
        out_specs=[vmem] * 2,
        scratch_shapes=[
            pltpu.VMEM((peers, 3, 8, LANES), f32),
            pltpu.VMEM((n_mem, n_reg, 3, 8, LANES), f32),
            pltpu.VMEM((n_reg, 8, LANES), f32),
            pltpu.VMEM((n_reg, 8, LANES), f32),
            pltpu.VMEM((n_mem, n_reg, 8, LANES), f32),
            pltpu.VMEM((n_mem, n_reg, 8, LANES), f32),
            pltpu.VMEM((n_mem, n_reg, 8, LANES), f32),
            pltpu.VMEM((n_mem, n_reg, 8, LANES), f32),
            pltpu.VMEM((3, n_reg + 2, 16, LANES), f32),
            pltpu.VMEM((n_reg + 2, 16, LANES), f32),
            pltpu.VMEM((n_reg + 2, 16, LANES), f32),
            pltpu.VMEM((3, n_reg, 16, members), f32),
            pltpu.VMEM((2, 3 * cells, obs), f32),
            pltpu.VMEM((2, 3 * cells, obs), jnp.bfloat16),
            pltpu.VMEM((2, 3 * cells, obs), jnp.bfloat16),
            pltpu.VMEM((3, cells, members + LANES), f32),
            pltpu.VMEM((n_mem, n_reg, 3, 8, LANES), f32),
            pltpu.VMEM((n_mem, n_reg, 3, 8, LANES), f32),
            pltpu.VMEM((n_reg, 8, LANES), f32),
            pltpu.VMEM((n_reg, 8, LANES), f32),
            pltpu.VMEM(flat, f32), pltpu.VMEM(flat, f32), pltpu.VMEM(flat, f32),
            pltpu.VMEM((2, 8, LANES), f32),
            pltpu.VMEM((n_mem, 4, 8, LANES), f32),
            pltpu.VMEM((tiles, LANES), f32), pltpu.VMEM((tiles, LANES), f32),
            pltpu.VMEM((2, 4, obs), jnp.int32), pltpu.VMEM((2, 4, obs), f32),
            pltpu.VMEM((2, obs), f32), pltpu.VMEM((2, obs), f32),
            pltpu.SMEM((2,), jnp.int32), pltpu.VMEM(flat_fine, f32),
            dma, dma((n_mem,)), dma, dma, dma((2, n_mem)), dma((2, n_mem)),
            dma, dma((n_mem,)), dma, dma, dma((11,)), dma,
        ],
        compiler_params=pltpu.CompilerParams(
            collective_id=0, has_side_effects=True, vmem_limit_bytes=56 * 1024 * 1024
        ),
    )(
        h.reshape(flat), u.reshape(flat), v.reshape(flat),
        cu.reshape(tiles, LANES), cv.reshape(tiles, LANES),
        obs_index.transpose(0, 2, 1), obs_weight.transpose(0, 2, 1),
        obs_value, obs_var, obs_count, fine.reshape(flat_fine),
    )
    return tuple(outs[0][var].reshape(h.shape) for var in range(3)) + (outs[1].reshape(fine.shape),)


def solution(mesh):
    fields = P("member", "region", "fine")
    regions = ("member", "region", "fine")
    fine = P(None, "region", "fine", "member")
    return jax.shard_map(
        functools.partial(step, mesh.shape["member"], mesh.shape["region"]),
        mesh=mesh,
        in_specs=(
            fields, fields, fields,
            P("region", "fine"), P("region", "fine"),
            P(regions, None, None), P(regions, None, None),
            P(regions, None), P(regions, None), P(regions),
            fine,
        ),
        out_specs=(fields, fields, fields, fine),
        check_vma=False,
    )
```
